32 devices in a mesh: seq: 8 (over y, x, core), wt: 4 (over z).
Axes of the slice: x: 2, y: 2, z: 4, core: 2. Of those that a mesh axis runs over, the one named last changes fastest.
Arguments:
- hidden: bfloat16 [4, 4096, 1024], P('wt', 'seq'), may hold values from -6 to 6
- doc_ids: int32 [4, 4096], P('wt'), may hold values from 0 to 15, never falling along the last dimension, each value on 1 to 1024 neighbouring positions
- norm_gain: float32 [1024], replicated, may hold values from 0.1 to 1.9
- in_weight: float32 [1024, 4384], P('wt'), may hold values from -0.1875 to 0.1875
- conv_weight: float32 [4, 2304], replicated, may hold values from -3 to 3
- conv_bias: float32 [2304], replicated, may hold values from -0.5 to 0.5
- step_bias: float32 [32], replicated, may hold values from -12 to -4
- decay_log: float32 [32], replicated, may hold values from 0 to 2.77
- skip_gain: float32 [32], replicated, may hold values from 0.5 to 1.5
- out_gain: float32 [2048], replicated, may hold values from 0.1 to 1.9
- out_weight: float32 [2048, 1024], P('wt'), may hold values from -0.125 to 0.125
- cotangent: bfloat16 [4, 4096, 1024], P('wt', 'seq'), may hold values from -6 to 6
Outputs:
- output: bfloat16 [4, 4096, 1024], P('wt', 'seq')
- input_grad: float32 [4, 4096, 1024], P('wt', 'seq')
- norm_gain_grad: float32 [1024], replicated
- in_weight_grad: float32 [1024, 4384], P('wt')
- conv_weight_grad: float32 [4, 2304], replicated
- conv_bias_grad: float32 [2304], replicated
- step_bias_grad: float32 [32], replicated
- decay_log_grad: float32 [32], replicated
- skip_gain_grad: float32 [32], replicated
- out_gain_grad: float32 [2048], replicated
- out_weight_grad: float32 [2048, 1024], P('wt')
The draws below stay inside these ranges and needn't reach their ends.
Inputs may be any that keep to these rules, and one draw needn't show every extreme that they name: `doc_ids`: along each stream the document numbers never fall; every document 0 to 15 has 1 to 1024 positions, and some document has exactly 1024.
All inputs are finite; a program needn't handle non-finite values.
Results may differ from the reference program's by a relative error of at most 0.0038.
The reference program's roundings to bfloat16 on the way count: a program that leaves them out, or rounds other values in their place, can miss the bound.
Values may be sent and summed in bfloat16 or wider, within the bound.
No kernel may reach another device: no remote copies, remote signals or barrier semaphores. Data moves between devices by JAX's collectives and lax.ppermute only.
A program may use at most 320 MiB of HBM per device.

```python
import math
import jax
import jax.numpy as jnp
import numpy as np
from jax import lax

WIDTH = 1024
INNER = 2048
HEADS = 32
STATE = 128
TAPS = 4
BLOCK = 256
DOCS = 16
STREAMS = 4
SEQ_LEN = 4096
DOC_MAX = 1024
PROJ = 4384
CONV_CH = 2304


def levels(key, dims, pieces, least, top_value):
    def one(position, blocks):
        heights = jax.random.uniform(jax.random.fold_in(jax.random.fold_in(key, 6), position), (blocks,), jnp.float32, least / len(pieces), top_value / len(pieces))
        return jnp.repeat(jnp.exp(heights), dims[position] // blocks).reshape((-1,) + (1,) * (len(dims) - position - 1))

    loudness = one(*pieces[0])
    for cut in pieces[1:]:
        loudness = loudness * one(*cut)
    return loudness


def profile(amount, total, limit, skew):
    portions = [(1 << 20) // math.isqrt(grade ** skew) + 1 for grade in range(2, amount + 1)]
    surplus, counts = total - limit - (amount - 1), [1] * (amount - 1)
    while surplus > 0:
        free = [i for i in range(amount - 1) if counts[i] < limit]
        pool, budget = sum([portions[i] for i in free]), surplus
        for i in free:
            more = min(limit - counts[i], max(1, budget * portions[i] // pool), surplus)
            counts[i] = counts[i] + more
            surplus = surplus - more
    return np.array([limit] + counts)


def ragged(rng, count, total, most, lean):
    if count == 2:
        one = jax.random.randint(rng, (), max(1, total - most), min(most, total - 1) + 1)
        return jnp.stack([one, total - one])
    sizes = jnp.asarray(profile(count, total, most, lean), jnp.int32)
    couples = (count - 1) // 2
    source_of, taker = sizes[1:1 + 2 * couples:2], sizes[2:2 + 2 * couples:2]
    room = jnp.minimum(source_of - 1, most - taker)
    moved = jax.random.randint(jax.random.fold_in(rng, 1), (couples,), 0, 1 << 20) % (room + 1)
    sizes = sizes.at[1:1 + 2 * couples:2].set(source_of - moved).at[2:2 + 2 * couples:2].set(taker + moved)
    return sizes[jax.random.permutation(jax.random.fold_in(rng, 2), count)]


def bell_draw(stream_key, dims, scale, limit, shards=(), dtype=jnp.bfloat16):
    values = jax.random.normal(stream_key, dims, jnp.float32) * scale
    if len(shards) > 0:
        values = levels(stream_key, dims, shards, -0.22, 0.18) * values
    return jnp.clip(values, min=-limit, max=limit).astype(dtype)


def setup_inputs(seed: int = 0) -> dict:
    arg_keys = jax.random.split(jax.random.key(seed), 13)
    return {
        "hidden": bell_draw(arg_keys[0], (STREAMS, SEQ_LEN, WIDTH), 1.0, 6.0, ((0, 4), (1, 8))),
        "doc_ids": jax.vmap(lambda own: jnp.searchsorted(jnp.cumsum(ragged(own, DOCS, SEQ_LEN, DOC_MAX, 1)), jnp.arange(SEQ_LEN), side="right"))(jax.random.split(arg_keys[1], STREAMS)).reshape((STREAMS, SEQ_LEN)).astype(jnp.int32),
        "norm_gain": jnp.clip(1.0 + 0.18 * jax.random.normal(arg_keys[2], (WIDTH,), jnp.float32), 0.1, 1.9),
        "in_weight": bell_draw(arg_keys[3], (WIDTH, PROJ), WIDTH ** -0.5, 0.1875, ((0, 4),), jnp.float32),
        "conv_weight": bell_draw(arg_keys[4], (TAPS, CONV_CH), TAPS ** -0.5, 3.0, (), jnp.float32),
        "conv_bias": jnp.clip(jax.random.uniform(arg_keys[5], (CONV_CH,), jnp.float32, -0.5, 0.5), -0.5, 0.5),
        "step_bias": jnp.clip(jax.random.uniform(arg_keys[6], (HEADS,), jnp.float32, -12.0, -4.0), -12.0, -4.0),
        "decay_log": jnp.clip(jax.random.uniform(arg_keys[7], (HEADS,), jnp.float32, 0.0, 2.77), 0.0, 2.77),
        "skip_gain": jnp.clip(jax.random.uniform(arg_keys[8], (HEADS,), jnp.float32, 0.5, 1.5), 0.5, 1.5),
        "out_gain": jnp.clip(1.0 + 0.18 * jax.random.normal(arg_keys[9], (INNER,), jnp.float32), 0.1, 1.9),
        "out_weight": bell_draw(arg_keys[10], (INNER, WIDTH), INNER ** -0.5, 0.125, ((0, 4),), jnp.float32),
        "cotangent": bell_draw(arg_keys[11], (STREAMS, SEQ_LEN, WIDTH), 1.0, 6.0, ((0, 4), (1, 8))),
    }


EPS = 1e-05
HIGH = lax.Precision.HIGHEST

@jax.custom_vjp
def low(v):
    return lax.optimization_barrier(v.astype(jnp.bfloat16)).astype(jnp.float32)

@jax.custom_vjp
def low_back(v):
    return v

def low_keep(v):
    return (low(v), None)

def low_pass(kept, grad):
    return (grad,)

def back_keep(v):
    return (v, None)

def back_low(kept, grad):
    return (low(grad),)
low.defvjp(low_keep, low_pass)
low_back.defvjp(back_keep, back_low)

def conv_silu(values, weight, bias_row, segment):
    summed = bias_row[None, :] + weight[0][None, :] * values
    for offset in range(1, weight.shape[0]):
        before = jnp.pad(values[:-offset], ((offset, 0), (0, 0)))
        same_doc = jnp.pad(segment[offset:] == segment[:-offset], (offset, 0))
        summed = summed + weight[offset][None, :] * jnp.where(same_doc[:, None], before, 0.0)
    return jax.nn.silu(summed)

def ssd_block(carried, inputs, decay_rate, skip_gain):
    states, prev_doc = carried
    x_block, b_block, c_block, step_block, doc_block = inputs
    cumul = jnp.cumsum(step_block * decay_rate[None, :], axis=0)
    length = doc_block.shape[0]
    row_pos = lax.broadcasted_iota(jnp.int32, (length, length), 0)
    col_pos = lax.broadcasted_iota(jnp.int32, (length, length), 1)
    within = (col_pos <= row_pos) & (doc_block[:, None] == doc_block[None, :])
    cumul_t = cumul.T
    spread = cumul_t[:, :, None] - cumul_t[:, None, :]
    weights_in = jnp.where(within[None], jnp.exp(jnp.where(within[None], spread, 0.0)), 0.0)
    intersection = jnp.dot(c_block, b_block.T, precision=HIGH)
    scaled = step_block[:, :, None] * x_block
    local_out = jnp.einsum('hij,jhp->ihp', intersection[None] * weights_in, scaled, precision=HIGH)
    carry_in = jnp.where((doc_block == prev_doc)[:, None], jnp.exp(cumul), 0.0)
    from_state = jnp.einsum('in,hpn->ihp', c_block, states, precision=HIGH) * carry_in[:, :, None]
    result = local_out + from_state + skip_gain[None, :, None] * x_block
    last_doc = doc_block[-1]
    tail = jnp.where((doc_block == last_doc)[:, None], jnp.exp(cumul[-1][None, :] - cumul), 0.0)
    kept_part = jnp.where(prev_doc == last_doc, jnp.exp(cumul[-1]), 0.0)
    new_states = kept_part[:, None, None] * states + jnp.einsum('jh,jhp,jn->hpn', tail, scaled, b_block, precision=HIGH)
    return ((new_states, last_doc), result)

def ssd(x_act, b_act, c_act, steps_dt, decay_rate, skip_gain, doc_ids, block_len):
    total_len = x_act.shape[0]
    head_count = steps_dt.shape[1]
    head_size = x_act.shape[1] // head_count
    block_count = total_len // block_len
    x_blocks = x_act.reshape(block_count, block_len, head_count, head_size)
    b_blocks = b_act.reshape(block_count, block_len, b_act.shape[1])
    c_blocks = c_act.reshape(block_count, block_len, c_act.shape[1])
    dt_blocks = steps_dt.reshape(block_count, block_len, head_count)
    doc_blocks = doc_ids.reshape(block_count, block_len)
    start_carry = (jnp.zeros((head_count, head_size, b_act.shape[1]), jnp.float32), jnp.array(-1, jnp.int32))
    step_fn = jax.checkpoint(lambda carried, inputs: ssd_block(carried, inputs, decay_rate, skip_gain))
    final_carry, outputs = lax.scan(step_fn, start_carry, (x_blocks, b_blocks, c_blocks, dt_blocks, doc_blocks))
    return outputs.reshape(total_len, head_count * head_size)

def head_mix(x_raw, bc_raw, dt_raw, conv_x, conv_bc, bias_x, bias_bc, step_bias, decay_log, skip_gain, doc_ids, block_len):
    x_act = conv_silu(x_raw, conv_x, bias_x, doc_ids)
    bc_act = conv_silu(bc_raw, conv_bc, bias_bc, doc_ids)
    state_dim = bc_raw.shape[1] // 2
    steps_dt = jax.nn.softplus(dt_raw + step_bias[None, :])
    decay_rate = -jnp.exp(decay_log)
    return ssd(x_act, bc_act[:, :state_dim], bc_act[:, state_dim:], steps_dt, decay_rate, skip_gain, doc_ids, block_len)

def layer_forward(hidden, params, doc_ids):
    norm_gain, in_weight, conv_weight, conv_bias, step_bias, decay_log, skip_gain, out_gain, out_weight = params
    ratio = lax.rsqrt(lax.optimization_barrier(jnp.mean(hidden * hidden, axis=-1, keepdims=True)) + EPS)
    normed = low(hidden * ratio * norm_gain[None, :])
    proj = low_back(low(jnp.dot(normed, low(in_weight), precision=HIGH)))
    gate = proj[:, :INNER]
    x_raw = proj[:, INNER:2 * INNER]
    bc_raw = proj[:, 2 * INNER:2 * INNER + 2 * STATE]
    dt_raw = proj[:, 2 * INNER + 2 * STATE:]
    mixed = head_mix(x_raw, bc_raw, dt_raw, conv_weight[:, :INNER], conv_weight[:, INNER:], conv_bias[:INNER], conv_bias[INNER:], step_bias, decay_log, skip_gain, doc_ids, BLOCK)
    mixed = low_back(low(mixed))
    gated = mixed * jax.nn.silu(gate)
    gnorm = lax.rsqrt(lax.optimization_barrier(jnp.mean(gated * gated, axis=-1, keepdims=True)) + EPS)
    final = low(gated * gnorm * out_gain[None, :])
    return hidden + jnp.dot(final, low(out_weight), precision=HIGH)

def reference(hidden, doc_ids, norm_gain, in_weight, conv_weight, conv_bias, step_bias, decay_log, skip_gain, out_gain, out_weight, cotangent):
    params = (norm_gain, in_weight, conv_weight, conv_bias, step_bias, decay_log, skip_gain, out_gain, out_weight)

    def per_stream(sums, inputs):
        stream_x, stream_docs, stream_cot = inputs
        result, pullback = jax.vjp(lambda x_in, weights: layer_forward(x_in, weights, stream_docs), stream_x.astype(jnp.float32), params)
        grads = pullback(stream_cot.astype(jnp.float32))
        new_sums = jax.tree.map(lambda first_term, second_term: first_term + second_term, sums, grads[1])
        return (new_sums, (result.astype(jnp.bfloat16), grads[0]))
    zero_sums = jax.tree.map(lambda array: jnp.zeros(array.shape, jnp.float32), params)
    sums, stacked = lax.scan(per_stream, zero_sums, (hidden, doc_ids, cotangent))
    return (stacked[0], stacked[1], sums[0], sums[1], sums[2], sums[3], sums[4], sums[5], sums[6], sums[7], sums[8])
```

```python
import functools

import jax
import jax.numpy as jnp
from jax import lax
from jax.experimental import pallas as pl
from jax.experimental.pallas import tpu as pltpu
from jax.sharding import PartitionSpec as P

EPS = 1e-05
LOG2E = 1.4426950408889634
CHUNK = 128
HALO = 16
LANES = 256
HEAD = 64
TAPS = 4
FULL = lax.Precision.HIGHEST
F32 = jnp.float32
BF16 = jnp.bfloat16
SEQ = "seq"
WT = "wt"


def mm(a, b):
    return jnp.dot(a, b, preferred_element_type=F32)


def mm_cols(a, b):
    return lax.dot_general(a, b, (((1,), (1,)), ((), ())), preferred_element_type=F32)


def mm_rows(a, b):
    return lax.dot_general(a, b, (((0,), (0,)), ((), ())), preferred_element_type=F32)


def sigmoid(x):
    return 0.5 * jnp.tanh(0.5 * x) + 0.5


def split2(x):
    high = x.astype(BF16)
    return high, (x - high.astype(F32)).astype(BF16)


def mm_split(x, ones):
    high, low = split2(x)
    return mm(high, ones) + mm(low, ones)


def mm3(a, b, mult=mm):
    a_high, a_low = a if isinstance(a, tuple) else split2(a)
    b_high, b_low = b if isinstance(b, tuple) else split2(b)
    return mult(a_high, b_high) + mult(a_high, b_low) + mult(a_low, b_high)


def pack3(x):
    high = x.astype(BF16).astype(F32)
    rest = x - high
    mid = rest.astype(BF16).astype(F32)
    low = rest - mid
    return (high + pltpu.roll(mid, 32, 1) + pltpu.roll(low, 64, 1)).astype(BF16)


def softplus(x):
    small = jnp.exp(-jnp.abs(x))
    series = small * (1.0 - small * (0.5 - small * (1.0 / 3.0 - small * (0.25 - small * 0.2))))
    return jnp.maximum(x, 0.0) + jnp.where(small < 0.02, series, jnp.log(1.0 + small))


def conv_inputs(window, shifts):
    moved = mm(shifts, window)
    return [window[HALO:].astype(F32)] + [
        moved[j * CHUNK : (j + 1) * CHUNK] for j in range(TAPS - 1)
    ]


def conv_sum(taps, cw):
    total = cw[TAPS : TAPS + 1]
    for j in range(TAPS):
        total = total + cw[j : j + 1] * taps[j]
    return total


def pair_cols(x):
    return x[:, :128], x[:, 128:]


def pair_rows(x):
    return x[:128], x[128:]


def rows_of(c):
    return slice(c * CHUNK, (c + 1) * CHUNK)


def window_of(c):
    return slice(c * CHUNK, (c + 1) * CHUNK + HALO)


def prep_kernel(
    bc_ref, dtr_ref, sh_ref, mask_ref, cols_ref, cw_ref, hp_ref,
    b_ref, c_ref, bt_ref, ct_ref, gm_ref, dtf_ref, dt_ref, e_ref, f_ref, ed_ref, la_ref, cat_ref, kept_ref,
):
    row = lax.broadcasted_iota(jnp.int32, (CHUNK, CHUNK), 0)
    col = lax.broadcasted_iota(jnp.int32, (CHUNK, CHUNK), 1)
    lower = jnp.where(col <= row, 1.0, 0.0).astype(F32)
    used = col < 32
    heads = cat_ref.shape[1]
    before = jnp.zeros((1, CHUNK), F32)
    cw = cw_ref[...]
    for c in range(sh_ref.shape[0]):
        rows = rows_of(c)
        taps = conv_inputs(bc_ref[window_of(c)], sh_ref[c])
        k = conv_sum(taps, cw)
        act = k * sigmoid(k)
        b_act, c_act = act[:, :128], act[:, 128:]
        b_high, b_low = split2(b_act)
        c_high, c_low = split2(c_act)
        gram = mm_cols(c_high, b_high) + mm_cols(c_high, b_low) + mm_cols(c_low, b_high)
        gm_ref[rows] = gram * mask_ref[rows]
        b_ref[rows] = jnp.concatenate([b_high, b_low], axis=1)
        c_ref[rows] = jnp.concatenate([c_high, c_low], axis=1)
        bt_ref[:, rows] = jnp.concatenate(split2(b_act.T), axis=0)
        ct_ref[:, rows] = jnp.concatenate(split2(c_act.T), axis=0)
        step_in = dtr_ref[c * CHUNK + HALO : (c + 1) * CHUNK + HALO].astype(F32) + hp_ref[0:1]
        dt = jnp.where(used, softplus(step_in), 0.0)
        cumul = jnp.dot(lower, dt * hp_ref[1:2], precision=FULL, preferred_element_type=F32)
        last = cumul[CHUNK - 1 : CHUNK]
        cols = cols_ref[rows]
        e = jnp.where(used, jnp.exp2(cumul) * cols[:, 0:1], 0.0)
        f = jnp.where(used, jnp.exp2(last - cumul) * cols[:, 1:2], 0.0)
        ed = jnp.where(used, jnp.exp2(before + cumul) * cols[:, 2:3], 0.0)
        before = before + last
        dtf_ref[rows] = dt
        dt_ref[rows] = pack3(dt)
        e_ref[rows] = pack3(e)
        f_ref[rows] = pack3(f)
        ed_ref[rows] = pack3(ed)
        la_ref[rows] = pack3(cumul)
        cat_ref[c] = cumul.T[:heads]
        kept_ref[...] = jnp.broadcast_to(ed[CHUNK - 1 : CHUNK], kept_ref.shape)


def weights_of(c, step, la_ref, sel, cat_ref):
    spread = mm(la_ref[rows_of(c)], sel)
    per_step = LANES // HEAD
    out = []
    for i in range(per_step):
        ahead = cat_ref[c, pl.ds(step * per_step + i, 1), :]
        out.append(jnp.exp2(jnp.minimum(spread[:, i * CHUNK : (i + 1) * CHUNK] - ahead, 0.0)))
    return out


def head_pairs(x):
    first = lax.broadcasted_iota(jnp.int32, x.shape, 1) < HEAD
    zero = jnp.zeros_like(x)
    return jnp.concatenate([jnp.where(first, x, zero), jnp.where(first, zero, x)], axis=0)


def fwd_kernel(
    x_ref, sh_ref, cw_ref, gm_ref, c_ref, bt_ref, dt_ref, e_ref, f_ref, la_ref, sel_ref, exp_ref, cat_ref,
    y_ref, s_ref,
):
    step = pl.program_id(0)
    cw, sel, expand = cw_ref[...], sel_ref[...], exp_ref[...]
    state = jnp.zeros((128, LANES), F32)
    for c in range(sh_ref.shape[0]):
        rows = rows_of(c)
        k = conv_sum(conv_inputs(x_ref[window_of(c)], sh_ref[c]), cw)
        xa = k * sigmoid(k)
        v = mm(dt_ref[rows], expand) * xa
        ex = mm(e_ref[rows], expand)
        fx = mm(f_ref[rows], expand)
        v_parts = split2(v)
        gm = gm_ref[rows]
        weights = [w * gm for w in weights_of(c, step, la_ref, sel, cat_ref)]
        local = []
        for p in range(LANES // 128):
            own = tuple(head_pairs(part[:, p * 128 : (p + 1) * 128]) for part in v_parts)
            local.append(mm3(jnp.concatenate(weights[2 * p : 2 * p + 2], axis=1), own))
        y = jnp.concatenate(local, axis=1) + ex * mm3(pair_cols(c_ref[rows]), state)
        y_ref[rows] = y + cw[5:6] * xa
        state = ex[CHUNK - 1 : CHUNK] * state + mm3(pair_rows(bt_ref[:, rows]), fx * v)
    s_ref[...] = state.astype(BF16)


def gate_kernel(
    y_ref, z_ref, c_ref, ct_ref, ed_ref, sin_ref, wo_ref, exp_ref, expt_ref, gain_ref, hid_ref, df_ref,
    out_ref, fin_ref, dz_ref, dy_ref, q_ref, og_ref, gs_ref, acc_ref,
):
    i = pl.program_id(0)

    @pl.when(i == 0)
    def _():
        og_ref[...] = jnp.zeros_like(og_ref)
        acc_ref[...] = jnp.zeros_like(acc_ref)

    gain = gain_ref[0:1]
    inner = y_ref.shape[1]
    edx = mm(ed_ref[...], exp_ref[...])
    y_full = y_ref[...] + edx * (mm(c_ref[:, :128], sin_ref[...]) + mm(c_ref[:, 128:], sin_ref[...]))
    y = y_full.astype(BF16).astype(F32)
    z = z_ref[...].astype(F32)
    sig = sigmoid(z)
    sz = z * sig
    gated = y * sz
    gnorm = lax.rsqrt(jnp.sum(gated * gated, axis=1, keepdims=True) * (1.0 / inner) + EPS)
    normal = gated * gnorm
    final = (normal * gain).astype(BF16)
    fin_ref[...] = final
    out_ref[...] = (hid_ref[...].astype(F32) + mm(final, wo_ref[...])).astype(BF16)
    dfinal = df_ref[...]
    share = dfinal * normal
    og_ref[...] += jnp.sum(share.reshape(-1, 8, inner), axis=0)
    e = dfinal * gain
    mean = jnp.sum(share * gain, axis=1, keepdims=True) * (1.0 / inner)
    dgated = gnorm * (e - normal * mean)
    dz_ref[...] = (dgated * y * (sig * (1.0 + z * (1.0 - sig)))).astype(BF16)
    dyb = (dgated * sz).astype(BF16)
    dy_ref[...] = dyb
    dy = dyb.astype(F32)
    q_ref[...] = mm_split(dy * y_full, expt_ref[...])
    acc_ref[...] += mm3(pair_rows(ct_ref[...]), edx * dy)

    @pl.when(i == pl.num_programs(0) - 1)
    def _():
        gs_ref[...] = acc_ref[...].astype(BF16)


def back_kernel(
    x_ref, dy_ref, sh_ref, sht_ref, cw_ref, gm_ref, b_ref, bt_ref, ct_ref, dt_ref, e_ref, f_ref, la_ref,
    sel_ref, exp_ref, expt_ref, cat_ref, sin_ref, din_ref,
    dx_ref, edge_ref, cg_ref, m_ref, dcb_ref, red_ref, sd_ref,
    k_ref, states_ref, dxw_ref,
):
    step = pl.program_id(0)

    @pl.when(step == 0)
    def _():
        m_ref[...] = jnp.zeros_like(m_ref)
        dcb_ref[...] = jnp.zeros_like(dcb_ref)
        red_ref[...] = jnp.zeros_like(red_ref)

    count = sh_ref.shape[0]
    cw, sel, expand = cw_ref[...], sel_ref[...], exp_ref[...]
    state = sin_ref[...].astype(F32)
    for c in range(count):
        rows = rows_of(c)
        k = conv_sum(conv_inputs(x_ref[window_of(c)], sh_ref[c]), cw)
        k_ref[rows] = k
        v = mm(dt_ref[rows], expand) * (k * sigmoid(k))
        ex_last = mm(e_ref[rows], expand)[CHUNK - 1 : CHUNK]
        fx = mm(f_ref[rows], expand)
        states_ref[c] = state
        state = ex_last * state + mm3(pair_rows(bt_ref[:, rows]), fx * v)
    grad = din_ref[...].astype(F32)
    cg = [jnp.zeros((8, LANES), F32) for _ in range(TAPS + 1)]
    sd_ref[...] = jnp.zeros_like(sd_ref)
    after = state
    for c in reversed(range(count)):
        rows = rows_of(c)
        gradb = grad.astype(BF16)
        sd_ref[c : c + 1] = jnp.sum(after * grad, axis=0, keepdims=True)
        after = states_ref[c]
        taps = conv_inputs(x_ref[window_of(c)], sh_ref[c])
        k = k_ref[rows]
        sig = sigmoid(k)
        xa = k * sig
        dtx = mm(dt_ref[rows], expand)
        ex = mm(e_ref[rows], expand)
        fx = mm(f_ref[rows], expand)
        v = dtx * xa
        vb = v.astype(BF16)
        dyb = dy_ref[rows]
        dy = dyb.astype(F32)
        gm = gm_ref[rows]
        weights = weights_of(c, step, la_ref, sel, cat_ref)
        dv = []
        total = None
        for p in range(LANES // 128):
            lanes = slice(p * 128, (p + 1) * 128)
            pair = weights[2 * p : 2 * p + 2]
            products = mm_cols(dyb[:, lanes], head_pairs(vb[:, lanes]))
            part = products[:, :CHUNK] * pair[0] + products[:, CHUNK:] * pair[1]
            total = part if total is None else total + part
            stacked = jnp.concatenate([w * gm for w in pair], axis=0)
            own = head_pairs(dyb[:, lanes])
            high, low = split2(stacked)
            dv.append(mm_rows(high, own) + mm_rows(low, own))
        m_ref[rows] += total
        dv = jnp.concatenate(dv, axis=1) + fx * mm3(pair_cols(b_ref[rows]), grad)
        edy = ex * dy
        edyb = edy.astype(BF16)
        dcb_ref[rows, 0:128] += mm_cols((fx * v).astype(BF16), gradb)
        dcb_ref[rows, 128:256] += mm_cols(edyb, after.astype(BF16))
        grad = ex[CHUNK - 1 : CHUNK] * grad + mm3(pair_rows(ct_ref[:, rows]), edy)
        red = mm_split(xa * dv, expt_ref[:, 0:128])
        red += mm_split(v * dv, expt_ref[:, 128:256])
        red += mm_split(dy * xa, expt_ref[:, 256:384])
        red_ref[rows] += red
        dxa = dtx * dv + cw[5:6] * dy
        dk = dxa * (sig * (1.0 + k * (1.0 - sig)))
        cg[TAPS] += jnp.sum(dk.reshape(-1, 8, LANES), axis=0)
        for j in range(TAPS):
            cg[j] += jnp.sum((dk * taps[j]).reshape(-1, 8, LANES), axis=0)
        shifted = jnp.concatenate([(cw[j : j + 1] * dk).astype(BF16) for j in range(1, TAPS)], axis=0)
        moved = mm(sht_ref[c], shifted)
        low, high = c * CHUNK, (c + 1) * CHUNK
        own = cw[0:1] * dk
        dxw_ref[low : low + HALO] = moved[:HALO]
        dxw_ref[low + HALO : high] = moved[HALO:CHUNK] + own[: CHUNK - HALO]
        end = moved[CHUNK:] + own[CHUNK - HALO :]
        if c == count - 1:
            dxw_ref[high : high + HALO] = end
        else:
            dxw_ref[high : high + HALO] += end
    cg_ref[...] = jnp.zeros_like(cg_ref)
    for j in range(TAPS + 1):
        cg_ref[j : j + 1] = jnp.sum(cg[j], axis=0, keepdims=True)
    dx_ref[...] = dxw_ref[HALO:].astype(BF16)
    edge_ref[:HALO] = dxw_ref[:HALO]
    edge_ref[HALO:] = dxw_ref[count * CHUNK :]


def post_kernel(
    bc_ref, dtr_ref, sh_ref, sht_ref, mask_ref, cw_ref, hp_ref, b_ref, c_ref, m_ref, dcb_ref, red_ref, sd_ref,
    expt_ref, q_ref, dtf_ref,
    dbc_ref, ddt_ref, edge_ref, cg_ref, hg_ref,
    dxw_ref,
):
    count = sh_ref.shape[0]
    cw = cw_ref[...]
    width = bc_ref.shape[1]
    row = lax.broadcasted_iota(jnp.int32, (CHUNK, CHUNK), 0)
    col = lax.broadcasted_iota(jnp.int32, (CHUNK, CHUNK), 1)
    upper = jnp.where(col >= row, 1.0, 0.0).astype(F32)
    used = col < 32
    cg = [jnp.zeros((8, width), F32) for _ in range(TAPS + 1)]
    step_grad = jnp.zeros((8, CHUNK), F32)
    decay_grad = jnp.zeros((8, CHUNK), F32)
    skip_grad = jnp.zeros((8, CHUNK), F32)
    ends = mm_split(sd_ref[...], expt_ref[...])
    rate = hp_ref[2:3]
    for c in reversed(range(count)):
        rows = rows_of(c)
        taps = conv_inputs(bc_ref[window_of(c)], sh_ref[c])
        k = conv_sum(taps, cw)
        sig = sigmoid(k)
        both = (m_ref[rows] * mask_ref[rows]).astype(BF16)
        db = mm_rows(both, c_ref[rows, :128]) + dcb_ref[rows, 0:128]
        dc = mm(both, b_ref[rows, :128]) + dcb_ref[rows, 128:256]
        dk = jnp.concatenate([db, dc], axis=1) * (sig * (1.0 + k * (1.0 - sig)))
        cg[TAPS] += jnp.sum(dk.reshape(-1, 8, width), axis=0)
        for j in range(TAPS):
            cg[j] += jnp.sum((dk * taps[j]).reshape(-1, 8, width), axis=0)
        shifted = jnp.concatenate([(cw[j : j + 1] * dk).astype(BF16) for j in range(1, TAPS)], axis=0)
        moved = mm(sht_ref[c], shifted)
        low, high = c * CHUNK, (c + 1) * CHUNK
        own = cw[0:1] * dk
        dxw_ref[low : low + HALO] = moved[:HALO]
        dxw_ref[low + HALO : high] = moved[HALO:CHUNK] + own[: CHUNK - HALO]
        end = moved[CHUNK:] + own[CHUNK - HALO :]
        if c == count - 1:
            dxw_ref[high : high + HALO] = end
        else:
            dxw_ref[high : high + HALO] += end
        red = red_ref[rows]
        xdv = red
        vdv = pltpu.roll(red, 96, 1)
        dyx = pltpu.roll(red, 64, 1)
        change = q_ref[rows] - hp_ref[3:4] * dyx - vdv
        change = jnp.where(used, change, 0.0)
        da = jnp.dot(upper, change, precision=FULL, preferred_element_type=F32) + ends[c : c + 1]
        dt = dtf_ref[rows]
        step_in = dtr_ref[c * CHUNK + HALO : (c + 1) * CHUNK + HALO].astype(F32) + hp_ref[0:1]
        ddt = jnp.where(used, (xdv + rate * da) * sigmoid(step_in), 0.0)
        ddt_ref[rows] = ddt.astype(BF16)
        step_grad += jnp.sum(ddt.reshape(-1, 8, CHUNK), axis=0)
        decay_grad += jnp.sum((dt * da).reshape(-1, 8, CHUNK), axis=0)
        skip_grad += jnp.sum(dyx.reshape(-1, 8, CHUNK), axis=0)
    cg_ref[...] = jnp.zeros_like(cg_ref)
    for j in range(TAPS + 1):
        cg_ref[j : j + 1] = jnp.sum(cg[j], axis=0, keepdims=True)
    dbc_ref[...] = dxw_ref[HALO:].astype(BF16)
    edge_ref[:HALO] = dxw_ref[:HALO]
    edge_ref[HALO:] = dxw_ref[count * CHUNK :]
    hg_ref[...] = jnp.zeros_like(hg_ref)
    hg_ref[0:1] = jnp.sum(step_grad, axis=0, keepdims=True)
    hg_ref[1:2] = rate * jnp.sum(decay_grad, axis=0, keepdims=True)
    hg_ref[2:3] = jnp.sum(skip_grad, axis=0, keepdims=True)


def whole(array):
    return pl.BlockSpec(array.shape, lambda *_: (0,) * array.ndim)


def lanes_block(array, width=LANES, first=0):
    return pl.BlockSpec((array.shape[0], width), lambda i: (0, first + i))


def shape(dims, dtype=F32):
    return jax.ShapeDtypeStruct(dims, dtype)


PARAMS = pltpu.CompilerParams(vmem_limit_bytes=56 * 1024 * 1024, dimension_semantics=("arbitrary",))


def gather_rows(part):
    count = lax.axis_size(SEQ)
    share = part.shape[0] // count
    mine = lax.dynamic_slice_in_dim(part, lax.axis_index(SEQ) * share, share, 0)
    return lax.all_gather(mine, (WT, SEQ), axis=0, tiled=True)


def reduce_rows(part):
    count = lax.axis_size(SEQ)
    part = part.reshape(lax.axis_size(WT), count, -1, part.shape[1]).transpose(1, 0, 2, 3).reshape(part.shape)
    mine = lax.psum_scatter(part, SEQ, scatter_dimension=0, tiled=True)
    mine = lax.psum_scatter(mine, WT, scatter_dimension=0, tiled=True)
    return lax.all_gather(mine, SEQ, axis=0, tiled=True)


def shift_seq(x, by):
    count = lax.axis_size(SEQ)
    pairs = [(i, i + by) for i in range(count) if 0 <= i + by < count]
    return lax.ppermute(x, SEQ, pairs)


def carried(part, kept, hops, sign):
    total, fade = None, None
    for hop in range(1, hops + 1):
        moved = shift_seq(part, sign * hop).astype(F32)
        if fade is not None:
            moved = moved * fade
        total = moved if total is None else total + moved
        if hop < hops:
            factor = jnp.repeat(shift_seq(kept, sign * hop), HEAD)[None, :]
            fade = factor if fade is None else fade * factor
    return total.astype(BF16)


def on_device(
    hidden, doc_ids, norm_gain, in_weight, conv_weight, conv_bias, step_bias, decay_log, skip_gain, out_gain,
    out_weight, cotangent,
):
    seq_count = lax.axis_size(SEQ)
    seq_index = lax.axis_index(SEQ)
    inner = out_gain.shape[0]
    heads = step_bias.shape[0]
    length = hidden.shape[1]
    state_dim = (conv_weight.shape[1] - inner) // 2
    width = hidden.shape[2]
    chunks = length // CHUNK
    x_cols = in_weight.shape[1] - inner
    x_pad = -x_cols % 128
    bc_block = inner // (2 * state_dim)
    dt_block = (inner + 2 * state_dim) // 128
    hops = (doc_ids.shape[1] // 4 - 2) // length + 1
    hops = min(hops, seq_count - 1)

    w_x = gather_rows(jnp.pad(in_weight[:, inner:].astype(BF16), ((0, 0), (0, x_pad))))
    w_z = gather_rows(in_weight[:, :inner].astype(BF16))
    w_out = gather_rows(out_weight.astype(BF16))

    docs_all = jnp.concatenate([jnp.full((HALO,), -1, jnp.int32), doc_ids[0]])
    docs_ext = lax.dynamic_slice_in_dim(docs_all, seq_index * length, length + HALO, 0)
    docs = docs_ext[HALO:].reshape(chunks, CHUNK)
    windows = jnp.stack([docs_ext[c * CHUNK : (c + 1) * CHUNK + HALO] for c in range(chunks)])
    at_t = jnp.arange(CHUNK)
    at_s = jnp.arange(CHUNK + HALO)
    back = jnp.arange(1, TAPS)
    hits = (at_s[None, None, :] == at_t[None, :, None] + HALO - back[:, None, None])[None] & (
        windows[:, None, None, :] == docs[:, None, :, None]
    )
    shifts = hits.astype(BF16).reshape(chunks, (TAPS - 1) * CHUNK, CHUNK + HALO)
    hits_t = (at_s[:, None, None] == at_t[None, None, :] + HALO - back[None, :, None])[None] & (
        windows[:, :, None, None] == docs[:, None, None, :]
    )
    shifts_t = hits_t.astype(BF16).reshape(chunks, CHUNK + HALO, (TAPS - 1) * CHUNK)
    mask = ((docs[:, :, None] == docs[:, None, :]) & (at_t[None, :] <= at_t[:, None])[None]).astype(F32)
    mask = mask.reshape(length, CHUNK)
    enters = docs == windows[:, HALO - 1 : HALO]
    leaves = docs == docs[:, CHUNK - 1 :]
    enters_device = docs == docs_ext[HALO - 1]
    cols = jnp.stack([enters, leaves, enters_device], axis=-1).reshape(length, 3).astype(F32)
    cols = jnp.pad(cols, ((0, 0), (0, 125)))

    part = jnp.arange(128)[:, None]
    in_use = part < 3 * heads
    expand = ((part % heads == jnp.arange(inner)[None, :] // HEAD) & in_use).astype(BF16)
    select = ((part % heads == jnp.arange(heads * CHUNK)[None, :] // CHUNK) & in_use).astype(BF16)
    owner = jnp.arange(inner)[:, None] // HEAD
    lane = jnp.arange(384)[None, :]
    collect = (owner + (lane // 128) * heads == lane % 128).astype(BF16)

    rate = -jnp.exp(decay_log)
    head_rows = jnp.pad(jnp.stack([step_bias, rate * LOG2E, rate, skip_gain]), ((0, 4), (0, 128 - heads)))
    skip_row = jnp.pad(jnp.repeat(skip_gain, HEAD), (0, 2 * state_dim))
    conv_rows = jnp.concatenate([conv_weight, conv_bias[None], skip_row[None]], axis=0)
    conv_rows = jnp.pad(conv_rows, ((0, 2), (0, 0)))
    gain_rows = jnp.broadcast_to(out_gain[None], (8, inner))

    tail = lax.ppermute(hidden[0, length - HALO :], SEQ, [(i, i + 1) for i in range(seq_count - 1)])
    tokens = jnp.concatenate([tail, hidden[0]], axis=0).astype(F32)
    ratio_ext = lax.rsqrt(jnp.mean(tokens * tokens, axis=-1, keepdims=True) + EPS)
    normed_ext = (tokens * ratio_ext * norm_gain[None, :]).astype(BF16)
    tokens, ratio, normed = tokens[HALO:], ratio_ext[HALO:], normed_ext[HALO:]
    proj_x = mm(normed_ext, w_x).astype(BF16)
    gate = mm(normed, w_z).astype(BF16)
    grad_final = mm_cols(cotangent[0], w_out)

    bc_spec = pl.BlockSpec((length + HALO, 2 * state_dim), lambda i: (0, bc_block))
    dt_spec = pl.BlockSpec((length + HALO, 128), lambda i: (0, dt_block))
    bc_rows = conv_rows[:, inner:]
    outs = [
        shape((length, 256), BF16), shape((length, 256), BF16), shape((256, length), BF16), shape((256, length), BF16),
        shape((length, 128)), shape((length, 128)), shape((length, 128), BF16), shape((length, 128), BF16),
        shape((length, 128), BF16), shape((length, 128), BF16), shape((length, 128), BF16),
        shape((chunks, heads, CHUNK)), shape((8, 128)),
    ]
    ins = [shifts, mask, cols, bc_rows, head_rows]
    b_act, c_act, b_t, c_t, gram, dt_full, dt, e, f, ed, la, cat, kept = pl.pallas_call(
        prep_kernel,
        grid=(1,),
        in_specs=[bc_spec, dt_spec] + [whole(a) for a in ins],
        out_specs=[whole(o) for o in outs],
        out_shape=outs,
        compiler_params=PARAMS,
        name="prep",
    )(proj_x, proj_x, *ins)
    kept_row = kept[0, :heads]

    steps = inner // LANES
    sel_width = (LANES // HEAD) * CHUNK
    x_rows = conv_rows[:, :inner]
    y_local, state_part = pl.pallas_call(
        fwd_kernel,
        grid=(steps,),
        in_specs=[
            lanes_block(proj_x), whole(shifts), lanes_block(x_rows), whole(gram), whole(c_act), whole(b_t),
            whole(dt), whole(e), whole(f), whole(la), lanes_block(select, sel_width), lanes_block(expand), whole(cat),
        ],
        out_specs=[pl.BlockSpec((length, LANES), lambda i: (0, i)), pl.BlockSpec((128, LANES), lambda i: (0, i))],
        out_shape=[shape((length, inner)), shape((128, inner), BF16)],
        compiler_params=PARAMS,
        name="scan_fwd",
    )(proj_x, shifts, x_rows, gram, c_act, b_t, dt, e, f, la, select, expand, cat)
    state_in = carried(state_part, kept_row, hops, 1)

    def rows_spec(cols_):
        return pl.BlockSpec((CHUNK, cols_), lambda i: (i, 0))

    output, final, grad_gate, grad_mixed, q, gain_part, grad_state = pl.pallas_call(
        gate_kernel,
        grid=(chunks,),
        in_specs=[
            rows_spec(inner), rows_spec(inner), rows_spec(256), pl.BlockSpec((256, CHUNK), lambda i: (0, i)),
            rows_spec(128), whole(state_in), whole(w_out), whole(expand),
            pl.BlockSpec((inner, 128), lambda i: (0, 0)), whole(gain_rows), rows_spec(width), rows_spec(inner),
        ],
        out_specs=[
            rows_spec(width), rows_spec(inner), rows_spec(inner), rows_spec(inner), rows_spec(128),
            pl.BlockSpec((8, inner), lambda i: (0, 0)), pl.BlockSpec((128, inner), lambda i: (0, 0)),
        ],
        out_shape=[
            shape((length, width), BF16), shape((length, inner), BF16), shape((length, inner), BF16),
            shape((length, inner), BF16), shape((length, 128)), shape((8, inner)), shape((128, inner), BF16),
        ],
        scratch_shapes=[pltpu.VMEM((128, inner), F32)],
        compiler_params=PARAMS,
        name="gate",
    )(y_local, gate, c_act, c_t, ed, state_in, w_out, expand, collect, gain_rows, hidden[0], grad_final)
    grad_in = carried(grad_state, kept_row, hops, -1)

    out_weight_part = mm_rows(final, cotangent[0])
    in_z_part = mm_rows(normed, grad_gate)
    grad_normed_z = mm_cols(grad_gate, w_z)

    block = lambda rows_: pl.BlockSpec((rows_, LANES), lambda i: (0, i))
    acc = lambda rows_, cols_: pl.BlockSpec((rows_, cols_), lambda i: (0, 0))
    grad_x, edge_x, cg_x, pair_sum, dcb, red, ends = pl.pallas_call(
        back_kernel,
        grid=(steps,),
        in_specs=[
            lanes_block(proj_x), lanes_block(grad_mixed), whole(shifts), whole(shifts_t), lanes_block(x_rows),
            whole(gram), whole(b_act), whole(b_t), whole(c_t), whole(dt), whole(e), whole(f), whole(la),
            lanes_block(select, sel_width), lanes_block(expand), pl.BlockSpec((LANES, 384), lambda i: (i, 0)),
            whole(cat), lanes_block(state_in), lanes_block(grad_in),
        ],
        out_specs=[
            block(length), block(2 * HALO), block(8), acc(length, 128), acc(length, 256), acc(length, 128), block(8),
        ],
        out_shape=[
            shape((length, inner), BF16), shape((2 * HALO, inner)), shape((8, inner)), shape((length, 128)),
            shape((length, 256)), shape((length, 128)), shape((8, inner)),
        ],
        scratch_shapes=[
            pltpu.VMEM((length, LANES), F32), pltpu.VMEM((chunks, 128, LANES), F32),
            pltpu.VMEM((length + HALO, LANES), F32),
        ],
        compiler_params=PARAMS,
        name="scan_bwd",
    )(proj_x, grad_mixed, shifts, shifts_t, x_rows, gram, b_act, b_t, c_t, dt, e, f, la, select, expand, collect,
      cat, state_in, grad_in)

    ins = [shifts, shifts_t, mask, bc_rows, head_rows, b_act, c_act, pair_sum, dcb, red, ends, collect, q, dt_full]
    in_specs = [whole(a) for a in ins]
    in_specs[11] = acc(inner, 128)
    outs = [
        shape((length, 2 * state_dim), BF16), shape((length, 128), BF16), shape((2 * HALO, 2 * state_dim)),
        shape((8, 2 * state_dim)), shape((8, 128)),
    ]
    grad_bc, grad_dt, edge_bc, cg_bc, head_grads = pl.pallas_call(
        post_kernel,
        grid=(1,),
        in_specs=[bc_spec, dt_spec] + in_specs,
        out_specs=[whole(o) for o in outs],
        out_shape=outs,
        scratch_shapes=[pltpu.VMEM((length + HALO, 2 * state_dim), F32)],
        compiler_params=PARAMS,
        name="post",
    )(proj_x, proj_x, *ins)

    edge = jnp.concatenate([edge_x, edge_bc], axis=1)
    from_next = shift_seq(edge[:HALO], -1)
    last_rows = (edge[HALO:] + from_next).astype(BF16)
    grad_conv = jnp.concatenate([grad_x, grad_bc], axis=1)
    grad_conv = jnp.concatenate([grad_conv[: length - HALO], last_rows], axis=0)
    grad_proj_x = jnp.concatenate([grad_conv, grad_dt], axis=1)

    in_x_part = mm_rows(normed, grad_proj_x)
    grad_normed = grad_normed_z + mm_cols(grad_proj_x, w_x)
    norm_gain_part = jnp.sum(grad_normed * tokens * ratio, axis=0)
    scaled_in = grad_normed * norm_gain[None, :]
    input_grad = (
        cotangent[0].astype(F32)
        + ratio * scaled_in
        - tokens * ratio * ratio * ratio * jnp.mean(scaled_in * tokens, axis=-1, keepdims=True)
    )

    small = jnp.concatenate(
        [
            norm_gain_part,
            jnp.sum(gain_part, axis=0),
            jnp.concatenate([cg_x, cg_bc], axis=1)[: TAPS + 1].reshape(-1),
            head_grads[:3, :heads].reshape(-1),
        ]
    )
    small = lax.psum(small, (SEQ, WT))
    at = 0
    pieces = []
    for size in (width, inner, TAPS * conv_bias.shape[0], conv_bias.shape[0], heads, heads, heads):
        pieces.append(small[at : at + size])
        at += size
    norm_total, gain_total, conv_w_total, conv_b_total, step_total, decay_total, skip_total = pieces

    out_grad = reduce_rows(out_weight_part).astype(F32)
    in_z = reduce_rows(in_z_part)
    in_x = reduce_rows(in_x_part)
    in_grad = jnp.concatenate([in_z, in_x[:, :x_cols]], axis=1).astype(F32)
    return (
        output[None], input_grad[None], norm_total, in_grad, conv_w_total.reshape(conv_weight.shape), conv_b_total,
        step_total, decay_total, skip_total, gain_total, out_grad,
    )


def solution(mesh):
    placed = (
        P(WT, SEQ, None), P(WT, None), P(), P(WT, None), P(), P(), P(), P(), P(), P(), P(WT, None), P(WT, SEQ, None),
    )
    return jax.shard_map(
        on_device,
        mesh=mesh,
        in_specs=placed,
        out_specs=(
            P(WT, SEQ, None), P(WT, SEQ, None), P(), P(WT, None), P(), P(), P(), P(), P(), P(), P(WT, None),
        ),
        check_vma=False,
    )
```

```python
import functools

import jax
import jax.numpy as jnp
import ml_dtypes
import numpy as np
from jax import lax
from jax.experimental import pallas as pl
from jax.experimental.pallas import tpu as pltpu
from jax.sharding import PartitionSpec as P

EPS = 1e-05
LOG2E = 1.4426950408889634
CHUNK = 128
HALO = 16
LANES = 256
HEAD = 64
TAPS = 4
FULL = lax.Precision.HIGHEST
F32 = jnp.float32
BF16 = jnp.bfloat16
SEQ = "seq"
WT = "wt"


def mm(a, b):
    return jnp.dot(a, b, preferred_element_type=F32)


def mm_cols(a, b):
    return lax.dot_general(a, b, (((1,), (1,)), ((), ())), preferred_element_type=F32)


def mm_rows(a, b):
    return lax.dot_general(a, b, (((0,), (0,)), ((), ())), preferred_element_type=F32)


def sigmoid(x):
    return 0.5 * jnp.tanh(0.5 * x) + 0.5


def split2(x):
    high = x.astype(BF16)
    return high, (x - high.astype(F32)).astype(BF16)


def mm_split(x, ones):
    high, low = split2(x)
    return mm(high, ones) + mm(low, ones)


def mm3(a, b, mult=mm):
    a_high, a_low = a if isinstance(a, tuple) else split2(a)
    b_high, b_low = b if isinstance(b, tuple) else split2(b)
    return mult(a_high, b_high) + mult(a_high, b_low) + mult(a_low, b_high)


def pack3(x):
    high = x.astype(BF16).astype(F32)
    rest = x - high
    mid = rest.astype(BF16).astype(F32)
    low = rest - mid
    return (high + pltpu.roll(mid, 32, 1) + pltpu.roll(low, 64, 1)).astype(BF16)


def softplus(x):
    small = jnp.exp(-jnp.abs(x))
    series = small * (1.0 - small * (0.5 - small * (1.0 / 3.0 - small * (0.25 - small * 0.2))))
    return jnp.maximum(x, 0.0) + jnp.where(small < 0.02, series, jnp.log(1.0 + small))


def conv_inputs(window, shifts):
    moved = mm(shifts, window)
    return [window[HALO:].astype(F32)] + [
        moved[j * CHUNK : (j + 1) * CHUNK] for j in range(TAPS - 1)
    ]


def conv_sum(taps, cw):
    total = cw[TAPS : TAPS + 1]
    for j in range(TAPS):
        total = total + cw[j : j + 1] * taps[j]
    return total


def pair_cols(x):
    return x[:, :128], x[:, 128:]


def pair_rows(x):
    return x[:128], x[128:]


def rows_of(c):
    return slice(c * CHUNK, (c + 1) * CHUNK)


def window_of(c):
    return slice(c * CHUNK, (c + 1) * CHUNK + HALO)


def prep_kernel(
    bc_ref, dtr_ref, sh_ref, mask_ref, cols_ref, cw_ref, hp_ref,
    b_ref, c_ref, bt_ref, ct_ref, gm_ref, dtf_ref, dt_ref, e_ref, f_ref, ed_ref, la_ref, cat_ref, kept_ref,
):
    row = lax.broadcasted_iota(jnp.int32, (CHUNK, CHUNK), 0)
    col = lax.broadcasted_iota(jnp.int32, (CHUNK, CHUNK), 1)
    lower = jnp.where(col <= row, 1.0, 0.0).astype(F32)
    used = col < 32
    heads = cat_ref.shape[1]
    before = jnp.zeros((1, CHUNK), F32)
    cw = cw_ref[...]
    for c in range(sh_ref.shape[0]):
        rows = rows_of(c)
        taps = conv_inputs(bc_ref[window_of(c)], sh_ref[c])
        k = conv_sum(taps, cw)
        act = k * sigmoid(k)
        b_act, c_act = act[:, :128], act[:, 128:]
        b_high, b_low = split2(b_act)
        c_high, c_low = split2(c_act)
        gram = mm_cols(c_high, b_high) + mm_cols(c_high, b_low) + mm_cols(c_low, b_high)
        gm_ref[rows] = gram * mask_ref[rows]
        b_ref[rows] = jnp.concatenate([b_high, b_low], axis=1)
        c_ref[rows] = jnp.concatenate([c_high, c_low], axis=1)
        bt_ref[:, rows] = jnp.concatenate(split2(b_act.T), axis=0)
        ct_ref[:, rows] = jnp.concatenate(split2(c_act.T), axis=0)
        step_in = dtr_ref[c * CHUNK + HALO : (c + 1) * CHUNK + HALO].astype(F32) + hp_ref[0:1]
        dt = jnp.where(used, softplus(step_in), 0.0)
        cumul = jnp.dot(lower, dt * hp_ref[1:2], precision=FULL, preferred_element_type=F32)
        last = cumul[CHUNK - 1 : CHUNK]
        cols = cols_ref[rows]
        e = jnp.where(used, jnp.exp2(cumul) * cols[:, 0:1], 0.0)
        f = jnp.where(used, jnp.exp2(last - cumul) * cols[:, 1:2], 0.0)
        ed = jnp.where(used, jnp.exp2(before + cumul) * cols[:, 2:3], 0.0)
        before = before + last
        dtf_ref[rows] = dt
        dt_ref[rows] = pack3(dt)
        e_ref[rows] = pack3(e)
        f_ref[rows] = pack3(f)
        ed_ref[rows] = pack3(ed)
        la_ref[rows] = pack3(cumul)
        cat_ref[c] = cumul.T[:heads]
        kept_ref[...] = jnp.broadcast_to(ed[CHUNK - 1 : CHUNK], kept_ref.shape)


def weights_of(c, step, la_ref, sel, cat_ref):
    spread = mm(la_ref[rows_of(c)], sel)
    per_step = LANES // HEAD
    out = []
    for i in range(per_step):
        ahead = cat_ref[c, pl.ds(step * per_step + i, 1), :]
        out.append(jnp.exp2(jnp.minimum(spread[:, i * CHUNK : (i + 1) * CHUNK] - ahead, 0.0)))
    return out


def head_pairs(x):
    first = lax.broadcasted_iota(jnp.int32, x.shape, 1) < HEAD
    zero = jnp.zeros_like(x)
    return jnp.concatenate([jnp.where(first, x, zero), jnp.where(first, zero, x)], axis=0)


def fwd_kernel(
    x_ref, sh_ref, cw_ref, gm_ref, c_ref, bt_ref, dt_ref, e_ref, f_ref, la_ref, sel_ref, exp_ref, cat_ref,
    y_ref, s_ref,
):
    step = pl.program_id(0)
    cw, sel, expand = cw_ref[...], sel_ref[...], exp_ref[...]
    state = jnp.zeros((128, LANES), F32)
    for c in range(sh_ref.shape[0]):
        rows = rows_of(c)
        k = conv_sum(conv_inputs(x_ref[window_of(c)], sh_ref[c]), cw)
        xa = k * sigmoid(k)
        v = mm(dt_ref[rows], expand) * xa
        ex = mm(e_ref[rows], expand)
        fx = mm(f_ref[rows], expand)
        v_parts = split2(v)
        gm = gm_ref[rows]
        weights = [w * gm for w in weights_of(c, step, la_ref, sel, cat_ref)]
        local = []
        for p in range(LANES // 128):
            own = tuple(head_pairs(part[:, p * 128 : (p + 1) * 128]) for part in v_parts)
            local.append(mm3(jnp.concatenate(weights[2 * p : 2 * p + 2], axis=1), own))
        y = jnp.concatenate(local, axis=1) + ex * mm3(pair_cols(c_ref[rows]), state)
        y_ref[rows] = y + cw[5:6] * xa
        state = ex[CHUNK - 1 : CHUNK] * state + mm3(pair_rows(bt_ref[:, rows]), fx * v)
    s_ref[...] = state.astype(BF16)


def gate_kernel(
    idx_ref, y_ref, z_ref, c_ref, ct_ref, ed_ref, sin_ref, wo_ref, exp_ref, expt_ref, gain_ref, hid_ref, df_ref,
    out_ref, fin_ref, fin_far_ref, dz_ref, dz_near_ref, dz_far_ref, dy_ref, q_ref, og_ref, gs_ref, acc_ref,
):
    i = pl.program_id(0)

    @pl.when(i == 0)
    def _():
        og_ref[...] = jnp.zeros_like(og_ref)
        acc_ref[...] = jnp.zeros_like(acc_ref)

    gain = gain_ref[0:1]
    inner = y_ref.shape[1]
    edx = mm(ed_ref[...], exp_ref[...])
    y_full = y_ref[...] + edx * (mm(c_ref[:, :128], sin_ref[...]) + mm(c_ref[:, 128:], sin_ref[...]))
    y = y_full.astype(BF16).astype(F32)
    z = z_ref[...].astype(F32)
    sig = sigmoid(z)
    sz = z * sig
    gated = y * sz
    gnorm = lax.rsqrt(jnp.sum(gated * gated, axis=1, keepdims=True) * (1.0 / inner) + EPS)
    normal = gated * gnorm
    final = (normal * gain).astype(BF16)
    first_core = idx_ref[2] == 0
    block = inner // 8
    for part in range(4):
        a = final[:, 2 * part * block : (2 * part + 1) * block]
        b = final[:, (2 * part + 1) * block : (2 * part + 2) * block]
        fin_ref[:, part * block : (part + 1) * block] = jnp.where(first_core, a, b)
        fin_far_ref[:, part * block : (part + 1) * block] = jnp.where(first_core, b, a)
    out_ref[...] = (hid_ref[...].astype(F32) + mm(final, wo_ref[...])).astype(BF16)
    dfinal = df_ref[...]
    share = dfinal * normal
    og_ref[...] += jnp.sum(share.reshape(-1, 8, inner), axis=0)
    e = dfinal * gain
    mean = jnp.sum(share * gain, axis=1, keepdims=True) * (1.0 / inner)
    dgated = gnorm * (e - normal * mean)
    dz = (dgated * y * (sig * (1.0 + z * (1.0 - sig)))).astype(BF16)
    dz_ref[...] = dz
    dz_near_ref[...] = jnp.where(first_core, dz[:, : inner // 2], dz[:, inner // 2 :])
    dz_far_ref[...] = jnp.where(first_core, dz[:, inner // 2 :], dz[:, : inner // 2])
    dyb = (dgated * sz).astype(BF16)
    dy_ref[...] = dyb
    dy = dyb.astype(F32)
    q_ref[...] = mm_split(dy * y_full, expt_ref[...])
    acc_ref[...] += mm3(pair_rows(ct_ref[...]), edx * dy)

    @pl.when(i == pl.num_programs(0) - 1)
    def _():
        gs_ref[...] = acc_ref[...].astype(BF16)


def back_kernel(
    x_ref, dy_ref, sh_ref, sht_ref, cw_ref, gm_ref, b_ref, bt_ref, ct_ref, dt_ref, e_ref, f_ref, la_ref,
    sel_ref, exp_ref, expt_ref, cat_ref, sin_ref, din_ref,
    dx_ref, edge_ref, cg_ref, m_ref, dcb_ref, red_ref, sd_ref,
    k_ref, states_ref, dxw_ref,
    *, first,
):
    step = pl.program_id(0) + first

    @pl.when(pl.program_id(0) == 0)
    def _():
        m_ref[...] = jnp.zeros_like(m_ref)
        dcb_ref[...] = jnp.zeros_like(dcb_ref)
        red_ref[...] = jnp.zeros_like(red_ref)

    count = sh_ref.shape[0]
    cw, sel, expand = cw_ref[...], sel_ref[...], exp_ref[...]
    state = sin_ref[...].astype(F32)
    for c in range(count):
        rows = rows_of(c)
        k = conv_sum(conv_inputs(x_ref[window_of(c)], sh_ref[c]), cw)
        k_ref[rows] = k
        v = mm(dt_ref[rows], expand) * (k * sigmoid(k))
        ex_last = mm(e_ref[rows], expand)[CHUNK - 1 : CHUNK]
        fx = mm(f_ref[rows], expand)
        states_ref[c] = state
        state = ex_last * state + mm3(pair_rows(bt_ref[:, rows]), fx * v)
    grad = din_ref[...].astype(F32)
    cg = [jnp.zeros((8, LANES), F32) for _ in range(TAPS + 1)]
    sd_ref[...] = jnp.zeros_like(sd_ref)
    after = state
    for c in reversed(range(count)):
        rows = rows_of(c)
        gradb = grad.astype(BF16)
        sd_ref[c : c + 1] = jnp.sum(after * grad, axis=0, keepdims=True)
        after = states_ref[c]
        taps = conv_inputs(x_ref[window_of(c)], sh_ref[c])
        k = k_ref[rows]
        sig = sigmoid(k)
        xa = k * sig
        dtx = mm(dt_ref[rows], expand)
        ex = mm(e_ref[rows], expand)
        fx = mm(f_ref[rows], expand)
        v = dtx * xa
        vb = v.astype(BF16)
        dyb = dy_ref[rows]
        dy = dyb.astype(F32)
        gm = gm_ref[rows]
        weights = weights_of(c, step, la_ref, sel, cat_ref)
        dv = []
        total = None
        for p in range(LANES // 128):
            lanes = slice(p * 128, (p + 1) * 128)
            pair = weights[2 * p : 2 * p + 2]
            products = mm_cols(dyb[:, lanes], head_pairs(vb[:, lanes]))
            part = products[:, :CHUNK] * pair[0] + products[:, CHUNK:] * pair[1]
            total = part if total is None else total + part
            stacked = jnp.concatenate([w * gm for w in pair], axis=0)
            own = head_pairs(dyb[:, lanes])
            high, low = split2(stacked)
            dv.append(mm_rows(high, own) + mm_rows(low, own))
        m_ref[rows] += total
        dv = jnp.concatenate(dv, axis=1) + fx * mm3(pair_cols(b_ref[rows]), grad)
        edy = ex * dy
        edyb = edy.astype(BF16)
        dcb_ref[rows, 0:128] += mm_cols((fx * v).astype(BF16), gradb)
        dcb_ref[rows, 128:256] += mm_cols(edyb, after.astype(BF16))
        grad = ex[CHUNK - 1 : CHUNK] * grad + mm3(pair_rows(ct_ref[:, rows]), edy)
        red = mm_split(xa * dv, expt_ref[:, 0:128])
        red += mm_split(v * dv, expt_ref[:, 128:256])
        red += mm_split(dy * xa, expt_ref[:, 256:384])
        red_ref[rows] += red
        dxa = dtx * dv + cw[5:6] * dy
        dk = dxa * (sig * (1.0 + k * (1.0 - sig)))
        cg[TAPS] += jnp.sum(dk.reshape(-1, 8, LANES), axis=0)
        for j in range(TAPS):
            cg[j] += jnp.sum((dk * taps[j]).reshape(-1, 8, LANES), axis=0)
        shifted = jnp.concatenate([(cw[j : j + 1] * dk).astype(BF16) for j in range(1, TAPS)], axis=0)
        moved = mm(sht_ref[c], shifted)
        low, high = c * CHUNK, (c + 1) * CHUNK
        own = cw[0:1] * dk
        dxw_ref[low : low + HALO] = moved[:HALO]
        dxw_ref[low + HALO : high] = moved[HALO:CHUNK] + own[: CHUNK - HALO]
        end = moved[CHUNK:] + own[CHUNK - HALO :]
        if c == count - 1:
            dxw_ref[high : high + HALO] = end
        else:
            dxw_ref[high : high + HALO] += end
    cg_ref[...] = jnp.zeros_like(cg_ref)
    for j in range(TAPS + 1):
        cg_ref[j : j + 1] = jnp.sum(cg[j], axis=0, keepdims=True)
    dx_ref[...] = dxw_ref[HALO:].astype(BF16)
    edge_ref[:HALO] = dxw_ref[:HALO]
    edge_ref[HALO:] = dxw_ref[count * CHUNK :]


def post_kernel(
    bc_ref, dtr_ref, sh_ref, sht_ref, mask_ref, cw_ref, hp_ref, b_ref, c_ref, m0_ref, m1_ref, dcb0_ref, dcb1_ref,
    red0_ref, red1_ref, sd0_ref, sd1_ref, expt_ref, q_ref, dtf_ref,
    dbcd_ref, edge_ref, cg_ref, hg_ref,
    dxw_ref,
):
    count = sh_ref.shape[0]
    cw = cw_ref[...]
    width = bc_ref.shape[1]
    row = lax.broadcasted_iota(jnp.int32, (CHUNK, CHUNK), 0)
    col = lax.broadcasted_iota(jnp.int32, (CHUNK, CHUNK), 1)
    upper = jnp.where(col >= row, 1.0, 0.0).astype(F32)
    used = col < 32
    cg = [jnp.zeros((8, width), F32) for _ in range(TAPS + 1)]
    step_grad = jnp.zeros((8, CHUNK), F32)
    decay_grad = jnp.zeros((8, CHUNK), F32)
    skip_grad = jnp.zeros((8, CHUNK), F32)
    half = sd0_ref.shape[1]
    ends = mm_split(sd0_ref[...], expt_ref[:half]) + mm_split(sd1_ref[...], expt_ref[half:])
    rate = hp_ref[2:3]
    for c in reversed(range(count)):
        rows = rows_of(c)
        taps = conv_inputs(bc_ref[window_of(c)], sh_ref[c])
        k = conv_sum(taps, cw)
        sig = sigmoid(k)
        both = ((m0_ref[rows] + m1_ref[rows]) * mask_ref[rows]).astype(BF16)
        dcb = dcb0_ref[rows] + dcb1_ref[rows]
        db = mm_rows(both, c_ref[rows, :128]) + dcb[:, :128]
        dc = mm(both, b_ref[rows, :128]) + dcb[:, 128:]
        dk = jnp.concatenate([db, dc], axis=1) * (sig * (1.0 + k * (1.0 - sig)))
        cg[TAPS] += jnp.sum(dk.reshape(-1, 8, width), axis=0)
        for j in range(TAPS):
            cg[j] += jnp.sum((dk * taps[j]).reshape(-1, 8, width), axis=0)
        shifted = jnp.concatenate([(cw[j : j + 1] * dk).astype(BF16) for j in range(1, TAPS)], axis=0)
        moved = mm(sht_ref[c], shifted)
        low, high = c * CHUNK, (c + 1) * CHUNK
        own = cw[0:1] * dk
        dxw_ref[low : low + HALO] = moved[:HALO]
        dxw_ref[low + HALO : high] = moved[HALO:CHUNK] + own[: CHUNK - HALO]
        end = moved[CHUNK:] + own[CHUNK - HALO :]
        if c == count - 1:
            dxw_ref[high : high + HALO] = end
        else:
            dxw_ref[high : high + HALO] += end
        red = red0_ref[rows] + red1_ref[rows]
        xdv = red
        vdv = pltpu.roll(red, 96, 1)
        dyx = pltpu.roll(red, 64, 1)
        change = q_ref[rows] - hp_ref[3:4] * dyx - vdv
        change = jnp.where(used, change, 0.0)
        da = jnp.dot(upper, change, precision=FULL, preferred_element_type=F32) + ends[c : c + 1]
        dt = dtf_ref[rows]
        step_in = dtr_ref[c * CHUNK + HALO : (c + 1) * CHUNK + HALO].astype(F32) + hp_ref[0:1]
        ddt = jnp.where(used, (xdv + rate * da) * sigmoid(step_in), 0.0)
        dbcd_ref[rows, width:] = ddt.astype(BF16)
        step_grad += jnp.sum(ddt.reshape(-1, 8, CHUNK), axis=0)
        decay_grad += jnp.sum((dt * da).reshape(-1, 8, CHUNK), axis=0)
        skip_grad += jnp.sum(dyx.reshape(-1, 8, CHUNK), axis=0)
    cg_ref[...] = jnp.zeros_like(cg_ref)
    for j in range(TAPS + 1):
        cg_ref[j : j + 1] = jnp.sum(cg[j], axis=0, keepdims=True)
    dbcd_ref[:, :width] = dxw_ref[HALO:].astype(BF16)
    edge_ref[:HALO] = dxw_ref[:HALO]
    edge_ref[HALO:] = dxw_ref[count * CHUNK :]
    hg_ref[...] = jnp.zeros_like(hg_ref)
    hg_ref[0:1] = jnp.sum(step_grad, axis=0, keepdims=True)
    hg_ref[1:2] = rate * jnp.sum(decay_grad, axis=0, keepdims=True)
    hg_ref[2:3] = jnp.sum(skip_grad, axis=0, keepdims=True)


def whole(array):
    return pl.BlockSpec(array.shape, lambda *_: (0,) * array.ndim)


def lanes_block(array, width=LANES, first=0):
    return pl.BlockSpec((array.shape[0], width), lambda i: (0, first + i))


def shape(dims, dtype=F32):
    return jax.ShapeDtypeStruct(dims, dtype)


PARAMS = pltpu.CompilerParams(vmem_limit_bytes=56 * 1024 * 1024, dimension_semantics=("arbitrary",))


def cost(micros):
    return pl.CostEstimate(flops=int(micros * 1.1e9), transcendentals=0, bytes_accessed=0)


def gather_rows(part):
    count = lax.axis_size(SEQ)
    share = part.shape[0] // count
    mine = lax.dynamic_slice_in_dim(part, lax.axis_index(SEQ) * share, share, 0)
    return lax.all_gather(mine, (WT, SEQ), axis=0, tiled=True)


def reduce_rows(part):
    count = lax.axis_size(SEQ)
    part = part.reshape(lax.axis_size(WT), count, -1, part.shape[1]).transpose(1, 0, 2, 3).reshape(part.shape)
    mine = lax.psum_scatter(part, SEQ, scatter_dimension=0, tiled=True)
    mine = lax.psum_scatter(mine, WT, scatter_dimension=0, tiled=True)
    return lax.all_gather(mine, SEQ, axis=0, tiled=True)


PLANES = 4
CHIPS = 4


def to_chip(x, k):
    return lax.ppermute(x, SEQ, [(i, i ^ (2 * k)) for i in range(2 * CHIPS)])


def to_core(x):
    return lax.ppermute(x, SEQ, [(i, i ^ 1) for i in range(2 * CHIPS)])


def to_plane(x, k):
    return lax.ppermute(x, WT, [(i, (i + k) % PLANES) for i in range(PLANES)])


def copies_into(idx_ref, a_ref, b_ref, own, place, sem):
    z, q, c = idx_ref[0], idx_ref[1], idx_ref[2]
    copies = own(z)
    for j in range(CHIPS):
        for k in range(1, PLANES):
            plane = lax.rem(z + PLANES - k, PLANES)
            chip = lax.bitwise_xor(q, j)
            at = j * (PLANES - 1) + k - 1
            copies += place(a_ref.at[at], plane, 2 * chip + c)
            copies += place(b_ref.at[at], plane, 2 * chip + 1 - c)
    return [pltpu.make_async_copy(source, target, sem) for source, target in copies]


def run(copies):
    for copy in copies:
        copy.start()
    for copy in copies:
        copy.wait()


def lanes_at(index, width=256):
    return pl.ds(pl.multiple_of(index * width, width), width)


def proj_x_kernel(idx_ref, own_ref, a_ref, b_ref, x_ref, out_ref, w_out_ref, w_ref, sem, sem_out):
    share = a_ref.shape[1]

    def place(source, plane, part):
        rows = pl.ds(pl.multiple_of(part * share, 16), share)
        return [(source, w_ref.at[rows, lanes_at(plane)])]

    def own(plane):
        return [(own_ref, w_ref.at[:, lanes_at(plane)])]

    run(copies_into(idx_ref, a_ref, b_ref, own, place, sem))
    keep = pltpu.make_async_copy(w_ref, w_out_ref, sem_out)
    keep.start()
    rows = w_ref.shape[0]
    for first in range(0, rows, 512):
        last = min(first + 512, rows)
        out_ref[:, first:last] = mm_cols(x_ref[...], w_ref[first:last]).astype(BF16)
    keep.wait()


def proj_z_kernel(
    idx_ref, oz_ref, oo_ref, a_ref, b_ref, x_ref, cot_ref,
    out_ref, df_ref, wz_out_ref, wo_out_ref, wz_ref, wo_ref, sem, sem_out,
):
    share = a_ref.shape[1] // 2
    rows = 2 * CHIPS * share

    def place(source, plane, part):
        to = pl.ds(pl.multiple_of(plane * rows + part * share, share), share)
        pairs = [(source.at[:share], wo_ref.at[to])]
        for i in range(wz_ref.shape[0] // rows):
            to = pl.ds(pl.multiple_of(i * rows + part * share, share), share)
            pairs.append((source.at[share:, 256 * i : 256 * (i + 1)], wz_ref.at[to, lanes_at(plane)]))
        return pairs

    def own(plane):
        return [(oz_ref, wz_ref.at[:, lanes_at(plane)]), (oo_ref, wo_ref.at[lanes_at(plane, rows)])]

    run(copies_into(idx_ref, a_ref, b_ref, own, place, sem))
    keep = [
        pltpu.make_async_copy(wz_ref, wz_out_ref, sem_out),
        pltpu.make_async_copy(wo_ref, wo_out_ref, sem_out),
    ]
    for copy in keep:
        copy.start()
    for first in range(0, wz_ref.shape[0], 512):
        cols = slice(first, first + 512)
        out_ref[:, cols] = mm_cols(x_ref[...], wz_ref[cols]).astype(BF16)
        df_ref[:, cols] = mm_cols(cot_ref[...], wo_ref[cols])
    for copy in keep:
        copy.wait()


def project(kernel, idx, gathered, ins, outs, kept, name):
    hbm = pl.BlockSpec(memory_space=pl.ANY)
    vmem = pl.BlockSpec(memory_space=pltpu.VMEM)
    return pl.pallas_call(
        kernel,
        in_specs=[pl.BlockSpec(memory_space=pltpu.SMEM)] + [hbm] * len(gathered) + [vmem] * len(ins),
        out_specs=[vmem] * len(outs) + [hbm] * len(kept),
        out_shape=outs + [shape(d, BF16) for d in kept],
        scratch_shapes=[pltpu.VMEM(d, BF16) for d in kept] + [pltpu.SemaphoreType.DMA, pltpu.SemaphoreType.DMA],
        compiler_params=pltpu.CompilerParams(vmem_limit_bytes=56 * 1024 * 1024),
        name=name,
        cost_estimate=cost(10),
    )(idx, *gathered, *ins)


def gather_far(mine, first=None, then=None):
    if first is None:
        return jnp.stack([to_plane(mine, k) for k in range(1, PLANES)])
    early, late = after(mine, first), after(mine, then)
    return jnp.stack([to_plane(early if k != 2 else late, k) for k in range(1, PLANES)])


def gather_plane(far):
    return jnp.concatenate([far] + [to_chip(far, k) for k in range(1, CHIPS)], axis=0)


def gather_last(plane):
    return plane, to_core(plane)


def keep_transposed(ref, near_ref, far_ref, cols):
    length = near_ref.shape[0]
    ref[:, :length] = near_ref[:, cols].T
    ref[:, length:] = far_ref[:, cols].T


def early_grads_kernel(idx_ref, n0_ref, n1_ref, f0_ref, f1_ref, dz0_ref, dz1_ref, g0_ref, g1_ref, *refs):
    outs, (dzt_ref, ft_ref) = refs[:CHIPS], refs[CHIPS:]
    block = 256
    length = n0_ref.shape[0]

    @pl.when(pl.program_id(0) == 0)
    def _():
        for k in range(CHIPS):
            rows = dzt_ref.at[k * block : (k + 1) * block]
            keep_transposed(rows, dz0_ref, dz1_ref, lanes_at(lax.bitwise_xor(idx_ref[1], k)))

    keep_transposed(ft_ref, f0_ref, f1_ref, slice(None))
    second = mm(dzt_ref[:, :length], n0_ref[...]) + mm(dzt_ref[:, length:], n1_ref[...])
    for k, out in enumerate(outs):
        lanes = lanes_at(lax.bitwise_xor(idx_ref[1], k))
        first = mm(ft_ref[:, :length], g0_ref[:, lanes]) + mm(ft_ref[:, length:], g1_ref[:, lanes])
        out[0, :block] = first.astype(out.dtype)
        out[0, block:] = second[k * block : (k + 1) * block].astype(out.dtype)


def late_grads_kernel(idx_ref, n0_ref, n1_ref, dx0_ref, dx1_ref, db0_ref, db1_ref, small_ref, *refs):
    outs, (dxt_ref, rest_ref) = refs[:CHIPS], refs[CHIPS:]
    block, share = 256, 64
    length = n0_ref.shape[0]
    q, c = idx_ref[1], idx_ref[2]

    @pl.when(pl.program_id(0) == 0)
    def _():
        for k in range(CHIPS):
            rows = dxt_ref.at[k * block : (k + 1) * block]
            keep_transposed(rows, dx0_ref, dx1_ref, lanes_at(lax.bitwise_xor(q, k)))
        keep_transposed(dxt_ref.at[CHIPS * block :], db0_ref, db1_ref, slice(None))

    total = mm(dxt_ref[:, :length], n0_ref[...]) + mm(dxt_ref[:, length:], n1_ref[...])
    rest_ref[...] = total[CHIPS * block :]
    high, low = split2(small_ref[...])
    small = jnp.concatenate([high.astype(F32), low.astype(F32)], axis=0)
    for k, out in enumerate(outs):
        chip = lax.bitwise_xor(q, k)
        main = total[k * block : (k + 1) * block]
        out[0, :block] = main.astype(out.dtype)

        @pl.when(chip < CHIPS - 1)
        def _(out=out, chip=chip):
            out[0, block:] = rest_ref[pl.ds(pl.multiple_of((2 * chip + c) * share, share), share)].astype(out.dtype)

        @pl.when(chip == CHIPS - 1)
        def _(out=out):
            out[0, block:] = small.astype(out.dtype)


def plane_blocks(rows, cols):
    return pl.BlockSpec((rows, cols), lambda i, idx: (0, lax.rem(idx[0] + i, PLANES)))


def grads_call(kernel, idx, blocked, full, rows, scratch, name):
    length = blocked[0].shape[0]
    out = lambda dtype: shape((PLANES, rows, 256), dtype)
    return pl.pallas_call(
        kernel,
        grid_spec=pltpu.PrefetchScalarGridSpec(
            num_scalar_prefetch=1,
            grid=(PLANES,),
            in_specs=[plane_blocks(length, a.shape[1] // PLANES) for a in blocked]
            + [pl.BlockSpec(a.shape, lambda i, idx, n=a.ndim: (0,) * n) for a in full],
            out_specs=[pl.BlockSpec((1, rows, 256), lambda i, idx: (i, 0, 0)) for _ in range(CHIPS)],
            scratch_shapes=scratch,
        ),
        out_shape=[out(F32)] + [out(BF16)] * (CHIPS - 1),
        compiler_params=PARAMS,
        name=name,
        cost_estimate=cost(9),
    )(idx, *blocked, *full)


SMALL = 32


def resplit(ref, total, rows, active):
    @pl.when(active)
    def _():
        high, low = split2(total[rows : rows + SMALL] + total[rows + SMALL : rows + 2 * SMALL])
        ref[rows : rows + SMALL] = high.astype(ref.dtype)
        ref[rows + SMALL : rows + 2 * SMALL] = low.astype(ref.dtype)


def chip_sum_kernel(idx_ref, own_ref, a_ref, b_ref, c_ref, *outs, small):
    for k, out in enumerate(outs):
        total = own_ref[k] + a_ref[k].astype(F32) + b_ref[k].astype(F32) + c_ref[k].astype(F32)
        out[...] = total.astype(out.dtype)
        if small:
            resplit(out, total, 256, idx_ref[1] == CHIPS - 1)


def plane_sum_kernel(idx_ref, own_ref, a_ref, b_ref, c_ref, out, *, small):
    total = own_ref[...] + a_ref[...].astype(F32) + b_ref[...].astype(F32) + c_ref[...].astype(F32)
    out[...] = total.astype(out.dtype)
    if small:
        resplit(out, total, 256, idx_ref[1] == CHIPS - 1)


def sum_call(kernel, idx, ins, dtypes, small, name):
    vmem = pl.BlockSpec(memory_space=pltpu.VMEM)
    return pl.pallas_call(
        functools.partial(kernel, small=small),
        in_specs=[pl.BlockSpec(memory_space=pltpu.SMEM)] + [vmem] * len(ins),
        out_specs=[vmem] * len(dtypes),
        out_shape=[shape(ins[0].shape[-2:], dtype) for dtype in dtypes],
        compiler_params=pltpu.CompilerParams(vmem_limit_bytes=56 * 1024 * 1024),
        cost_estimate=cost(2),
        name=name,
    )(idx, *ins)


def sum_over_chips(idx, parts, small=False):
    ins = [parts[0]] + [to_chip(parts[k], k) for k in range(1, CHIPS)]
    return sum_call(chip_sum_kernel, idx, ins, [F32] + [BF16] * (PLANES - 1), small, "chip_sum")


def sum_over_planes(idx, parts, small=False):
    ins = [parts[0]] + [to_plane(parts[k], k) for k in range(1, PLANES)]
    return sum_call(plane_sum_kernel, idx, ins, [BF16], small, "plane_sum")[0]


def share_in_plane(block):
    plane = jnp.stack([block] + [to_chip(block, k) for k in range(1, CHIPS)])
    return plane, to_core(plane)


def finish_kernel(idx_ref, ea_ref, eb_ref, la_ref, lb_ref, in_ref, out_ref, small_ref):
    q, c = idx_ref[1], idx_ref[2]
    block, share = 256, 64
    inner = 2 * CHIPS * block
    rest = in_ref.shape[0] - 2 * inner
    for j in range(CHIPS):
        chip = lax.bitwise_xor(q, j)
        for core, early, late in ((c, ea_ref, la_ref), (1 - c, eb_ref, lb_ref)):
            out_ref[lanes_at(core), lanes_at(chip)] = early[j, :block].astype(F32)
            row = (core * CHIPS + chip) * block
            in_ref[pl.ds(pl.multiple_of(row, block), block)] = early[j, block:].astype(F32)
            in_ref[pl.ds(pl.multiple_of(inner + row, block), block)] = late[j, :block].astype(F32)
            part = 2 * chip + core

            @pl.when(part < rest // share)
            def _(late=late, part=part, j=j):
                in_ref[pl.ds(pl.multiple_of(2 * inner + part * share, share), share)] = late[j, block:].astype(F32)

            @pl.when(part == rest // share)
            def _(late=late, j=j):
                in_ref[2 * inner + rest // share * share :] = late[j, block : block + rest % share].astype(F32)

            @pl.when(chip == CHIPS - 1)
            def _(late=late, core=core, j=j):
                total = late[j, block : block + SMALL].astype(F32) + late[j, block + SMALL :].astype(F32)
                small_ref[lanes_at(core, SMALL)] = total


def shift_seq(x, by):
    count = lax.axis_size(SEQ)
    pairs = [(i, i + by) for i in range(count) if 0 <= i + by < count]
    return lax.ppermute(x, SEQ, pairs)


def pass_on(part, kept, hops, sign):
    return [
        (shift_seq(part, sign * hop), shift_seq(kept, sign * hop) if hop < hops else None) for hop in range(1, hops + 1)
    ]


def entering(passed):
    total, fade = None, None
    for moved, kept in passed:
        moved = moved.astype(F32)
        if fade is not None:
            moved = moved * fade
        total = moved if total is None else total + moved
        if kept is not None:
            factor = jnp.repeat(kept, HEAD)[None, :]
            fade = factor if fade is None else fade * factor
    return total.astype(BF16)


def after(x, *others):
    return lax.optimization_barrier((x, others))[0]


def on_device(
    hidden, doc_ids, norm_gain, in_weight, conv_weight, conv_bias, step_bias, decay_log, skip_gain, out_gain,
    out_weight, cotangent,
):
    seq_count = lax.axis_size(SEQ)
    seq_index = lax.axis_index(SEQ)
    inner = out_gain.shape[0]
    heads = step_bias.shape[0]
    length = hidden.shape[1]
    state_dim = (conv_weight.shape[1] - inner) // 2
    width = hidden.shape[2]
    chunks = length // CHUNK
    x_cols = in_weight.shape[1] - inner
    x_pad = -x_cols % 128
    bc_block = inner // (2 * state_dim)
    dt_block = (inner + 2 * state_dim) // 128
    hops = (doc_ids.shape[1] // 4 - 2) // length + 1
    hops = min(hops, seq_count - 1)

    fast = (
        seq_count == 2 * CHIPS
        and lax.axis_size(WT) == PLANES
        and inner == seq_count * LANES
        and width == PLANES * 256
        and state_dim == 128
        and heads == 32
    )
    core = seq_index % 2
    idx = jnp.stack([lax.axis_index(WT), seq_index // 2, core]).astype(jnp.int32)
    shard = in_weight.T.astype(BF16)
    own_x = jnp.pad(shard[inner:], ((0, x_pad), (0, 0)))
    own_z = shard[:inner]
    own_out = out_weight.astype(BF16)
    if fast:
        share = own_x.shape[0] // seq_count
        far_x = gather_far(lax.dynamic_slice_in_dim(own_x, seq_index * share, share, 0))
        plane_x = gather_plane(far_x)
        doc_ids, out_weight, conv_weight, conv_bias, step_bias, decay_log, skip_gain, out_gain = after(
            (doc_ids, out_weight, conv_weight, conv_bias, step_bias, decay_log, skip_gain, out_gain), far_x
        )
        own_z = after(shard, far_x)[:inner]
        own_out = out_weight.astype(BF16)
        parts_x = (own_x, *gather_last(plane_x))
        rows = own_out.shape[0]
        share = rows // seq_count
        mine = [lax.dynamic_slice_in_dim(own_z, i * rows + seq_index * share, share, 0) for i in range(inner // rows)]
        mine = [lax.dynamic_slice_in_dim(own_out, seq_index * share, share, 0), jnp.concatenate(mine, axis=1)]
        far_rest = gather_far(jnp.concatenate(mine, axis=0), far_x, plane_x)
    else:
        w_x, w_z, w_out = gather_rows(own_x.T).T, gather_rows(own_z.T).T, gather_rows(own_out)

    docs_all = jnp.concatenate([jnp.full((HALO,), -1, jnp.int32), doc_ids[0]])
    docs_ext = lax.dynamic_slice_in_dim(docs_all, seq_index * length, length + HALO, 0)
    docs = docs_ext[HALO:].reshape(chunks, CHUNK)
    windows = jnp.stack([docs_ext[c * CHUNK : (c + 1) * CHUNK + HALO] for c in range(chunks)])
    at_t = jnp.arange(CHUNK)
    at_s = jnp.arange(CHUNK + HALO)
    back = jnp.arange(1, TAPS)
    hits = (at_s[None, None, :] == at_t[None, :, None] + HALO - back[:, None, None])[None] & (
        windows[:, None, None, :] == docs[:, None, :, None]
    )
    shifts = hits.astype(BF16).reshape(chunks, (TAPS - 1) * CHUNK, CHUNK + HALO)
    hits_t = (at_s[:, None, None] == at_t[None, None, :] + HALO - back[None, :, None])[None] & (
        windows[:, :, None, None] == docs[:, None, None, :]
    )
    shifts_t = hits_t.astype(BF16).reshape(chunks, CHUNK + HALO, (TAPS - 1) * CHUNK)
    mask = ((docs[:, :, None] == docs[:, None, :]) & (at_t[None, :] <= at_t[:, None])[None]).astype(F32)
    mask = mask.reshape(length, CHUNK)
    enters = docs == windows[:, HALO - 1 : HALO]
    leaves = docs == docs[:, CHUNK - 1 :]
    enters_device = docs == docs_ext[HALO - 1]
    cols = jnp.stack([enters, leaves, enters_device], axis=-1).reshape(length, 3).astype(F32)
    cols = jnp.pad(cols, ((0, 0), (0, 125)))

    part = np.arange(128)[:, None]
    in_use = part < 3 * heads
    expand = ((part % heads == np.arange(inner)[None, :] // HEAD) & in_use).astype(ml_dtypes.bfloat16)
    select = ((part % heads == np.arange(heads * CHUNK)[None, :] // CHUNK) & in_use).astype(ml_dtypes.bfloat16)
    owner = np.arange(inner)[:, None] // HEAD
    lane = np.arange(384)[None, :]
    collect = (owner + (lane // 128) * heads == lane % 128).astype(ml_dtypes.bfloat16)

    rate = -jnp.exp(decay_log)
    head_rows = jnp.pad(jnp.stack([step_bias, rate * LOG2E, rate, skip_gain]), ((0, 4), (0, 128 - heads)))
    skip_row = jnp.pad(jnp.repeat(skip_gain, HEAD), (0, 2 * state_dim))
    conv_rows = jnp.concatenate([conv_weight, conv_bias[None], skip_row[None]], axis=0)
    conv_rows = jnp.pad(conv_rows, ((0, 2), (0, 0)))
    gain_rows = jnp.broadcast_to(out_gain[None], (8, inner))

    tail = lax.ppermute(hidden[0, length - HALO :], SEQ, [(i, i + 1) for i in range(seq_count - 1)])
    tokens = jnp.concatenate([tail, hidden[0]], axis=0).astype(F32)
    ratio_ext = lax.rsqrt(jnp.mean(tokens * tokens, axis=-1, keepdims=True) + EPS)
    normed_ext = (tokens * ratio_ext * norm_gain[None, :]).astype(BF16)
    tokens, ratio, normed = tokens[HALO:], ratio_ext[HALO:], normed_ext[HALO:]
    if fast:
        x_width = x_cols + x_pad
        proj_x, w_x = project(
            proj_x_kernel, idx, parts_x, [normed_ext], [shape((length + HALO, x_width), BF16)], [(x_width, width)],
            "proj_x",
        )
        plane_rest = gather_plane(after(far_rest, parts_x[2]))
    else:
        proj_x = mm_cols(normed_ext, w_x).astype(BF16)
        gate = mm_cols(normed, w_z).astype(BF16)
        grad_final = mm_cols(cotangent[0], w_out)

    bc_spec = pl.BlockSpec((length + HALO, 2 * state_dim), lambda i: (0, bc_block))
    dt_spec = pl.BlockSpec((length + HALO, 128), lambda i: (0, dt_block))
    bc_rows = conv_rows[:, inner:]
    outs = [
        shape((length, 256), BF16), shape((length, 256), BF16), shape((256, length), BF16), shape((256, length), BF16),
        shape((length, 128)), shape((length, 128)), shape((length, 128), BF16), shape((length, 128), BF16),
        shape((length, 128), BF16), shape((length, 128), BF16), shape((length, 128), BF16),
        shape((chunks, heads, CHUNK)), shape((8, 128)),
    ]
    ins = [shifts, mask, cols, bc_rows, head_rows]
    b_act, c_act, b_t, c_t, gram, dt_full, dt, e, f, ed, la, cat, kept = pl.pallas_call(
        prep_kernel,
        grid=(1,),
        in_specs=[bc_spec, dt_spec] + [whole(a) for a in ins],
        out_specs=[whole(o) for o in outs],
        out_shape=outs,
        compiler_params=PARAMS,
        name="prep",
        cost_estimate=cost(4),
    )(proj_x, proj_x, *ins)
    kept_row = kept[0, :heads]

    steps = inner // LANES
    sel_width = (LANES // HEAD) * CHUNK
    x_rows = conv_rows[:, :inner]
    y_local, state_part = pl.pallas_call(
        fwd_kernel,
        grid=(steps,),
        in_specs=[
            lanes_block(proj_x), whole(shifts), lanes_block(x_rows), whole(gram), whole(c_act), whole(b_t),
            whole(dt), whole(e), whole(f), whole(la), lanes_block(select, sel_width), lanes_block(expand), whole(cat),
        ],
        out_specs=[pl.BlockSpec((length, LANES), lambda i: (0, i)), pl.BlockSpec((128, LANES), lambda i: (0, i))],
        out_shape=[shape((length, inner)), shape((128, inner), BF16)],
        compiler_params=PARAMS,
        name="scan_fwd",
        cost_estimate=cost(19),
    )(proj_x, shifts, x_rows, gram, c_act, b_t, dt, e, f, la, select, expand, cat)
    passed = pass_on(state_part, kept_row, hops, 1)
    if fast:
        parts_rest = (own_z, own_out, *gather_last(after(plane_rest, state_part)))
        gate, grad_final, w_z, w_out = project(
            proj_z_kernel, idx, parts_rest, [normed, cotangent[0]], [shape((length, inner), BF16), shape((length, inner))],
            [(inner, width), (inner, width)], "proj_z",
        )
        passed = after(passed, gate)
    state_in = entering(passed)

    def rows_spec(cols_):
        return pl.BlockSpec((CHUNK, cols_), lambda i: (i, 0))

    output, final, final_far, grad_gate, gate_near, gate_far, grad_mixed, q, gain_part, grad_state = pl.pallas_call(
        gate_kernel,
        grid=(chunks,),
        in_specs=[
            pl.BlockSpec(memory_space=pltpu.SMEM), rows_spec(inner), rows_spec(inner), rows_spec(256), pl.BlockSpec((256, CHUNK), lambda i: (0, i)),
            rows_spec(128), whole(state_in), whole(w_out), whole(expand),
            pl.BlockSpec((inner, 128), lambda i: (0, 0)), whole(gain_rows), rows_spec(width), rows_spec(inner),
        ],
        out_specs=[
            rows_spec(width), rows_spec(inner // 2), rows_spec(inner // 2), rows_spec(inner), rows_spec(inner // 2),
            rows_spec(inner // 2), rows_spec(inner), rows_spec(128),
            pl.BlockSpec((8, inner), lambda i: (0, 0)), pl.BlockSpec((128, inner), lambda i: (0, 0)),
        ],
        out_shape=[
            shape((length, width), BF16), shape((length, inner // 2), BF16), shape((length, inner // 2), BF16),
            shape((length, inner), BF16), shape((length, inner // 2), BF16), shape((length, inner // 2), BF16),
            shape((length, inner), BF16), shape((length, 128)), shape((8, inner)), shape((128, inner), BF16),
        ],
        scratch_shapes=[pltpu.VMEM((128, inner), F32)],
        compiler_params=PARAMS,
        name="gate",
        cost_estimate=cost(18),
    )(idx, y_local, gate, c_act, c_t, ed, state_in, w_out, expand, collect, gain_rows, hidden[0], grad_final)
    passed = pass_on(grad_state, kept_row, hops, -1)

    if fast:
        other = 1 - core
        normed_far, cot_far = to_core(normed), to_core(cotangent[0])
        final_far, gate_far = to_core(final_far), to_core(gate_far)
        early = grads_call(
            early_grads_kernel, idx, [normed, normed_far, final, final_far],
            [gate_near, gate_far, cotangent[0], cot_far], 512,
            [pltpu.VMEM((CHIPS * 256, 2 * length), BF16), pltpu.VMEM((256, 2 * length), BF16)], "early_grads",
        )
        grad_mixed = after(grad_mixed, early)
        passed = after(passed, early)
        early = sum_over_chips(idx, early)
    else:
        both = jnp.stack([final, final_far]).reshape(2, length, 4, inner // 8)
        order = jnp.where(core == 0, both, both[::-1])
        final = order.transpose(1, 2, 0, 3).reshape(length, inner)
        out_grad = reduce_rows(mm_rows(final, cotangent[0]))
        in_z = reduce_rows(mm_rows(normed, grad_gate))
    grad_normed_z = mm(grad_gate, w_z)
    grad_in = entering(passed)

    acc = lambda rows_, cols_: pl.BlockSpec((rows_, cols_), lambda i: (0, 0))
    halves = []
    for half in range(2):
        count = steps // 2
        first = half * count
        block = lambda rows_: pl.BlockSpec((rows_, LANES), lambda i: (0, i))
        at = lambda array, size=LANES: lanes_block(array, size, first)
        halves.append(
            pl.pallas_call(
                functools.partial(back_kernel, first=first),
                grid=(count,),
                in_specs=[
                    at(proj_x), at(grad_mixed), whole(shifts), whole(shifts_t), at(x_rows),
                    whole(gram), whole(b_act), whole(b_t), whole(c_t), whole(dt), whole(e), whole(f), whole(la),
                    at(select, sel_width), at(expand), pl.BlockSpec((LANES, 384), lambda i: (first + i, 0)),
                    whole(cat), at(state_in), at(grad_in),
                ],
                out_specs=[
                    block(length), block(2 * HALO), block(8), acc(length, 128), acc(length, 256), acc(length, 128),
                    block(8),
                ],
                out_shape=[
                    shape((length, inner // 2), BF16), shape((2 * HALO, inner // 2)), shape((8, inner // 2)),
                    shape((length, 128)), shape((length, 256)), shape((length, 128)), shape((8, inner // 2)),
                ],
                scratch_shapes=[
                    pltpu.VMEM((length, LANES), F32), pltpu.VMEM((chunks, 128, LANES), F32),
                    pltpu.VMEM((length + HALO, LANES), F32),
                ],
                compiler_params=PARAMS,
                name="scan_bwd" + str(half),
                cost_estimate=cost(22),
            )(proj_x, grad_mixed, shifts, shifts_t, x_rows, gram, b_act, b_t, c_t, dt, e, f, la, select, expand,
              collect, cat, state_in, grad_in)
        )
    grad_x, edge_x, cg_x, pair_sum, dcb, red, ends = zip(*halves)

    if fast:
        early, dt_full = lax.optimization_barrier((early, dt_full))
    ins = [shifts, shifts_t, mask, bc_rows, head_rows, b_act, c_act, *pair_sum, *dcb, *red, *ends, collect, q, dt_full]
    in_specs = [whole(a) for a in ins]
    in_specs[-3] = acc(inner, 128)
    outs = [
        shape((length, 2 * state_dim + 128), BF16), shape((2 * HALO, 2 * state_dim)), shape((8, 2 * state_dim)),
        shape((8, 128)),
    ]
    grad_bcd, edge_bc, cg_bc, head_grads = pl.pallas_call(
        post_kernel,
        grid=(1,),
        in_specs=[bc_spec, dt_spec] + in_specs,
        out_specs=[whole(o) for o in outs],
        out_shape=outs,
        scratch_shapes=[pltpu.VMEM((length + HALO, 2 * state_dim), F32)],
        compiler_params=PARAMS,
        name="post",
        cost_estimate=cost(5),
    )(proj_x, proj_x, *ins)

    edge = jnp.concatenate([*edge_x, edge_bc], axis=1)
    from_next = shift_seq(edge[:HALO], -1)
    last_rows = (edge[HALO:] + from_next).astype(BF16)

    def with_last(part, first):
        return lax.dynamic_update_slice(part, last_rows[:, first : first + part.shape[1]], (length - HALO, 0))

    grad_x = [with_last(part, i * inner // 2) for i, part in enumerate(grad_x)]
    grad_bcd = lax.dynamic_update_slice(grad_bcd, last_rows[:, inner:], (length - HALO, 0))
    grad_normed = grad_normed_z + mm(jnp.concatenate([*grad_x, grad_bcd], axis=1), w_x)
    norm_gain_part = jnp.sum(grad_normed * tokens * ratio, axis=0)
    scaled_in = grad_normed * norm_gain[None, :]
    small = [jnp.sum(gain_part, axis=0), jnp.concatenate([*cg_x, cg_bc], axis=1)[: TAPS + 1].reshape(-1)]
    small = jnp.concatenate(small + [head_grads[:3, :heads].reshape(-1)])
    if fast:
        norm_rows = width // 256
        small_rows = SMALL - norm_rows
        small = jnp.pad(small, (0, 2 * small_rows * 256 - small.shape[0])).reshape(2, small_rows, 256)
        small = lax.dynamic_index_in_dim(small + to_core(small), core, 0, False)
        small = jnp.concatenate([small, norm_gain_part.reshape(norm_rows, 256)], axis=0)
        take = lambda i: jnp.where(i == 0, grad_x[0], grad_x[1])
        early = sum_over_planes(idx, early)
        late = grads_call(
            late_grads_kernel, idx, [after(normed, early), normed_far],
            [take(core), to_core(take(other)), grad_bcd, to_core(grad_bcd), small], 256 + 2 * SMALL,
            [pltpu.VMEM((CHIPS * 256 + 384, 2 * length), BF16), pltpu.VMEM((384, 256), F32)],
            "late_grads",
        )
        late = sum_over_chips(idx, late, True)
        early = share_in_plane(after(early, late[0]))
        late = share_in_plane(sum_over_planes(idx, late, True))
        in_grad, out_grad, small = pl.pallas_call(
            finish_kernel,
            in_specs=[pl.BlockSpec(memory_space=pltpu.SMEM)] + [pl.BlockSpec(memory_space=pltpu.VMEM)] * 4,
            out_specs=[pl.BlockSpec(memory_space=pltpu.VMEM)] * 3,
            out_shape=[
                shape((in_weight.shape[1], width // PLANES)), shape((inner // PLANES, width)), shape((2 * SMALL, 256)),
            ],
            compiler_params=pltpu.CompilerParams(vmem_limit_bytes=56 * 1024 * 1024),
            name="finish",
            cost_estimate=cost(5),
        )(idx, *early, *late)
        in_grad = in_grad.T
        small = small.reshape(2, SMALL, 256)
        norm_total = jnp.sum(small[:, small_rows:], axis=0).reshape(-1)
        small = small[:, :small_rows].reshape(-1)
    else:
        in_x = reduce_rows(mm_rows(normed, jnp.concatenate([*grad_x, grad_bcd], axis=1)))
        in_grad = jnp.concatenate([in_z, in_x[:, :x_cols]], axis=1)
        small, norm_total = lax.psum((small, norm_gain_part), (SEQ, WT))
    input_grad = (
        cotangent[0].astype(F32)
        + ratio * scaled_in
        - tokens * ratio * ratio * ratio * jnp.mean(scaled_in * tokens, axis=-1, keepdims=True)
    )

    at = 0
    pieces = []
    for size in (inner, TAPS * conv_bias.shape[0], conv_bias.shape[0], heads, heads, heads):
        pieces.append(small[at : at + size])
        at += size
    gain_total, conv_w_total, conv_b_total, step_total, decay_total, skip_total = pieces

    return (
        output[None], input_grad[None], norm_total, in_grad, conv_w_total.reshape(conv_weight.shape), conv_b_total,
        step_total, decay_total, skip_total, gain_total, out_grad,
    )


def solution(mesh):
    placed = (
        P(WT, SEQ, None), P(WT, None), P(), P(WT, None), P(), P(), P(), P(), P(), P(), P(WT, None), P(WT, SEQ, None),
    )
    return jax.shard_map(
        on_device,
        mesh=mesh,
        in_specs=placed,
        out_specs=(
            P(WT, SEQ, None), P(WT, SEQ, None), P(), P(WT, None), P(), P(), P(), P(), P(), P(), P(WT, None),
        ),
        check_vma=False,
    )
```

```python
import functools

import jax
import jax.numpy as jnp
import ml_dtypes
import numpy as np
from jax import lax
from jax.experimental import pallas as pl
from jax.experimental.pallas import tpu as pltpu
from jax.sharding import PartitionSpec as P

EPS = 1e-05
LOG2E = 1.4426950408889634
CHUNK = 128
HALO = 16
LANES = 256
HEAD = 64
TAPS = 4
FULL = lax.Precision.HIGHEST
F32 = jnp.float32
BF16 = jnp.bfloat16
SEQ = "seq"
WT = "wt"


def mm(a, b):
    return jnp.dot(a, b, preferred_element_type=F32)


def mm_cols(a, b):
    return lax.dot_general(a, b, (((1,), (1,)), ((), ())), preferred_element_type=F32)


def mm_rows(a, b):
    return lax.dot_general(a, b, (((0,), (0,)), ((), ())), preferred_element_type=F32)


def sigmoid(x):
    return 0.5 * jnp.tanh(0.5 * x) + 0.5


def split2(x):
    high = x.astype(BF16)
    return high, (x - high.astype(F32)).astype(BF16)


def mm_split(x, ones):
    high, low = split2(x)
    return mm(high, ones) + mm(low, ones)


def mm3(a, b, mult=mm):
    a_high, a_low = a if isinstance(a, tuple) else split2(a)
    b_high, b_low = b if isinstance(b, tuple) else split2(b)
    return mult(a_high, b_high) + mult(a_high, b_low) + mult(a_low, b_high)


def pack3(x):
    high = x.astype(BF16).astype(F32)
    rest = x - high
    mid = rest.astype(BF16).astype(F32)
    low = rest - mid
    return (high + pltpu.roll(mid, 32, 1) + pltpu.roll(low, 64, 1)).astype(BF16)


def softplus(x):
    small = jnp.exp(-jnp.abs(x))
    series = small * (1.0 - small * (0.5 - small * (1.0 / 3.0 - small * (0.25 - small * 0.2))))
    return jnp.maximum(x, 0.0) + jnp.where(small < 0.02, series, jnp.log(1.0 + small))


def conv_inputs(window, shifts):
    moved = mm(shifts, window)
    return [window[HALO:].astype(F32)] + [
        moved[j * CHUNK : (j + 1) * CHUNK] for j in range(TAPS - 1)
    ]


def conv_sum(taps, cw):
    total = cw[TAPS : TAPS + 1]
    for j in range(TAPS):
        total = total + cw[j : j + 1] * taps[j]
    return total


def pair_cols(x):
    return x[:, :128], x[:, 128:]


def pair_rows(x):
    return x[:128], x[128:]


def rows_of(c):
    return slice(c * CHUNK, (c + 1) * CHUNK)


def window_of(c):
    return slice(c * CHUNK, (c + 1) * CHUNK + HALO)


def prep_kernel(
    bc_ref, dtr_ref, sh_ref, mask_ref, cols_ref, cw_ref, hp_ref,
    b_ref, c_ref, bt_ref, ct_ref, gm_ref, dtf_ref, dt_ref, e_ref, f_ref, ed_ref, la_ref, cat_ref, kept_ref,
):
    row = lax.broadcasted_iota(jnp.int32, (CHUNK, CHUNK), 0)
    col = lax.broadcasted_iota(jnp.int32, (CHUNK, CHUNK), 1)
    lower = jnp.where(col <= row, 1.0, 0.0).astype(F32)
    used = col < 32
    heads = cat_ref.shape[1]
    before = jnp.zeros((1, CHUNK), F32)
    cw = cw_ref[...]
    for c in range(sh_ref.shape[0]):
        rows = rows_of(c)
        taps = conv_inputs(bc_ref[window_of(c)], sh_ref[c])
        k = conv_sum(taps, cw)
        act = k * sigmoid(k)
        b_act, c_act = act[:, :128], act[:, 128:]
        b_high, b_low = split2(b_act)
        c_high, c_low = split2(c_act)
        gram = mm_cols(c_high, b_high) + mm_cols(c_high, b_low) + mm_cols(c_low, b_high)
        gm_ref[rows] = gram * mask_ref[rows]
        b_ref[rows] = jnp.concatenate([b_high, b_low], axis=1)
        c_ref[rows] = jnp.concatenate([c_high, c_low], axis=1)
        bt_ref[:, rows] = jnp.concatenate(split2(b_act.T), axis=0)
        ct_ref[:, rows] = jnp.concatenate(split2(c_act.T), axis=0)
        step_in = dtr_ref[c * CHUNK + HALO : (c + 1) * CHUNK + HALO].astype(F32) + hp_ref[0:1]
        dt = jnp.where(used, softplus(step_in), 0.0)
        cumul = jnp.dot(lower, dt * hp_ref[1:2], precision=FULL, preferred_element_type=F32)
        last = cumul[CHUNK - 1 : CHUNK]
        cols = cols_ref[rows]
        e = jnp.where(used, jnp.exp2(cumul) * cols[:, 0:1], 0.0)
        f = jnp.where(used, jnp.exp2(last - cumul) * cols[:, 1:2], 0.0)
        ed = jnp.where(used, jnp.exp2(before + cumul) * cols[:, 2:3], 0.0)
        before = before + last
        dtf_ref[rows] = dt
        dt_ref[rows] = pack3(dt)
        e_ref[rows] = pack3(e)
        f_ref[rows] = pack3(f)
        ed_ref[rows] = pack3(ed)
        la_ref[rows] = pack3(cumul)
        cat_ref[c] = cumul.T[:heads]
        kept_ref[...] = jnp.broadcast_to(ed[CHUNK - 1 : CHUNK], kept_ref.shape)


def weights_of(c, step, la_ref, sel, cat_ref):
    spread = mm(la_ref[rows_of(c)], sel)
    per_step = LANES // HEAD
    out = []
    for i in range(per_step):
        ahead = cat_ref[c, pl.ds(step * per_step + i, 1), :]
        out.append(jnp.exp2(jnp.minimum(spread[:, i * CHUNK : (i + 1) * CHUNK] - ahead, 0.0)))
    return out


def head_pairs(x):
    first = lax.broadcasted_iota(jnp.int32, x.shape, 1) < HEAD
    zero = jnp.zeros_like(x)
    return jnp.concatenate([jnp.where(first, x, zero), jnp.where(first, zero, x)], axis=0)


def fwd_kernel(
    x_ref, sh_ref, cw_ref, gm_ref, c_ref, bt_ref, dt_ref, e_ref, f_ref, la_ref, sel_ref, exp_ref, cat_ref,
    y_ref, s_ref, states_ref,
):
    step = pl.program_id(0)
    cw, sel, expand = cw_ref[...], sel_ref[...], exp_ref[...]
    state = jnp.zeros((128, LANES), F32)
    for c in range(sh_ref.shape[0]):
        rows = rows_of(c)
        k = conv_sum(conv_inputs(x_ref[window_of(c)], sh_ref[c]), cw)
        xa = k * sigmoid(k)
        v = mm(dt_ref[rows], expand) * xa
        ex = mm(e_ref[rows], expand)
        fx = mm(f_ref[rows], expand)
        v_parts = split2(v)
        gm = gm_ref[rows]
        weights = [w * gm for w in weights_of(c, step, la_ref, sel, cat_ref)]
        local = []
        for p in range(LANES // 128):
            own = tuple(head_pairs(part[:, p * 128 : (p + 1) * 128]) for part in v_parts)
            local.append(mm3(jnp.concatenate(weights[2 * p : 2 * p + 2], axis=1), own))
        y = jnp.concatenate(local, axis=1) + ex * mm3(pair_cols(c_ref[rows]), state)
        y_ref[rows] = y + cw[5:6] * xa
        state = ex[CHUNK - 1 : CHUNK] * state + mm3(pair_rows(bt_ref[:, rows]), fx * v)
        states_ref[c] = state
    s_ref[...] = state.astype(BF16)


def gate_kernel(
    idx_ref, y_ref, z_ref, c_ref, ct_ref, ed_ref, sin_ref, wo_ref, exp_ref, expt_ref, gain_ref, hid_ref, df_ref,
    out_ref, fin_ref, fin_far_ref, dz_ref, dz_near_ref, dz_far_ref, dy_ref, q_ref, og_ref, gs_ref, acc_ref,
):
    i = pl.program_id(0)

    @pl.when(i == 0)
    def _():
        og_ref[...] = jnp.zeros_like(og_ref)
        acc_ref[...] = jnp.zeros_like(acc_ref)

    gain = gain_ref[0:1]
    inner = y_ref.shape[1]
    edx = mm(ed_ref[...], exp_ref[...])
    y_full = y_ref[...] + edx * (mm(c_ref[:, :128], sin_ref[...]) + mm(c_ref[:, 128:], sin_ref[...]))
    y = y_full.astype(BF16).astype(F32)
    z = z_ref[...].astype(F32)
    sig = sigmoid(z)
    sz = z * sig
    gated = y * sz
    gnorm = lax.rsqrt(jnp.sum(gated * gated, axis=1, keepdims=True) * (1.0 / inner) + EPS)
    normal = gated * gnorm
    final = (normal * gain).astype(BF16)
    first_core = idx_ref[2] == 0
    block = inner // 8
    for part in range(4):
        a = final[:, 2 * part * block : (2 * part + 1) * block]
        b = final[:, (2 * part + 1) * block : (2 * part + 2) * block]
        fin_ref[:, part * block : (part + 1) * block] = jnp.where(first_core, a, b)
        fin_far_ref[:, part * block : (part + 1) * block] = jnp.where(first_core, b, a)
    out_ref[...] = (hid_ref[...].astype(F32) + mm(final, wo_ref[...])).astype(BF16)
    dfinal = df_ref[...]
    share = dfinal * normal
    og_ref[...] += jnp.sum(share.reshape(-1, 8, inner), axis=0)
    e = dfinal * gain
    mean = jnp.sum(share * gain, axis=1, keepdims=True) * (1.0 / inner)
    dgated = gnorm * (e - normal * mean)
    dz = (dgated * y * (sig * (1.0 + z * (1.0 - sig)))).astype(BF16)
    dz_ref[...] = dz
    dz_near_ref[...] = jnp.where(first_core, dz[:, : inner // 2], dz[:, inner // 2 :])
    dz_far_ref[...] = jnp.where(first_core, dz[:, inner // 2 :], dz[:, : inner // 2])
    dyb = (dgated * sz).astype(BF16)
    dy_ref[...] = dyb
    dy = dyb.astype(F32)
    q_ref[...] = mm_split(dy * y_full, expt_ref[...])
    acc_ref[...] += mm3(pair_rows(ct_ref[...]), edx * dy)

    @pl.when(i == pl.num_programs(0) - 1)
    def _():
        gs_ref[...] = acc_ref[...].astype(BF16)


def back_kernel(
    x_ref, dy_ref, sh_ref, sht_ref, cw_ref, gm_ref, b_ref, ct_ref, dt_ref, e_ref, f_ref, la_ref,
    sel_ref, exp_ref, expt_ref, cat_ref, states_ref, sin_ref, din_ref,
    dx_ref, edge_ref, cg_ref, m_ref, dcb_ref, red_ref, sd_ref,
    dxw_ref,
    *, first,
):
    step = pl.program_id(0) + first

    @pl.when(pl.program_id(0) == 0)
    def _():
        m_ref[...] = jnp.zeros_like(m_ref)
        dcb_ref[...] = jnp.zeros_like(dcb_ref)
        red_ref[...] = jnp.zeros_like(red_ref)

    count = sh_ref.shape[0]
    cw, sel, expand = cw_ref[...], sel_ref[...], exp_ref[...]
    first_state = sin_ref[...].astype(F32)
    fades = [jnp.ones((1, LANES), F32)]
    for c in range(count):
        end = mm(e_ref[(c + 1) * CHUNK - 16 : (c + 1) * CHUNK], expand)
        fades.append(fades[-1] * end[15:])
    grad = din_ref[...].astype(F32)
    cg = [jnp.zeros((8, LANES), F32) for _ in range(TAPS + 1)]
    sd_ref[...] = jnp.zeros_like(sd_ref)
    after = states_ref[count - 1] + fades[count] * first_state
    for c in reversed(range(count)):
        rows = rows_of(c)
        gradb = grad.astype(BF16)
        sd_ref[c : c + 1] = jnp.sum(after * grad, axis=0, keepdims=True)
        after = fades[c] * first_state
        if c > 0:
            after += states_ref[c - 1]
        taps = conv_inputs(x_ref[window_of(c)], sh_ref[c])
        k = conv_sum(taps, cw)
        sig = sigmoid(k)
        xa = k * sig
        dtx = mm(dt_ref[rows], expand)
        ex = mm(e_ref[rows], expand)
        fx = mm(f_ref[rows], expand)
        v = dtx * xa
        vb = v.astype(BF16)
        dyb = dy_ref[rows]
        dy = dyb.astype(F32)
        gm = gm_ref[rows]
        weights = weights_of(c, step, la_ref, sel, cat_ref)
        dv = []
        total = None
        for p in range(LANES // 128):
            lanes = slice(p * 128, (p + 1) * 128)
            pair = weights[2 * p : 2 * p + 2]
            products = mm_cols(dyb[:, lanes], head_pairs(vb[:, lanes]))
            part = products[:, :CHUNK] * pair[0] + products[:, CHUNK:] * pair[1]
            total = part if total is None else total + part
            stacked = jnp.concatenate([w * gm for w in pair], axis=0)
            own = head_pairs(dyb[:, lanes])
            high, low = split2(stacked)
            dv.append(mm_rows(high, own) + mm_rows(low, own))
        m_ref[rows] += total
        dv = jnp.concatenate(dv, axis=1) + fx * mm3(pair_cols(b_ref[rows]), grad)
        edy = ex * dy
        edyb = edy.astype(BF16)
        dcb_ref[rows, 0:128] += mm_cols((fx * v).astype(BF16), gradb)
        dcb_ref[rows, 128:256] += mm_cols(edyb, after.astype(BF16))
        grad = ex[CHUNK - 1 : CHUNK] * grad + mm3(pair_rows(ct_ref[:, rows]), edy)
        red = mm_split(xa * dv, expt_ref[:, 0:128])
        red += mm_split(dy * xa, expt_ref[:, 128:256])
        red_ref[rows] += red
        dxa = dtx * dv + cw[5:6] * dy
        dk = dxa * (sig * (1.0 + k * (1.0 - sig)))
        cg[TAPS] += jnp.sum(dk.reshape(-1, 8, LANES), axis=0)
        for j in range(TAPS):
            cg[j] += jnp.sum((dk * taps[j]).reshape(-1, 8, LANES), axis=0)
        shifted = jnp.concatenate([(cw[j : j + 1] * dk).astype(BF16) for j in range(1, TAPS)], axis=0)
        moved = mm(sht_ref[c], shifted)
        low, high = c * CHUNK, (c + 1) * CHUNK
        own = cw[0:1] * dk
        dxw_ref[low : low + HALO] = moved[:HALO]
        dxw_ref[low + HALO : high] = moved[HALO:CHUNK] + own[: CHUNK - HALO]
        end = moved[CHUNK:] + own[CHUNK - HALO :]
        if c == count - 1:
            dxw_ref[high : high + HALO] = end
        else:
            dxw_ref[high : high + HALO] += end
    cg_ref[...] = jnp.zeros_like(cg_ref)
    for j in range(TAPS + 1):
        cg_ref[j : j + 1] = jnp.sum(cg[j], axis=0, keepdims=True)
    dx_ref[...] = dxw_ref[HALO:].astype(BF16)
    edge_ref[:HALO] = dxw_ref[:HALO]
    edge_ref[HALO:] = dxw_ref[count * CHUNK :]


def post_kernel(
    bc_ref, dtr_ref, sh_ref, sht_ref, mask_ref, cw_ref, hp_ref, b_ref, c_ref, m0_ref, m1_ref, dcb0_ref, dcb1_ref,
    red0_ref, red1_ref, sd0_ref, sd1_ref, expt_ref, q_ref, dtf_ref,
    dbcd_ref, edge_ref, cg_ref, hg_ref,
    dxw_ref,
):
    count = sh_ref.shape[0]
    cw = cw_ref[...]
    width = bc_ref.shape[1]
    row = lax.broadcasted_iota(jnp.int32, (CHUNK, CHUNK), 0)
    col = lax.broadcasted_iota(jnp.int32, (CHUNK, CHUNK), 1)
    upper = jnp.where(col >= row, 1.0, 0.0).astype(F32)
    used = col < 32
    cg = [jnp.zeros((8, width), F32) for _ in range(TAPS + 1)]
    step_grad = jnp.zeros((8, CHUNK), F32)
    decay_grad = jnp.zeros((8, CHUNK), F32)
    skip_grad = jnp.zeros((8, CHUNK), F32)
    half = sd0_ref.shape[1]
    ends = mm_split(sd0_ref[...], expt_ref[:half]) + mm_split(sd1_ref[...], expt_ref[half:])
    rate = hp_ref[2:3]
    for c in reversed(range(count)):
        rows = rows_of(c)
        taps = conv_inputs(bc_ref[window_of(c)], sh_ref[c])
        k = conv_sum(taps, cw)
        sig = sigmoid(k)
        both = ((m0_ref[rows] + m1_ref[rows]) * mask_ref[rows]).astype(BF16)
        dcb = dcb0_ref[rows] + dcb1_ref[rows]
        db = mm_rows(both, c_ref[rows, :128]) + dcb[:, :128]
        dc = mm(both, b_ref[rows, :128]) + dcb[:, 128:]
        dk = jnp.concatenate([db, dc], axis=1) * (sig * (1.0 + k * (1.0 - sig)))
        cg[TAPS] += jnp.sum(dk.reshape(-1, 8, width), axis=0)
        for j in range(TAPS):
            cg[j] += jnp.sum((dk * taps[j]).reshape(-1, 8, width), axis=0)
        shifted = jnp.concatenate([(cw[j : j + 1] * dk).astype(BF16) for j in range(1, TAPS)], axis=0)
        moved = mm(sht_ref[c], shifted)
        low, high = c * CHUNK, (c + 1) * CHUNK
        own = cw[0:1] * dk
        dxw_ref[low : low + HALO] = moved[:HALO]
        dxw_ref[low + HALO : high] = moved[HALO:CHUNK] + own[: CHUNK - HALO]
        end = moved[CHUNK:] + own[CHUNK - HALO :]
        if c == count - 1:
            dxw_ref[high : high + HALO] = end
        else:
            dxw_ref[high : high + HALO] += end
        red = red0_ref[rows] + red1_ref[rows]
        xdv = red
        dt = dtf_ref[rows]
        vdv = dt * xdv
        dyx = pltpu.roll(red, 96, 1)
        change = q_ref[rows] - hp_ref[3:4] * dyx - vdv
        change = jnp.where(used, change, 0.0)
        da = jnp.dot(upper, change, precision=FULL, preferred_element_type=F32) + ends[c : c + 1]
        step_in = dtr_ref[c * CHUNK + HALO : (c + 1) * CHUNK + HALO].astype(F32) + hp_ref[0:1]
        ddt = jnp.where(used, (xdv + rate * da) * sigmoid(step_in), 0.0)
        dbcd_ref[rows, width:] = ddt.astype(BF16)
        step_grad += jnp.sum(ddt.reshape(-1, 8, CHUNK), axis=0)
        decay_grad += jnp.sum((dt * da).reshape(-1, 8, CHUNK), axis=0)
        skip_grad += jnp.sum(dyx.reshape(-1, 8, CHUNK), axis=0)
    cg_ref[...] = jnp.zeros_like(cg_ref)
    for j in range(TAPS + 1):
        cg_ref[j : j + 1] = jnp.sum(cg[j], axis=0, keepdims=True)
    dbcd_ref[:, :width] = dxw_ref[HALO:].astype(BF16)
    edge_ref[:HALO] = dxw_ref[:HALO]
    edge_ref[HALO:] = dxw_ref[count * CHUNK :]
    hg_ref[...] = jnp.zeros_like(hg_ref)
    hg_ref[0:1] = jnp.sum(step_grad, axis=0, keepdims=True)
    hg_ref[1:2] = rate * jnp.sum(decay_grad, axis=0, keepdims=True)
    hg_ref[2:3] = jnp.sum(skip_grad, axis=0, keepdims=True)


def norm_back_kernel(
    dz_ref, dx0_ref, dx1_ref, db_ref, wz_ref, wx_ref, hid_ref, cot_ref, gain_ref, out_ref, ng_ref
):
    @pl.when(pl.program_id(0) == 0)
    def _():
        ng_ref[...] = jnp.zeros_like(ng_ref)

    half = dx0_ref.shape[1]
    width = out_ref.shape[1]
    dn = mm(dz_ref[...], wz_ref[...]) + mm(dx0_ref[...], wx_ref[:half])
    dn = dn + mm(dx1_ref[...], wx_ref[half : 2 * half]) + mm(db_ref[...], wx_ref[2 * half :])
    x = hid_ref[...].astype(F32)
    ratio = lax.rsqrt(jnp.sum(x * x, axis=1, keepdims=True) * (1.0 / width) + EPS)
    ng_ref[...] += jnp.sum((dn * (x * ratio)).reshape(-1, 8, width), axis=0)
    e = dn * gain_ref[0:1]
    mean = jnp.sum(e * x, axis=1, keepdims=True) * (1.0 / width)
    out_ref[...] = cot_ref[...].astype(F32) + ratio * e - x * (ratio * ratio * ratio * mean)


def whole(array):
    return pl.BlockSpec(array.shape, lambda *_: (0,) * array.ndim)


def lanes_block(array, width=LANES, first=0):
    return pl.BlockSpec((array.shape[0], width), lambda i: (0, first + i))


def shape(dims, dtype=F32):
    return jax.ShapeDtypeStruct(dims, dtype)


PARAMS = pltpu.CompilerParams(vmem_limit_bytes=56 * 1024 * 1024, dimension_semantics=("arbitrary",))


def cost(micros):
    return pl.CostEstimate(flops=int(micros * 1.1e9), transcendentals=0, bytes_accessed=0)


def gather_rows(part):
    count = lax.axis_size(SEQ)
    share = part.shape[0] // count
    mine = lax.dynamic_slice_in_dim(part, lax.axis_index(SEQ) * share, share, 0)
    return lax.all_gather(mine, (WT, SEQ), axis=0, tiled=True)


def reduce_rows(part):
    count = lax.axis_size(SEQ)
    part = part.reshape(lax.axis_size(WT), count, -1, part.shape[1]).transpose(1, 0, 2, 3).reshape(part.shape)
    mine = lax.psum_scatter(part, SEQ, scatter_dimension=0, tiled=True)
    mine = lax.psum_scatter(mine, WT, scatter_dimension=0, tiled=True)
    return lax.all_gather(mine, SEQ, axis=0, tiled=True)


PLANES = 4
CHIPS = 4


def to_chip(x, k):
    return lax.ppermute(x, SEQ, [(i, i ^ (2 * k)) for i in range(2 * CHIPS)])


def to_core(x):
    return lax.ppermute(x, SEQ, [(i, i ^ 1) for i in range(2 * CHIPS)])


def to_plane(x, k):
    return lax.ppermute(x, WT, [(i, (i + k) % PLANES) for i in range(PLANES)])


def copies_into(idx_ref, own, parts, sem):
    z, q, c = idx_ref[0], idx_ref[1], idx_ref[2]
    pairs = own(z)
    for a_ref, b_ref, near, place in parts:
        for j, away in enumerate((0, near, CHIPS - 1 - near, CHIPS - 1)):
            for k in range(1, PLANES):
                plane = lax.rem(z + PLANES - k, PLANES)
                chip = lax.bitwise_xor(q, away)
                at = j * (PLANES - 1) + k - 1
                pairs.append(place(a_ref.at[at], plane, 2 * chip + c))
                pairs.append(place(b_ref.at[at], plane, 2 * chip + 1 - c))
    return [pltpu.make_async_copy(source, target, sem) for source, target in pairs]


def rows_from(start, size):
    return pl.ds(pl.multiple_of(start, 16), size)


def run(copies):
    for copy in copies:
        copy.start()
    for copy in copies:
        copy.wait()


def lanes_at(index, width=256):
    return pl.ds(pl.multiple_of(index * width, width), width)


def proj_x_kernel(
    idx_ref, own_ref, a0_ref, b0_ref, a1_ref, b1_ref, x_ref, out_ref, w_out_ref, w_ref, sem, sem_out
):
    first = a0_ref.shape[1]
    second = a1_ref.shape[1]

    def place_first(source, plane, part):
        return source, w_ref.at[rows_from(part * (first + second), first), lanes_at(plane)]

    def place_second(source, plane, part):
        return source, w_ref.at[rows_from(part * (first + second) + first, second), lanes_at(plane)]

    def own(plane):
        return [(own_ref, w_ref.at[:, lanes_at(plane)])]

    parts = [(a0_ref, b0_ref, 1, place_first), (a1_ref, b1_ref, 2, place_second)]
    run(copies_into(idx_ref, own, parts, sem))
    keep = pltpu.make_async_copy(w_ref, w_out_ref, sem_out)
    keep.start()
    rows = w_ref.shape[0]
    for first in range(0, rows, 512):
        last = min(first + 512, rows)
        out_ref[:, first:last] = mm_cols(x_ref[...], w_ref[first:last]).astype(BF16)
    keep.wait()


def proj_z_kernel(
    idx_ref, oz_ref, oo_ref, a0_ref, b0_ref, a1_ref, b1_ref, x_ref, cot_ref,
    out_ref, df_ref, wz_out_ref, wo_out_ref, wz_ref, wo_ref, sem, sem_out,
):
    share_z = a1_ref.shape[1]
    rows = wo_ref.shape[0] // PLANES

    def place_out(half):
        def place(source, plane, part):
            to = wo_ref.at[rows_from((2 * plane + half) * (rows // 2), rows // 2), lanes_at(part, 128)]
            return source.at[:, half * 128 : (half + 1) * 128], to

        return place

    def place_z(source, plane, part):
        return source, wz_ref.at[rows_from(part * share_z, share_z), lanes_at(plane)]

    def own(plane):
        return [(oz_ref, wz_ref.at[:, lanes_at(plane)]), (oo_ref, wo_ref.at[lanes_at(plane, rows)])]

    parts = [(a0_ref, b0_ref, 1, place_out(half)) for half in range(2)]
    run(copies_into(idx_ref, own, parts + [(a1_ref, b1_ref, 2, place_z)], sem))
    keep = [
        pltpu.make_async_copy(wz_ref, wz_out_ref, sem_out),
        pltpu.make_async_copy(wo_ref, wo_out_ref, sem_out),
    ]
    for copy in keep:
        copy.start()
    for first in range(0, wz_ref.shape[0], 512):
        cols = slice(first, first + 512)
        out_ref[:, cols] = mm_cols(x_ref[...], wz_ref[cols]).astype(BF16)
        df_ref[:, cols] = mm_cols(cot_ref[...], wo_ref[cols])
    for copy in keep:
        copy.wait()


def project(kernel, idx, gathered, ins, outs, kept, name):
    hbm = pl.BlockSpec(memory_space=pl.ANY)
    vmem = pl.BlockSpec(memory_space=pltpu.VMEM)
    return pl.pallas_call(
        kernel,
        in_specs=[pl.BlockSpec(memory_space=pltpu.SMEM)] + [hbm] * len(gathered) + [vmem] * len(ins),
        out_specs=[vmem] * len(outs) + [hbm] * len(kept),
        out_shape=outs + [shape(d, BF16) for d in kept],
        scratch_shapes=[pltpu.VMEM(d, BF16) for d in kept] + [pltpu.SemaphoreType.DMA, pltpu.SemaphoreType.DMA],
        compiler_params=pltpu.CompilerParams(vmem_limit_bytes=56 * 1024 * 1024),
        name=name,
        cost_estimate=cost(10),
    )(idx, *gathered, *ins)


def gather_far(mine):
    return jnp.stack([to_plane(mine, k) for k in range(1, PLANES)])


def gather_first(far, near):
    return jnp.concatenate([far, to_chip(far, near)], axis=0)


def gather_second(two, near):
    return jnp.concatenate([two, to_chip(two, CHIPS - 1 - near)], axis=0)


def keep_transposed(ref, near_ref, far_ref, cols):
    length = near_ref.shape[0]
    ref[:, :length] = near_ref[:, cols].T
    ref[:, length:] = far_ref[:, cols].T


def early_grads_kernel(idx_ref, n0_ref, n1_ref, f0_ref, f1_ref, dz0_ref, dz1_ref, g0_ref, g1_ref, *refs):
    outs, (dzt_ref, ft_ref) = refs[:CHIPS], refs[CHIPS:]
    block = 256
    length = n0_ref.shape[0]

    @pl.when(pl.program_id(0) == 0)
    def _():
        for k in range(CHIPS):
            rows = dzt_ref.at[k * block : (k + 1) * block]
            keep_transposed(rows, dz0_ref, dz1_ref, lanes_at(lax.bitwise_xor(idx_ref[1], k)))

    keep_transposed(ft_ref, f0_ref, f1_ref, slice(None))
    second = mm(dzt_ref[:, :length], n0_ref[...]) + mm(dzt_ref[:, length:], n1_ref[...])
    for k, out in enumerate(outs):
        lanes = lanes_at(lax.bitwise_xor(idx_ref[1], k))
        first = mm(ft_ref[:, :length], g0_ref[:, lanes]) + mm(ft_ref[:, length:], g1_ref[:, lanes])
        out[0, :block] = first.astype(out.dtype)
        out[0, block:] = second[k * block : (k + 1) * block].astype(out.dtype)


def late_grads_kernel(idx_ref, n0_ref, n1_ref, dx0_ref, dx1_ref, *refs, with_others):
    if with_others:
        db0_ref, db1_ref, small_ref, *outs, dxt_ref, rest_ref = refs
    else:
        *outs, dxt_ref = refs
    block, share = 128, 64
    length = n0_ref.shape[0]
    q, c = idx_ref[1], idx_ref[2]

    @pl.when(pl.program_id(0) == 0)
    def _():
        for k in range(CHIPS):
            rows = dxt_ref.at[k * block : (k + 1) * block]
            keep_transposed(rows, dx0_ref, dx1_ref, lanes_at(lax.bitwise_xor(q, k), block))
        if with_others:
            keep_transposed(dxt_ref.at[CHIPS * block :], db0_ref, db1_ref, slice(None))

    total = mm(dxt_ref[:, :length], n0_ref[...]) + mm(dxt_ref[:, length:], n1_ref[...])
    if with_others:
        rest_ref[: total.shape[0] - CHIPS * block] = total[CHIPS * block :]
        for part in range(2 * CHIPS - 2, 2 * CHIPS):
            for i, x in enumerate(split2(small_ref[...])):
                rest_ref[part * share + i * SMALL : part * share + (i + 1) * SMALL] = x.astype(F32)
    for k, out in enumerate(outs):
        chip = lax.bitwise_xor(q, k)
        out[0, :block] = total[k * block : (k + 1) * block].astype(out.dtype)
        if with_others:
            out[0, block:] = rest_ref[pl.ds(pl.multiple_of((2 * chip + c) * share, share), share)].astype(out.dtype)


def plane_blocks(rows, cols):
    return pl.BlockSpec((rows, cols), lambda i, idx: (0, lax.rem(idx[0] + i, PLANES)))


def grads_call(kernel, idx, blocked, full, rows, scratch, name):
    length = blocked[0].shape[0]
    out = lambda dtype: shape((PLANES, rows, 256), dtype)
    return pl.pallas_call(
        kernel,
        grid_spec=pltpu.PrefetchScalarGridSpec(
            num_scalar_prefetch=1,
            grid=(PLANES,),
            in_specs=[plane_blocks(length, a.shape[1] // PLANES) for a in blocked]
            + [pl.BlockSpec(a.shape, lambda i, idx, n=a.ndim: (0,) * n) for a in full],
            out_specs=[pl.BlockSpec((1, rows, 256), lambda i, idx: (i, 0, 0)) for _ in range(CHIPS)],
            scratch_shapes=scratch,
        ),
        out_shape=[out(F32)] + [out(BF16)] * (CHIPS - 1),
        compiler_params=PARAMS,
        name=name,
        cost_estimate=cost(9),
    )(idx, *blocked, *full)


SMALL = 32


def put_small(ref, total, first, active):
    @pl.when(active)
    def _():
        high, low = split2(total)
        ref[first : first + SMALL] = high.astype(ref.dtype)
        ref[first + SMALL : first + 2 * SMALL] = low.astype(ref.dtype)


def chip_sum_kernel(idx_ref, *refs, small):
    parts, outs = refs[:-PLANES], refs[-PLANES:]
    for k, out in enumerate(outs):
        at = 0
        for i in range(0, len(parts), CHIPS):
            total = parts[i][k]
            for ref in parts[i + 1 : i + CHIPS]:
                total = total + ref[k].astype(F32)
            out[at : at + total.shape[0]] = total.astype(out.dtype)
            at += total.shape[0]
        if small:
            first = total.shape[0] - 2 * SMALL
            total = total[first : first + SMALL] + total[first + SMALL :]
            put_small(out, total, at - 2 * SMALL, idx_ref[1] == CHIPS - 1)


def plane_sum_kernel(idx_ref, *refs, small):
    parts, out = refs[:-1], refs[-1]
    at = 0
    for i in range(0, len(parts), PLANES):
        total = parts[i][...]
        for ref in parts[i + 1 : i + PLANES]:
            total = total + ref[...].astype(F32)
        rows = total.shape[0]
        out[at : at + rows] = total.astype(out.dtype)
        at += rows
    if small:
        total = total[rows - 2 * SMALL : rows - SMALL] + total[rows - SMALL :]
        put_small(out, total, at - 2 * SMALL, idx_ref[1] == CHIPS - 1)


def sum_call(kernel, idx, ins, outs, name):
    vmem = pl.BlockSpec(memory_space=pltpu.VMEM)
    return pl.pallas_call(
        kernel,
        in_specs=[pl.BlockSpec(memory_space=pltpu.SMEM)] + [vmem] * len(ins),
        out_specs=[vmem] * len(outs),
        out_shape=outs,
        compiler_params=pltpu.CompilerParams(vmem_limit_bytes=56 * 1024 * 1024),
        cost_estimate=cost(2),
        name=name,
    )(idx, *ins)


def to_chips(parts):
    return [parts[0]] + [to_chip(parts[k], k) for k in range(1, CHIPS)]


def sum_over_chips(idx, parts, small=False):
    rows = sum(part.shape[1] for part in parts[::CHIPS])
    outs = [shape((rows, 256), dtype) for dtype in [F32] + [BF16] * (PLANES - 1)]
    return sum_call(functools.partial(chip_sum_kernel, small=small), idx, parts, outs, "chip_sum")


def to_planes(parts):
    return [parts[0]] + [to_plane(parts[k], k) for k in range(1, PLANES)]


def sum_over_planes(idx, parts, small=False):
    rows = sum(part.shape[0] for part in parts[::PLANES])
    kernel = functools.partial(plane_sum_kernel, small=small)
    return sum_call(kernel, idx, parts, [shape((rows, 256), BF16)], "plane_sum")[0]


def share_in_plane(block):
    return jnp.stack([block] + [to_chip(block, k) for k in range(1, CHIPS)])


def both_cores(plane):
    return plane, to_core(plane)


def finish_early_kernel(idx_ref, a_ref, b_ref, in_ref, out_ref, rows_ref, sem):
    q, c = idx_ref[1], idx_ref[2]
    block = 256
    for j in range(CHIPS):
        chip = lax.bitwise_xor(q, j)
        for core, ref in ((c, a_ref), (1 - c, b_ref)):
            rows_ref[lanes_at(core * CHIPS + chip)] = ref[j, block:].astype(F32)
            out_ref[lanes_at(core), lanes_at(chip)] = ref[j, :block].astype(F32)
    copy = pltpu.make_async_copy(rows_ref, in_ref.at[: rows_ref.shape[0]], sem)
    copy.start()
    copy.wait()


def finish_late_kernel(idx_ref, a_ref, b_ref, _, in_ref, small_ref, rows_ref, sem):
    q, c = idx_ref[1], idx_ref[2]
    block, share = 128, 64
    inner = 4 * CHIPS * block
    rest = rows_ref.shape[0] - inner
    for j in range(CHIPS):
        chip = lax.bitwise_xor(q, j)
        for core, ref in ((c, a_ref), (1 - c, b_ref)):
            for half in range(2):
                row = ((2 * half + core) * CHIPS + chip) * block
                rows_ref[pl.ds(pl.multiple_of(row, block), block)] = ref[j, half * block : (half + 1) * block].astype(F32)
            part = 2 * chip + core

            @pl.when(part < rest // share)
            def _(ref=ref, part=part, j=j):
                rows_ref[pl.ds(pl.multiple_of(inner + part * share, share), share)] = ref[j, 2 * block :].astype(F32)

            @pl.when(part == rest // share)
            def _(ref=ref, j=j):
                rows_ref[inner + rest // share * share :] = ref[j, 2 * block : 2 * block + rest % share].astype(F32)

            @pl.when(chip == CHIPS - 1)
            def _(ref=ref, core=core, j=j):
                first = 2 * block
                total = ref[j, first : first + SMALL].astype(F32) + ref[j, first + SMALL :].astype(F32)
                small_ref[lanes_at(core, SMALL)] = total

    copy = pltpu.make_async_copy(rows_ref, in_ref.at[in_ref.shape[0] - rows_ref.shape[0] :], sem)
    copy.start()
    copy.wait()


ANY, VMEM, SMEM = (pl.BlockSpec(memory_space=m) for m in (pl.ANY, pltpu.VMEM, pltpu.SMEM))


def finish_early(idx, early, in_dims, out_dims):
    return pl.pallas_call(
        finish_early_kernel,
        in_specs=[SMEM, VMEM, VMEM],
        out_specs=[ANY, VMEM],
        out_shape=[shape(in_dims), shape(out_dims)],
        scratch_shapes=[pltpu.VMEM((8 * 256, in_dims[1]), F32), pltpu.SemaphoreType.DMA],
        compiler_params=pltpu.CompilerParams(vmem_limit_bytes=56 * 1024 * 1024),
        cost_estimate=cost(4),
        name="finish_early",
    )(idx, *early)


def finish_late(idx, late, grad):
    return pl.pallas_call(
        finish_late_kernel,
        in_specs=[SMEM, VMEM, VMEM, ANY],
        out_specs=[ANY, VMEM],
        out_shape=[shape(grad.shape), shape((2 * SMALL, 256))],
        scratch_shapes=[pltpu.VMEM((grad.shape[0] - 8 * 256, grad.shape[1]), F32), pltpu.SemaphoreType.DMA],
        input_output_aliases={3: 0},
        compiler_params=pltpu.CompilerParams(vmem_limit_bytes=56 * 1024 * 1024),
        cost_estimate=cost(4),
        name="finish_late",
    )(idx, *late, grad)


def shift_seq(x, by):
    count = lax.axis_size(SEQ)
    pairs = [(i, i + by) for i in range(count) if 0 <= i + by < count]
    return lax.ppermute(x, SEQ, pairs)


def pass_on(part, kept, hops, sign):
    return [
        (shift_seq(part, sign * hop), shift_seq(kept, sign * hop) if hop < hops else None) for hop in range(1, hops + 1)
    ]


def entering(passed):
    total, fade = None, None
    for moved, kept in passed:
        moved = moved.astype(F32)
        if fade is not None:
            moved = moved * fade
        total = moved if total is None else total + moved
        if kept is not None:
            factor = jnp.repeat(kept, HEAD)[None, :]
            fade = factor if fade is None else fade * factor
    return total.astype(BF16)


def after(x, *others):
    return lax.optimization_barrier((x, others))[0]


def on_device(
    hidden, doc_ids, norm_gain, in_weight, conv_weight, conv_bias, step_bias, decay_log, skip_gain, out_gain,
    out_weight, cotangent,
):
    seq_count = lax.axis_size(SEQ)
    seq_index = lax.axis_index(SEQ)
    inner = out_gain.shape[0]
    heads = step_bias.shape[0]
    length = hidden.shape[1]
    state_dim = (conv_weight.shape[1] - inner) // 2
    width = hidden.shape[2]
    chunks = length // CHUNK
    x_cols = in_weight.shape[1] - inner
    x_pad = -x_cols % 128
    bc_block = inner // (2 * state_dim)
    dt_block = (inner + 2 * state_dim) // 128
    hops = (doc_ids.shape[1] // 4 - 2) // length + 1
    hops = min(hops, seq_count - 1)

    fast = (
        seq_count == 2 * CHIPS
        and lax.axis_size(WT) == PLANES
        and inner == seq_count * LANES
        and width == PLANES * 256
        and state_dim == 128
        and heads == 32
    )
    core = seq_index % 2
    idx = jnp.stack([lax.axis_index(WT), seq_index // 2, core]).astype(jnp.int32)
    shard = in_weight.T.astype(BF16)
    own_x = jnp.pad(shard[inner:], ((0, x_pad), (0, 0)))
    own_z = shard[:inner]
    own_out = out_weight.astype(BF16)
    if fast:
        share = own_x.shape[0] // seq_count
        far_x = gather_far(lax.dynamic_slice_in_dim(own_x, seq_index * share, share, 0))
        cut = share // 32 * 16
        first_x = [gather_first(far_x[:, :cut], 1), gather_first(far_x[:, cut:], 2)]
        plane_x = [gather_second(two, near) for near, two in enumerate(first_x, 1)]
        parts_x = (own_x, plane_x[0], to_core(plane_x[0]), plane_x[1], to_core(plane_x[1]))
        doc_ids, out_weight, conv_weight, conv_bias, step_bias, decay_log, skip_gain, out_gain = after(
            (doc_ids, out_weight, conv_weight, conv_bias, step_bias, decay_log, skip_gain, out_gain), far_x
        )
        own_z = after(shard, far_x)[:inner]
        own_out = out_weight.astype(BF16)
        mine = lax.dynamic_slice_in_dim(own_out, seq_index * 128, 128, 1)
        mine = [lax.dynamic_slice_in_dim(own_z, seq_index * 256, 256, 0), mine[:256], mine[256:]]
        far_rest = gather_far(after(jnp.concatenate(mine, axis=1), far_x))
        far_rest = after(far_rest, parts_x)
        first_rest = [gather_first(far_rest[:, :, 256:], 1), gather_first(far_rest[:, :, :256], 2)]
    else:
        w_x, w_z, w_out = gather_rows(own_x.T).T, gather_rows(own_z.T).T, gather_rows(own_out)

    docs_all = jnp.concatenate([jnp.full((HALO,), -1, jnp.int32), doc_ids[0]])
    docs_ext = lax.dynamic_slice_in_dim(docs_all, seq_index * length, length + HALO, 0)
    docs = docs_ext[HALO:].reshape(chunks, CHUNK)
    windows = jnp.stack([docs_ext[c * CHUNK : (c + 1) * CHUNK + HALO] for c in range(chunks)])
    at_t = jnp.arange(CHUNK)
    at_s = jnp.arange(CHUNK + HALO)
    back = jnp.arange(1, TAPS)
    hits = (at_s[None, None, :] == at_t[None, :, None] + HALO - back[:, None, None])[None] & (
        windows[:, None, None, :] == docs[:, None, :, None]
    )
    shifts = hits.astype(BF16).reshape(chunks, (TAPS - 1) * CHUNK, CHUNK + HALO)
    hits_t = (at_s[:, None, None] == at_t[None, None, :] + HALO - back[None, :, None])[None] & (
        windows[:, :, None, None] == docs[:, None, None, :]
    )
    shifts_t = hits_t.astype(BF16).reshape(chunks, CHUNK + HALO, (TAPS - 1) * CHUNK)
    mask = ((docs[:, :, None] == docs[:, None, :]) & (at_t[None, :] <= at_t[:, None])[None]).astype(F32)
    mask = mask.reshape(length, CHUNK)
    enters = docs == windows[:, HALO - 1 : HALO]
    leaves = docs == docs[:, CHUNK - 1 :]
    enters_device = docs == docs_ext[HALO - 1]
    cols = jnp.stack([enters, leaves, enters_device], axis=-1).reshape(length, 3).astype(F32)
    cols = jnp.pad(cols, ((0, 0), (0, 125)))

    part = np.arange(128)[:, None]
    in_use = part < 3 * heads
    expand = ((part % heads == np.arange(inner)[None, :] // HEAD) & in_use).astype(ml_dtypes.bfloat16)
    select = ((part % heads == np.arange(heads * CHUNK)[None, :] // CHUNK) & in_use).astype(ml_dtypes.bfloat16)
    owner = np.arange(inner)[:, None] // HEAD
    lane = np.arange(256)[None, :]
    collect = (owner + (lane // 128) * heads == lane % 128).astype(ml_dtypes.bfloat16)

    rate = -jnp.exp(decay_log)
    head_rows = jnp.pad(jnp.stack([step_bias, rate * LOG2E, rate, skip_gain]), ((0, 4), (0, 128 - heads)))
    skip_row = jnp.pad(jnp.repeat(skip_gain, HEAD), (0, 2 * state_dim))
    conv_rows = jnp.concatenate([conv_weight, conv_bias[None], skip_row[None]], axis=0)
    conv_rows = jnp.pad(conv_rows, ((0, 2), (0, 0)))
    gain_rows = jnp.broadcast_to(out_gain[None], (8, inner))

    tail = lax.ppermute(hidden[0, length - HALO :], SEQ, [(i, i + 1) for i in range(seq_count - 1)])
    tokens = jnp.concatenate([tail, hidden[0]], axis=0).astype(F32)
    ratio_ext = lax.rsqrt(jnp.mean(tokens * tokens, axis=-1, keepdims=True) + EPS)
    normed_ext = (tokens * ratio_ext * norm_gain[None, :]).astype(BF16)
    normed = normed_ext[HALO:]
    if fast:
        x_width = x_cols + x_pad
        proj_x, w_x = project(
            proj_x_kernel, idx, parts_x, [normed_ext], [shape((length + HALO, x_width), BF16)], [(x_width, width)],
            "proj_x",
        )
        plane_rest = [gather_second(two, near) for near, two in enumerate(after(first_rest, proj_x), 1)]
    else:
        proj_x = mm_cols(normed_ext, w_x).astype(BF16)
        gate = mm_cols(normed, w_z).astype(BF16)
        grad_final = mm_cols(cotangent[0], w_out)

    bc_spec = pl.BlockSpec((length + HALO, 2 * state_dim), lambda i: (0, bc_block))
    dt_spec = pl.BlockSpec((length + HALO, 128), lambda i: (0, dt_block))
    bc_rows = conv_rows[:, inner:]
    outs = [
        shape((length, 256), BF16), shape((length, 256), BF16), shape((256, length), BF16), shape((256, length), BF16),
        shape((length, 128)), shape((length, 128)), shape((length, 128), BF16), shape((length, 128), BF16),
        shape((length, 128), BF16), shape((length, 128), BF16), shape((length, 128), BF16),
        shape((chunks, heads, CHUNK)), shape((8, 128)),
    ]
    ins = [shifts, mask, cols, bc_rows, head_rows]
    b_act, c_act, b_t, c_t, gram, dt_full, dt, e, f, ed, la, cat, kept = pl.pallas_call(
        prep_kernel,
        grid=(1,),
        in_specs=[bc_spec, dt_spec] + [whole(a) for a in ins],
        out_specs=[whole(o) for o in outs],
        out_shape=outs,
        compiler_params=PARAMS,
        name="prep",
        cost_estimate=cost(4),
    )(proj_x, proj_x, *ins)
    kept_row = kept[0, :heads]

    steps = inner // LANES
    sel_width = (LANES // HEAD) * CHUNK
    x_rows = conv_rows[:, :inner]
    y_local, state_part, states = pl.pallas_call(
        fwd_kernel,
        grid=(steps,),
        in_specs=[
            lanes_block(proj_x), whole(shifts), lanes_block(x_rows), whole(gram), whole(c_act), whole(b_t),
            whole(dt), whole(e), whole(f), whole(la), lanes_block(select, sel_width), lanes_block(expand), whole(cat),
        ],
        out_specs=[
            pl.BlockSpec((length, LANES), lambda i: (0, i)), pl.BlockSpec((128, LANES), lambda i: (0, i)),
            pl.BlockSpec((chunks, 128, LANES), lambda i: (0, 0, i)),
        ],
        out_shape=[shape((length, inner)), shape((128, inner), BF16), shape((chunks, 128, inner))],
        compiler_params=PARAMS,
        name="scan_fwd",
        cost_estimate=cost(19),
    )(proj_x, shifts, x_rows, gram, c_act, b_t, dt, e, f, la, select, expand, cat)
    passed = pass_on(state_part, kept_row, hops, 1)
    if fast:
        plane_rest = after(plane_rest, state_part)
        parts_rest = (own_z, own_out, plane_rest[0], to_core(plane_rest[0]), plane_rest[1], to_core(plane_rest[1]))
        gate, grad_final, w_z, w_out = project(
            proj_z_kernel, idx, parts_rest, [normed, cotangent[0]], [shape((length, inner), BF16), shape((length, inner))],
            [(inner, width), (inner, width)], "proj_z",
        )
        passed = after(passed, gate)
    state_in = entering(passed)

    def rows_spec(cols_):
        return pl.BlockSpec((CHUNK, cols_), lambda i: (i, 0))

    output, final, final_far, grad_gate, gate_near, gate_far, grad_mixed, q, gain_part, grad_state = pl.pallas_call(
        gate_kernel,
        grid=(chunks,),
        in_specs=[
            pl.BlockSpec(memory_space=pltpu.SMEM), rows_spec(inner), rows_spec(inner), rows_spec(256), pl.BlockSpec((256, CHUNK), lambda i: (0, i)),
            rows_spec(128), whole(state_in), whole(w_out), whole(expand),
            pl.BlockSpec((inner, 128), lambda i: (0, 0)), whole(gain_rows), rows_spec(width), rows_spec(inner),
        ],
        out_specs=[
            rows_spec(width), rows_spec(inner // 2), rows_spec(inner // 2), rows_spec(inner), rows_spec(inner // 2),
            rows_spec(inner // 2), rows_spec(inner), rows_spec(128),
            pl.BlockSpec((8, inner), lambda i: (0, 0)), pl.BlockSpec((128, inner), lambda i: (0, 0)),
        ],
        out_shape=[
            shape((length, width), BF16), shape((length, inner // 2), BF16), shape((length, inner // 2), BF16),
            shape((length, inner), BF16), shape((length, inner // 2), BF16), shape((length, inner // 2), BF16),
            shape((length, inner), BF16), shape((length, 128)), shape((8, inner)), shape((128, inner), BF16),
        ],
        scratch_shapes=[pltpu.VMEM((128, inner), F32)],
        compiler_params=PARAMS,
        name="gate",
        cost_estimate=cost(18),
    )(idx, y_local, gate, c_act, c_t, ed, state_in, w_out, expand, collect, gain_rows, hidden[0], grad_final)
    passed = pass_on(grad_state, kept_row, hops, -1)

    if fast:
        other = 1 - core
        normed_far, cot_far = to_core(normed), to_core(cotangent[0])
        final_far, gate_far = to_core(final_far), to_core(gate_far)
        early = grads_call(
            early_grads_kernel, idx, [normed, normed_far, final, final_far],
            [gate_near, gate_far, cotangent[0], cot_far], 512,
            [pltpu.VMEM((CHIPS * 256, 2 * length), BF16), pltpu.VMEM((256, 2 * length), BF16)], "early_grads",
        )
        grad_mixed = after(grad_mixed, early)
        passed = after(passed, early)
        early = to_chips(early)
    else:
        both = jnp.stack([final, final_far]).reshape(2, length, 4, inner // 8)
        order = jnp.where(core == 0, both, both[::-1])
        final = order.transpose(1, 2, 0, 3).reshape(length, inner)
        out_grad = reduce_rows(mm_rows(final, cotangent[0]))
        in_z = reduce_rows(mm_rows(normed, grad_gate))
    grad_in = entering(passed)

    acc = lambda rows_, cols_: pl.BlockSpec((rows_, cols_), lambda i: (0, 0))
    halves = []
    for half in range(2):
        count = steps // 2
        first = half * count
        dy = after(grad_mixed, halves[0][0]) if half else grad_mixed
        block = lambda rows_: pl.BlockSpec((rows_, LANES), lambda i: (0, i))
        at = lambda array, size=LANES: lanes_block(array, size, first)
        halves.append(
            pl.pallas_call(
                functools.partial(back_kernel, first=first),
                grid=(count,),
                in_specs=[
                    at(proj_x), at(dy), whole(shifts), whole(shifts_t), at(x_rows),
                    whole(gram), whole(b_act), whole(c_t), whole(dt), whole(e), whole(f), whole(la),
                    at(select, sel_width), at(expand), pl.BlockSpec((LANES, 256), lambda i: (first + i, 0)),
                    whole(cat), pl.BlockSpec((chunks, 128, LANES), lambda i: (0, 0, first + i)), at(state_in), at(grad_in),
                ],
                out_specs=[
                    block(length), block(2 * HALO), block(8), acc(length, 128), acc(length, 256), acc(length, 128),
                    block(8),
                ],
                out_shape=[
                    shape((length, inner // 2), BF16), shape((2 * HALO, inner // 2)), shape((8, inner // 2)),
                    shape((length, 128)), shape((length, 256)), shape((length, 128)), shape((8, inner // 2)),
                ],
                scratch_shapes=[pltpu.VMEM((length + HALO, LANES), F32)],
                compiler_params=PARAMS,
                name="scan_bwd" + str(half),
                cost_estimate=cost(22),
            )(proj_x, dy, shifts, shifts_t, x_rows, gram, b_act, c_t, dt, e, f, la, select, expand,
              collect, cat, states, state_in, grad_in)
        )
    grad_x, edge_x, cg_x, pair_sum, dcb, red, ends = zip(*halves)

    ins = [shifts, shifts_t, mask, bc_rows, head_rows, b_act, c_act, *pair_sum, *dcb, *red, *ends, collect, q, dt_full]
    in_specs = [whole(a) for a in ins]
    in_specs[-3] = acc(inner, 128)
    outs = [
        shape((length, 2 * state_dim + 128), BF16), shape((2 * HALO, 2 * state_dim)), shape((8, 2 * state_dim)),
        shape((8, 128)),
    ]
    grad_bcd, edge_bc, cg_bc, head_grads = pl.pallas_call(
        post_kernel,
        grid=(1,),
        in_specs=[bc_spec, dt_spec] + in_specs,
        out_specs=[whole(o) for o in outs],
        out_shape=outs,
        scratch_shapes=[pltpu.VMEM((length + HALO, 2 * state_dim), F32)],
        compiler_params=PARAMS,
        name="post",
        cost_estimate=cost(5),
    )(proj_x, proj_x, *ins)

    def with_last(part, edge):
        from_next = jnp.pad(shift_seq(edge[HALO - 8 : HALO], -1), ((HALO - 8, 0), (0, 0)))
        return lax.dynamic_update_slice(part, (edge[HALO:] + from_next).astype(BF16), (length - HALO, 0))

    grad_x = [with_last(*pair) for pair in zip(grad_x, edge_x)]
    raw_bcd = grad_bcd
    grad_bcd = with_last(grad_bcd, edge_bc)
    late = []
    if fast:
        quarter = inner // 4
        scratch = lambda others: [pltpu.VMEM((CHIPS * 128 + others, 2 * length), BF16)]
        halves = []
        for part in grad_x:
            near = jnp.where(core == 0, part[:, :quarter], part[:, quarter:])
            far = jnp.where(core == 0, part[:, quarter:], part[:, :quarter])
            halves.append([near, to_core(far)])
        late = late_a = grads_call(
            functools.partial(late_grads_kernel, with_others=False), idx, [after(normed, raw_bcd, early), normed_far],
            halves[0], 128, scratch(0), "late_grads_a",
        )
    norm_row = jnp.broadcast_to(norm_gain[None], (8, width))
    input_grad, norm_gain_part = pl.pallas_call(
        norm_back_kernel,
        grid=(chunks,),
        in_specs=[
            rows_spec(inner), rows_spec(inner // 2), rows_spec(inner // 2), rows_spec(grad_bcd.shape[1]), whole(w_z),
            whole(w_x), rows_spec(width), rows_spec(width), whole(norm_row),
        ],
        out_specs=[rows_spec(width), acc(8, width)],
        out_shape=[shape((length, width)), shape((8, width))],
        compiler_params=PARAMS,
        cost_estimate=cost(8),
        name="norm_back",
    )(grad_gate, *after(grad_x, late), grad_bcd, w_z, w_x, hidden[0], cotangent[0], norm_row)
    norm_gain_part = jnp.sum(norm_gain_part, axis=0)
    small = [jnp.sum(gain_part, axis=0), jnp.concatenate([*cg_x, cg_bc], axis=1)[: TAPS + 1].reshape(-1)]
    small = after(jnp.concatenate(small + [head_grads[:3, :heads].reshape(-1)]), late)
    if fast:
        norm_rows = width // 256
        small_rows = SMALL - norm_rows
        small = jnp.pad(small, (0, 2 * small_rows * 256 - small.shape[0])).reshape(2, small_rows, 256)
        small = lax.dynamic_index_in_dim(small + to_core(small), core, 0, False)
        small = jnp.concatenate([small, norm_gain_part.reshape(norm_rows, 256)], axis=0)
        early = to_planes(sum_over_chips(idx, after(early, late_a)))
        late_a = to_chips(late_a)
        late_b = grads_call(
            functools.partial(late_grads_kernel, with_others=True), idx, [after(normed, late_a, early[0]), normed_far],
            [*halves[1], grad_bcd, to_core(grad_bcd), small], 128 + 2 * SMALL,
            scratch(384) + [pltpu.VMEM((8 * 2 * SMALL, 256), F32)], "late_grads_b",
        )
        early = sum_over_planes(idx, after(early, late_b))
        late = sum_over_chips(idx, after([*late_a, *to_chips(late_b)], early), True)
        early = share_in_plane(after(early, late))
        late = to_planes(late)
        early = both_cores(after(early, late))
        late = share_in_plane(sum_over_planes(idx, late, True))
        in_grad, out_grad = finish_early(idx, early, (in_weight.shape[1], width // PLANES), (inner // PLANES, width))
        in_grad, small = finish_late(idx, both_cores(after(late, out_grad)), in_grad)
        in_grad = in_grad.T
        small = small.reshape(2, SMALL, 256)
        norm_total = jnp.sum(small[:, small_rows:], axis=0).reshape(-1)
        small = small[:, :small_rows].reshape(-1)
    else:
        in_x = reduce_rows(mm_rows(normed, jnp.concatenate([*grad_x, grad_bcd], axis=1)))
        in_grad = jnp.concatenate([in_z, in_x[:, :x_cols]], axis=1)
        small, norm_total = lax.psum((small, norm_gain_part), (SEQ, WT))
    at = 0
    pieces = []
    for size in (inner, TAPS * conv_bias.shape[0], conv_bias.shape[0], heads, heads, heads):
        pieces.append(small[at : at + size])
        at += size
    gain_total, conv_w_total, conv_b_total, step_total, decay_total, skip_total = pieces

    return (
        output[None], input_grad[None], norm_total, in_grad, conv_w_total.reshape(conv_weight.shape), conv_b_total,
        step_total, decay_total, skip_total, gain_total, out_grad,
    )


def solution(mesh):
    placed = (
        P(WT, SEQ, None), P(WT, None), P(), P(WT, None), P(), P(), P(), P(), P(), P(), P(WT, None), P(WT, SEQ, None),
    )
    return jax.shard_map(
        on_device,
        mesh=mesh,
        in_specs=placed,
        out_specs=(
            P(WT, SEQ, None), P(WT, SEQ, None), P(), P(WT, None), P(), P(), P(), P(), P(), P(), P(WT, None),
        ),
        check_vma=False,
    )
```

```python
import functools

import jax
import jax.numpy as jnp
import ml_dtypes
import numpy as np
from jax import lax
from jax.experimental import pallas as pl
from jax.experimental.pallas import tpu as pltpu
from jax.sharding import PartitionSpec as P

EPS = 1e-05
LOG2E = 1.4426950408889634
CHUNK = 128
HALO = 16
LANES = 256
HEAD = 64
TAPS = 4
FULL = lax.Precision.HIGHEST
F32 = jnp.float32
BF16 = jnp.bfloat16
SEQ = "seq"
WT = "wt"


def mm(a, b):
    return jnp.dot(a, b, preferred_element_type=F32)


def mm_cols(a, b):
    return lax.dot_general(a, b, (((1,), (1,)), ((), ())), preferred_element_type=F32)


def mm_rows(a, b):
    return lax.dot_general(a, b, (((0,), (0,)), ((), ())), preferred_element_type=F32)


def sigmoid(x):
    return 0.5 * jnp.tanh(0.5 * x) + 0.5


def split2(x):
    high = x.astype(BF16)
    return high, (x - high.astype(F32)).astype(BF16)


def mm_split(x, ones):
    high, low = split2(x)
    return mm(high, ones) + mm(low, ones)


def mm3(a, b, mult=mm):
    a_high, a_low = a if isinstance(a, tuple) else split2(a)
    b_high, b_low = b if isinstance(b, tuple) else split2(b)
    return mult(a_high, b_high) + mult(a_high, b_low) + mult(a_low, b_high)


def pack3(x):
    high = x.astype(BF16).astype(F32)
    rest = x - high
    mid = rest.astype(BF16).astype(F32)
    low = rest - mid
    return (high + pltpu.roll(mid, 32, 1) + pltpu.roll(low, 64, 1)).astype(BF16)


def softplus(x):
    small = jnp.exp(-jnp.abs(x))
    series = small * (1.0 - small * (0.5 - small * (1.0 / 3.0 - small * (0.25 - small * 0.2))))
    return jnp.maximum(x, 0.0) + jnp.where(small < 0.02, series, jnp.log(1.0 + small))


def conv_inputs(window, shifts):
    moved = mm(shifts, window)
    return [window[HALO:].astype(F32)] + [
        moved[j * CHUNK : (j + 1) * CHUNK] for j in range(TAPS - 1)
    ]


def conv_sum(taps, cw):
    total = cw[TAPS : TAPS + 1]
    for j in range(TAPS):
        total = total + cw[j : j + 1] * taps[j]
    return total


def pair_cols(x):
    return x[:, :128], x[:, 128:]


def pair_rows(x):
    return x[:128], x[128:]


def put_state(ref, state, kept):
    ref[:128] = state.astype(BF16)
    row = lax.broadcasted_iota(jnp.int32, (HALO, kept.shape[1]), 0)
    high = kept.astype(BF16).astype(F32)
    mid = (kept - high).astype(BF16).astype(F32)
    low = kept - high - mid
    parts = jnp.where(row == 0, high, jnp.where(row == 1, mid, jnp.where(row == 2, low, 0.0)))
    ref[128:] = parts.astype(BF16)


def rows_of(c):
    return slice(c * CHUNK, (c + 1) * CHUNK)


def window_of(c):
    return slice(c * CHUNK, (c + 1) * CHUNK + HALO)


def prep_kernel(
    bc_ref, dtr_ref, sh_ref, mask_ref, cols_ref, cw_ref, hp_ref,
    b_ref, c_ref, bt_ref, ct_ref, gm_ref, dtf_ref, dt_ref, e_ref, f_ref, ed_ref, la_ref, cat_ref,
):
    row = lax.broadcasted_iota(jnp.int32, (CHUNK, CHUNK), 0)
    col = lax.broadcasted_iota(jnp.int32, (CHUNK, CHUNK), 1)
    lower = jnp.where(col <= row, 1.0, 0.0).astype(F32)
    used = col < 32
    heads = cat_ref.shape[1]
    before = jnp.zeros((1, CHUNK), F32)
    cw = cw_ref[...]
    for c in range(sh_ref.shape[0]):
        rows = rows_of(c)
        taps = conv_inputs(bc_ref[window_of(c)], sh_ref[c])
        k = conv_sum(taps, cw)
        act = k * sigmoid(k)
        b_act, c_act = act[:, :128], act[:, 128:]
        b_high, b_low = split2(b_act)
        c_high, c_low = split2(c_act)
        gram = mm_cols(c_high, b_high) + mm_cols(c_high, b_low) + mm_cols(c_low, b_high)
        gm_ref[rows] = gram * mask_ref[rows]
        b_ref[rows] = jnp.concatenate([b_high, b_low], axis=1)
        c_ref[rows] = jnp.concatenate([c_high, c_low], axis=1)
        bt_ref[:, rows] = jnp.concatenate(split2(b_act.T), axis=0)
        ct_ref[:, rows] = jnp.concatenate(split2(c_act.T), axis=0)
        step_in = dtr_ref[c * CHUNK + HALO : (c + 1) * CHUNK + HALO].astype(F32) + hp_ref[0:1]
        dt = jnp.where(used, softplus(step_in), 0.0)
        cumul = jnp.dot(lower, dt * hp_ref[1:2], precision=FULL, preferred_element_type=F32)
        last = cumul[CHUNK - 1 : CHUNK]
        cols = cols_ref[rows]
        e = jnp.where(used, jnp.exp2(cumul) * cols[:, 0:1], 0.0)
        f = jnp.where(used, jnp.exp2(last - cumul) * cols[:, 1:2], 0.0)
        ed = jnp.where(used, jnp.exp2(before + cumul) * cols[:, 2:3], 0.0)
        before = before + last
        dtf_ref[rows] = dt
        dt_ref[rows] = pack3(dt)
        e_ref[rows] = pack3(e)
        f_ref[rows] = pack3(f)
        ed_ref[rows] = pack3(ed)
        la_ref[rows] = pack3(cumul)
        cat_ref[c] = cumul.T[:heads]


def weights_of(c, step, la_ref, sel, cat_ref):
    spread = mm(la_ref[rows_of(c)], sel)
    per_step = LANES // HEAD
    out = []
    for i in range(per_step):
        ahead = cat_ref[c, pl.ds(step * per_step + i, 1), :]
        out.append(jnp.exp2(jnp.minimum(spread[:, i * CHUNK : (i + 1) * CHUNK] - ahead, 0.0)))
    return out


def head_pairs(x):
    first = lax.broadcasted_iota(jnp.int32, x.shape, 1) < HEAD
    zero = jnp.zeros_like(x)
    return jnp.concatenate([jnp.where(first, x, zero), jnp.where(first, zero, x)], axis=0)


def fwd_kernel(
    x_ref, sh_ref, cw_ref, gm_ref, c_ref, bt_ref, dt_ref, e_ref, f_ref, la_ref, sel_ref, exp_ref, cat_ref,
    y_ref, s_ref, states_ref,
):
    step = pl.program_id(0)
    cw, sel, expand = cw_ref[...], sel_ref[...], exp_ref[...]
    state = jnp.zeros((128, LANES), F32)
    kept = jnp.ones((1, LANES), F32)
    for c in range(sh_ref.shape[0]):
        rows = rows_of(c)
        k = conv_sum(conv_inputs(x_ref[window_of(c)], sh_ref[c]), cw)
        xa = k * sigmoid(k)
        v = mm(dt_ref[rows], expand) * xa
        ex = mm(e_ref[rows], expand)
        fx = mm(f_ref[rows], expand)
        v_parts = split2(v)
        gm = gm_ref[rows]
        weights = [w * gm for w in weights_of(c, step, la_ref, sel, cat_ref)]
        local = []
        for p in range(LANES // 128):
            own = tuple(head_pairs(part[:, p * 128 : (p + 1) * 128]) for part in v_parts)
            local.append(mm3(jnp.concatenate(weights[2 * p : 2 * p + 2], axis=1), own))
        y = jnp.concatenate(local, axis=1) + ex * mm3(pair_cols(c_ref[rows]), state)
        y_ref[rows] = y + cw[5:6] * xa
        state = ex[CHUNK - 1 : CHUNK] * state + mm3(pair_rows(bt_ref[:, rows]), fx * v)
        states_ref[c] = state
        kept = kept * ex[CHUNK - 1 : CHUNK]
    put_state(s_ref, state, kept)


def gate_kernel(
    idx_ref, y_ref, z_ref, c_ref, ct_ref, ed_ref, sin_ref, wo_ref, exp_ref, expt_ref, gain_ref, hid_ref, df_ref,
    out_ref, fin_ref, fin_far_ref, dz_ref, dz_near_ref, dz_far_ref, dy_ref, q_ref, og_ref, gs_ref, acc_ref,
):
    i = pl.program_id(0)

    @pl.when(i == 0)
    def _():
        og_ref[...] = jnp.zeros_like(og_ref)
        acc_ref[...] = jnp.zeros_like(acc_ref)

    gain = gain_ref[0:1]
    inner = y_ref.shape[1]
    edx = mm(ed_ref[...], exp_ref[...])
    y_full = y_ref[...] + edx * (mm(c_ref[:, :128], sin_ref[...]) + mm(c_ref[:, 128:], sin_ref[...]))
    y = y_full.astype(BF16).astype(F32)
    z = z_ref[...].astype(F32)
    sig = sigmoid(z)
    sz = z * sig
    gated = y * sz
    gnorm = lax.rsqrt(jnp.sum(gated * gated, axis=1, keepdims=True) * (1.0 / inner) + EPS)
    normal = gated * gnorm
    final = (normal * gain).astype(BF16)
    first_core = idx_ref[2] == 0
    block = inner // 8
    for part in range(4):
        a = final[:, 2 * part * block : (2 * part + 1) * block]
        b = final[:, (2 * part + 1) * block : (2 * part + 2) * block]
        fin_ref[:, part * block : (part + 1) * block] = jnp.where(first_core, a, b)
        fin_far_ref[:, part * block : (part + 1) * block] = jnp.where(first_core, b, a)
    out_ref[...] = (hid_ref[...].astype(F32) + mm(final, wo_ref[...])).astype(BF16)
    dfinal = df_ref[...]
    share = dfinal * normal
    og_ref[...] += jnp.sum(share.reshape(-1, 8, inner), axis=0)
    e = dfinal * gain
    mean = jnp.sum(share * gain, axis=1, keepdims=True) * (1.0 / inner)
    dgated = gnorm * (e - normal * mean)
    dz = (dgated * y * (sig * (1.0 + z * (1.0 - sig)))).astype(BF16)
    dz_ref[...] = dz
    dz_near_ref[...] = jnp.where(first_core, dz[:, : inner // 2], dz[:, inner // 2 :])
    dz_far_ref[...] = jnp.where(first_core, dz[:, inner // 2 :], dz[:, : inner // 2])
    dyb = (dgated * sz).astype(BF16)
    dy_ref[...] = dyb
    dy = dyb.astype(F32)
    q_ref[...] = mm_split(dy * y_full, expt_ref[...])
    acc_ref[...] += mm3(pair_rows(ct_ref[...]), edx * dy)

    @pl.when(i == pl.num_programs(0) - 1)
    def _():
        put_state(gs_ref, acc_ref[...], edx[CHUNK - 1 : CHUNK])


def back_kernel(
    x_ref, dy_ref, sh_ref, sht_ref, cw_ref, gm_ref, b_ref, ct_ref, dt_ref, e_ref, f_ref, la_ref,
    sel_ref, exp_ref, expt_ref, cat_ref, states_ref, sin_ref, din_ref,
    dx_ref, edge_ref, cg_ref, m_ref, dcb_ref, red_ref, sd_ref,
    dxw_ref,
    *, first,
):
    step = pl.program_id(0) + first

    @pl.when(pl.program_id(0) == 0)
    def _():
        m_ref[...] = jnp.zeros_like(m_ref)
        dcb_ref[...] = jnp.zeros_like(dcb_ref)
        red_ref[...] = jnp.zeros_like(red_ref)

    count = sh_ref.shape[0]
    cw, sel, expand = cw_ref[...], sel_ref[...], exp_ref[...]
    first_state = sin_ref[...].astype(F32)
    fades = [jnp.ones((1, LANES), F32)]
    for c in range(count):
        end = mm(e_ref[(c + 1) * CHUNK - 16 : (c + 1) * CHUNK], expand)
        fades.append(fades[-1] * end[15:])
    grad = din_ref[...].astype(F32)
    cg = [jnp.zeros((8, LANES), F32) for _ in range(TAPS + 1)]
    sd_ref[...] = jnp.zeros_like(sd_ref)
    after = states_ref[count - 1] + fades[count] * first_state
    for c in reversed(range(count)):
        rows = rows_of(c)
        gradb = grad.astype(BF16)
        sd_ref[c : c + 1] = jnp.sum(after * grad, axis=0, keepdims=True)
        after = fades[c] * first_state
        if c > 0:
            after += states_ref[c - 1]
        taps = conv_inputs(x_ref[window_of(c)], sh_ref[c])
        k = conv_sum(taps, cw)
        sig = sigmoid(k)
        xa = k * sig
        dtx = mm(dt_ref[rows], expand)
        ex = mm(e_ref[rows], expand)
        fx = mm(f_ref[rows], expand)
        v = dtx * xa
        vb = v.astype(BF16)
        dyb = dy_ref[rows]
        dy = dyb.astype(F32)
        gm = gm_ref[rows]
        weights = weights_of(c, step, la_ref, sel, cat_ref)
        dv = []
        total = None
        for p in range(LANES // 128):
            lanes = slice(p * 128, (p + 1) * 128)
            pair = weights[2 * p : 2 * p + 2]
            products = mm_cols(dyb[:, lanes], head_pairs(vb[:, lanes]))
            part = products[:, :CHUNK] * pair[0] + products[:, CHUNK:] * pair[1]
            total = part if total is None else total + part
            stacked = jnp.concatenate([w * gm for w in pair], axis=0)
            own = head_pairs(dyb[:, lanes])
            high, low = split2(stacked)
            dv.append(mm_rows(high, own) + mm_rows(low, own))
        m_ref[rows] += total
        dv = jnp.concatenate(dv, axis=1) + fx * mm3(pair_cols(b_ref[rows]), grad)
        edy = ex * dy
        edyb = edy.astype(BF16)
        dcb_ref[rows, 0:128] += mm_cols((fx * v).astype(BF16), gradb)
        dcb_ref[rows, 128:256] += mm_cols(edyb, after.astype(BF16))
        grad = ex[CHUNK - 1 : CHUNK] * grad + mm3(pair_rows(ct_ref[:, rows]), edy)
        red = mm_split(xa * dv, expt_ref[:, 0:128])
        red += mm_split(dy * xa, expt_ref[:, 128:256])
        red_ref[rows] += red
        dxa = dtx * dv + cw[5:6] * dy
        dk = dxa * (sig * (1.0 + k * (1.0 - sig)))
        cg[TAPS] += jnp.sum(dk.reshape(-1, 8, LANES), axis=0)
        for j in range(TAPS):
            cg[j] += jnp.sum((dk * taps[j]).reshape(-1, 8, LANES), axis=0)
        shifted = jnp.concatenate([(cw[j : j + 1] * dk).astype(BF16) for j in range(1, TAPS)], axis=0)
        moved = mm(sht_ref[c], shifted)
        low, high = c * CHUNK, (c + 1) * CHUNK
        own = cw[0:1] * dk
        dxw_ref[low : low + HALO] = moved[:HALO]
        dxw_ref[low + HALO : high] = moved[HALO:CHUNK] + own[: CHUNK - HALO]
        end = moved[CHUNK:] + own[CHUNK - HALO :]
        if c == count - 1:
            dxw_ref[high : high + HALO] = end
        else:
            dxw_ref[high : high + HALO] += end
    cg_ref[...] = jnp.zeros_like(cg_ref)
    for j in range(TAPS + 1):
        cg_ref[j : j + 1] = jnp.sum(cg[j], axis=0, keepdims=True)
    dx_ref[...] = dxw_ref[HALO:].astype(BF16)
    edge_ref[:HALO] = dxw_ref[:HALO]
    edge_ref[HALO:] = dxw_ref[count * CHUNK :]


def post_kernel(
    bc_ref, dtr_ref, sh_ref, sht_ref, mask_ref, cw_ref, hp_ref, b_ref, c_ref, m0_ref, m1_ref, dcb0_ref, dcb1_ref,
    red0_ref, red1_ref, sd0_ref, sd1_ref, expt_ref, q_ref, dtf_ref,
    dbcd_ref, edge_ref, cg_ref, hg_ref,
    dxw_ref,
):
    count = sh_ref.shape[0]
    cw = cw_ref[...]
    width = bc_ref.shape[1]
    row = lax.broadcasted_iota(jnp.int32, (CHUNK, CHUNK), 0)
    col = lax.broadcasted_iota(jnp.int32, (CHUNK, CHUNK), 1)
    upper = jnp.where(col >= row, 1.0, 0.0).astype(F32)
    used = col < 32
    cg = [jnp.zeros((8, width), F32) for _ in range(TAPS + 1)]
    step_grad = jnp.zeros((8, CHUNK), F32)
    decay_grad = jnp.zeros((8, CHUNK), F32)
    skip_grad = jnp.zeros((8, CHUNK), F32)
    half = sd0_ref.shape[1]
    ends = mm_split(sd0_ref[...], expt_ref[:half]) + mm_split(sd1_ref[...], expt_ref[half:])
    rate = hp_ref[2:3]
    for c in reversed(range(count)):
        rows = rows_of(c)
        taps = conv_inputs(bc_ref[window_of(c)], sh_ref[c])
        k = conv_sum(taps, cw)
        sig = sigmoid(k)
        both = ((m0_ref[rows] + m1_ref[rows]) * mask_ref[rows]).astype(BF16)
        dcb = dcb0_ref[rows] + dcb1_ref[rows]
        db = mm_rows(both, c_ref[rows, :128]) + dcb[:, :128]
        dc = mm(both, b_ref[rows, :128]) + dcb[:, 128:]
        dk = jnp.concatenate([db, dc], axis=1) * (sig * (1.0 + k * (1.0 - sig)))
        cg[TAPS] += jnp.sum(dk.reshape(-1, 8, width), axis=0)
        for j in range(TAPS):
            cg[j] += jnp.sum((dk * taps[j]).reshape(-1, 8, width), axis=0)
        shifted = jnp.concatenate([(cw[j : j + 1] * dk).astype(BF16) for j in range(1, TAPS)], axis=0)
        moved = mm(sht_ref[c], shifted)
        low, high = c * CHUNK, (c + 1) * CHUNK
        own = cw[0:1] * dk
        dxw_ref[low : low + HALO] = moved[:HALO]
        dxw_ref[low + HALO : high] = moved[HALO:CHUNK] + own[: CHUNK - HALO]
        end = moved[CHUNK:] + own[CHUNK - HALO :]
        if c == count - 1:
            dxw_ref[high : high + HALO] = end
        else:
            dxw_ref[high : high + HALO] += end
        red = red0_ref[rows] + red1_ref[rows]
        xdv = red
        dt = dtf_ref[rows]
        vdv = dt * xdv
        dyx = pltpu.roll(red, 96, 1)
        change = q_ref[rows] - hp_ref[3:4] * dyx - vdv
        change = jnp.where(used, change, 0.0)
        da = jnp.dot(upper, change, precision=FULL, preferred_element_type=F32) + ends[c : c + 1]
        step_in = dtr_ref[c * CHUNK + HALO : (c + 1) * CHUNK + HALO].astype(F32) + hp_ref[0:1]
        ddt = jnp.where(used, (xdv + rate * da) * sigmoid(step_in), 0.0)
        dbcd_ref[rows, width:] = ddt.astype(BF16)
        step_grad += jnp.sum(ddt.reshape(-1, 8, CHUNK), axis=0)
        decay_grad += jnp.sum((dt * da).reshape(-1, 8, CHUNK), axis=0)
        skip_grad += jnp.sum(dyx.reshape(-1, 8, CHUNK), axis=0)
    cg_ref[...] = jnp.zeros_like(cg_ref)
    for j in range(TAPS + 1):
        cg_ref[j : j + 1] = jnp.sum(cg[j], axis=0, keepdims=True)
    dbcd_ref[:, :width] = dxw_ref[HALO:].astype(BF16)
    edge_ref[:HALO] = dxw_ref[:HALO]
    edge_ref[HALO:] = dxw_ref[count * CHUNK :]
    hg_ref[...] = jnp.zeros_like(hg_ref)
    hg_ref[0:1] = jnp.sum(step_grad, axis=0, keepdims=True)
    hg_ref[1:2] = rate * jnp.sum(decay_grad, axis=0, keepdims=True)
    hg_ref[2:3] = jnp.sum(skip_grad, axis=0, keepdims=True)


def norm_back_kernel(
    dn_ref, dx0_ref, dx1_ref, db_ref, wx_ref, hid_ref, cot_ref, gain_ref, out_ref, ng_ref
):
    @pl.when(pl.program_id(0) == 0)
    def _():
        ng_ref[...] = jnp.zeros_like(ng_ref)

    half = dx0_ref.shape[1]
    width = out_ref.shape[1]
    dn = dn_ref[...] + mm(dx0_ref[...], wx_ref[:half])
    dn = dn + mm(dx1_ref[...], wx_ref[half : 2 * half]) + mm(db_ref[...], wx_ref[2 * half :])
    x = hid_ref[...].astype(F32)
    ratio = lax.rsqrt(jnp.sum(x * x, axis=1, keepdims=True) * (1.0 / width) + EPS)
    ng_ref[...] += jnp.sum((dn * (x * ratio)).reshape(-1, 8, width), axis=0)
    e = dn * gain_ref[0:1]
    mean = jnp.sum(e * x, axis=1, keepdims=True) * (1.0 / width)
    out_ref[...] = cot_ref[...].astype(F32) + ratio * e - x * (ratio * ratio * ratio * mean)


def whole(array):
    return pl.BlockSpec(array.shape, lambda *_: (0,) * array.ndim)


def lanes_block(array, width=LANES, first=0):
    return pl.BlockSpec((array.shape[0], width), lambda i: (0, first + i))


def shape(dims, dtype=F32):
    return jax.ShapeDtypeStruct(dims, dtype)


PARAMS = pltpu.CompilerParams(vmem_limit_bytes=56 * 1024 * 1024, dimension_semantics=("arbitrary",))


def cost(micros):
    return pl.CostEstimate(flops=int(micros * 1.1e9), transcendentals=0, bytes_accessed=0)


def gather_rows(part):
    count = lax.axis_size(SEQ)
    share = part.shape[0] // count
    mine = lax.dynamic_slice_in_dim(part, lax.axis_index(SEQ) * share, share, 0)
    return lax.all_gather(mine, (WT, SEQ), axis=0, tiled=True)


def reduce_rows(part):
    count = lax.axis_size(SEQ)
    part = part.reshape(lax.axis_size(WT), count, -1, part.shape[1]).transpose(1, 0, 2, 3).reshape(part.shape)
    mine = lax.psum_scatter(part, SEQ, scatter_dimension=0, tiled=True)
    mine = lax.psum_scatter(mine, WT, scatter_dimension=0, tiled=True)
    return lax.all_gather(mine, SEQ, axis=0, tiled=True)


PLANES = 4
CHIPS = 4


def to_chip(x, k):
    return lax.ppermute(x, SEQ, [(i, i ^ (2 * k)) for i in range(2 * CHIPS)])


def to_core(x):
    return lax.ppermute(x, SEQ, [(i, i ^ 1) for i in range(2 * CHIPS)])


def to_plane(x, k):
    return lax.ppermute(x, WT, [(i, (i + k) % PLANES) for i in range(PLANES)])


def copies_into(idx_ref, own, parts, sem):
    z, q, c = idx_ref[0], idx_ref[1], idx_ref[2]
    pairs = own(z)
    for a_ref, b_ref, near, place in parts:
        for j, away in enumerate((0, near, CHIPS - 1 - near, CHIPS - 1)):
            for k in range(1, PLANES):
                plane = lax.rem(z + PLANES - k, PLANES)
                chip = lax.bitwise_xor(q, away)
                at = j * (PLANES - 1) + k - 1
                pairs.append(place(a_ref.at[at], plane, 2 * chip + c))
                pairs.append(place(b_ref.at[at], plane, 2 * chip + 1 - c))
    return [pltpu.make_async_copy(source, target, sem) for source, target in pairs]


def rows_from(start, size):
    return pl.ds(pl.multiple_of(start, 16), size)


def run(copies):
    for copy in copies:
        copy.start()
    for copy in copies:
        copy.wait()


def lanes_at(index, width=256):
    return pl.ds(pl.multiple_of(index * width, width), width)


def proj_x_kernel(
    idx_ref, own_ref, a0_ref, b0_ref, a1_ref, b1_ref, x_ref, out_ref, w_out_ref, w_ref, sem, sem_out
):
    first = a0_ref.shape[1]
    second = a1_ref.shape[1]

    def place_first(source, plane, part):
        return source, w_ref.at[rows_from(part * (first + second), first), lanes_at(plane)]

    def place_second(source, plane, part):
        return source, w_ref.at[rows_from(part * (first + second) + first, second), lanes_at(plane)]

    def own(plane):
        return [(own_ref, w_ref.at[:, lanes_at(plane)])]

    parts = [(a0_ref, b0_ref, 1, place_first), (a1_ref, b1_ref, 2, place_second)]
    run(copies_into(idx_ref, own, parts, sem))
    keep = pltpu.make_async_copy(w_ref, w_out_ref, sem_out)
    keep.start()
    rows = w_ref.shape[0]
    for first in range(0, rows, 512):
        last = min(first + 512, rows)
        out_ref[:, first:last] = mm_cols(x_ref[...], w_ref[first:last]).astype(BF16)
    keep.wait()


def proj_z_kernel(
    idx_ref, oz_ref, oo_ref, a0_ref, b0_ref, a1_ref, b1_ref, x_ref, cot_ref,
    out_ref, df_ref, wz_out_ref, wo_out_ref, wz_ref, wo_ref, sem, sem_out,
):
    share_z = a1_ref.shape[1]
    rows = wo_ref.shape[0] // PLANES

    def place_out(half):
        def place(source, plane, part):
            to = wo_ref.at[rows_from((2 * plane + half) * (rows // 2), rows // 2), lanes_at(part, 128)]
            return source.at[:, half * 128 : (half + 1) * 128], to

        return place

    def place_z(source, plane, part):
        return source, wz_ref.at[rows_from(part * share_z, share_z), lanes_at(plane)]

    def own(plane):
        return [(oz_ref, wz_ref.at[:, lanes_at(plane)]), (oo_ref, wo_ref.at[lanes_at(plane, rows)])]

    parts = [(a0_ref, b0_ref, 1, place_out(half)) for half in range(2)]
    run(copies_into(idx_ref, own, parts + [(a1_ref, b1_ref, 2, place_z)], sem))
    keep = [
        pltpu.make_async_copy(wz_ref, wz_out_ref, sem_out),
        pltpu.make_async_copy(wo_ref, wo_out_ref, sem_out),
    ]
    for copy in keep:
        copy.start()
    for first in range(0, wz_ref.shape[0], 512):
        cols = slice(first, first + 512)
        out_ref[:, cols] = mm_cols(x_ref[...], wz_ref[cols]).astype(BF16)
        df_ref[:, cols] = mm_cols(cot_ref[...], wo_ref[cols])
    for copy in keep:
        copy.wait()


def project(kernel, idx, gathered, ins, outs, kept, name):
    hbm = pl.BlockSpec(memory_space=pl.ANY)
    vmem = pl.BlockSpec(memory_space=pltpu.VMEM)
    return pl.pallas_call(
        kernel,
        in_specs=[pl.BlockSpec(memory_space=pltpu.SMEM)] + [hbm] * len(gathered) + [vmem] * len(ins),
        out_specs=[vmem] * len(outs) + [hbm] * len(kept),
        out_shape=outs + [shape(d, BF16) for d in kept],
        scratch_shapes=[pltpu.VMEM(d, BF16) for d in kept] + [pltpu.SemaphoreType.DMA, pltpu.SemaphoreType.DMA],
        compiler_params=pltpu.CompilerParams(vmem_limit_bytes=56 * 1024 * 1024),
        name=name,
        cost_estimate=cost(10),
    )(idx, *gathered, *ins)


def gather_far(mine):
    return jnp.stack([to_plane(mine, k) for k in range(1, PLANES)])


def gather_first(far, near):
    return jnp.concatenate([far, to_chip(far, near)], axis=0)


def gather_second(two, near):
    return jnp.concatenate([two, to_chip(two, CHIPS - 1 - near)], axis=0)


def keep_transposed(ref, near_ref, far_ref, cols, far_cols=None):
    length = near_ref.shape[0]
    ref[:, :length] = near_ref[:, cols].T
    ref[:, length:] = far_ref[:, cols if far_cols is None else far_cols].T


def early_grads_kernel(idx_ref, n0_ref, n1_ref, f0_ref, f1_ref, dz0_ref, dz1_ref, g0_ref, g1_ref, *refs):
    outs, (dzt_ref, ft_ref) = refs[:CHIPS], refs[CHIPS:]
    block = 256
    length = n0_ref.shape[0]

    @pl.when(pl.program_id(0) == 0)
    def _():
        for k in range(CHIPS):
            rows = dzt_ref.at[k * block : (k + 1) * block]
            keep_transposed(rows, dz0_ref, dz1_ref, lanes_at(lax.bitwise_xor(idx_ref[1], k)))

    keep_transposed(ft_ref, f0_ref, f1_ref, slice(None))
    second = mm(dzt_ref[:, :length], n0_ref[...]) + mm(dzt_ref[:, length:], n1_ref[...])
    for k, out in enumerate(outs):
        lanes = lanes_at(lax.bitwise_xor(idx_ref[1], k))
        first = mm(ft_ref[:, :length], g0_ref[:, lanes]) + mm(ft_ref[:, length:], g1_ref[:, lanes])
        out[0, :block] = first.astype(out.dtype)
        out[0, block:] = second[k * block : (k + 1) * block].astype(out.dtype)


def late_grads_kernel(idx_ref, n0_ref, n1_ref, dx0_ref, dx1_ref, *refs, with_others):
    if with_others:
        db0_ref, small_ref, *outs, dxt_ref, rest_ref = refs
    else:
        *outs, dxt_ref = refs
    block, share = 128, 64
    length = n0_ref.shape[0]
    q, c = idx_ref[1], idx_ref[2]

    @pl.when(pl.program_id(0) == 0)
    def _():
        for k in range(CHIPS):
            rows = dxt_ref.at[k * block : (k + 1) * block]
            keep_transposed(rows, dx0_ref, dx1_ref, lanes_at(lax.bitwise_xor(q, k), block))
        if with_others:
            far_cols = slice(dx0_ref.shape[1], None)
            keep_transposed(dxt_ref.at[CHIPS * block :], db0_ref, dx1_ref, slice(None), far_cols)

    total = mm(dxt_ref[:, :length], n0_ref[...]) + mm(dxt_ref[:, length:], n1_ref[...])
    if with_others:
        rest_ref[: total.shape[0] - CHIPS * block] = total[CHIPS * block :]
        for part in range(2 * CHIPS - 2, 2 * CHIPS):
            for i, x in enumerate(split2(small_ref[...])):
                rest_ref[part * share + i * SMALL : part * share + (i + 1) * SMALL] = x.astype(F32)
    for k, out in enumerate(outs):
        chip = lax.bitwise_xor(q, k)
        out[0, :block] = total[k * block : (k + 1) * block].astype(out.dtype)
        if with_others:
            out[0, block:] = rest_ref[pl.ds(pl.multiple_of((2 * chip + c) * share, share), share)].astype(out.dtype)


def plane_blocks(rows, cols):
    return pl.BlockSpec((rows, cols), lambda i, idx: (0, lax.rem(idx[0] + i, PLANES)))


def grads_call(kernel, idx, blocked, full, rows, scratch, name):
    length = blocked[0].shape[0]
    out = lambda dtype: shape((PLANES, rows, 256), dtype)
    return pl.pallas_call(
        kernel,
        grid_spec=pltpu.PrefetchScalarGridSpec(
            num_scalar_prefetch=1,
            grid=(PLANES,),
            in_specs=[plane_blocks(length, a.shape[1] // PLANES) for a in blocked]
            + [pl.BlockSpec(a.shape, lambda i, idx, n=a.ndim: (0,) * n) for a in full],
            out_specs=[pl.BlockSpec((1, rows, 256), lambda i, idx: (i, 0, 0)) for _ in range(CHIPS)],
            scratch_shapes=scratch,
        ),
        out_shape=[out(F32)] + [out(BF16)] * (CHIPS - 1),
        compiler_params=PARAMS,
        name=name,
        cost_estimate=cost(9),
    )(idx, *blocked, *full)


SMALL = 32


def put_small(ref, total, first, active):
    @pl.when(active)
    def _():
        high, low = split2(total)
        ref[first : first + SMALL] = high.astype(ref.dtype)
        ref[first + SMALL : first + 2 * SMALL] = low.astype(ref.dtype)


def chip_sum_kernel(idx_ref, *refs, small):
    parts, outs = refs[:-PLANES], refs[-PLANES:]
    for k, out in enumerate(outs):
        at = 0
        for i in range(0, len(parts), CHIPS):
            total = parts[i][k]
            for ref in parts[i + 1 : i + CHIPS]:
                total = total + ref[k].astype(F32)
            out[at : at + total.shape[0]] = total.astype(out.dtype)
            at += total.shape[0]
        if small:
            first = total.shape[0] - 2 * SMALL
            total = total[first : first + SMALL] + total[first + SMALL :]
            put_small(out, total, at - 2 * SMALL, idx_ref[1] == CHIPS - 1)


def plane_sum_kernel(idx_ref, *refs, small):
    parts, out = refs[:-1], refs[-1]
    at = 0
    for i in range(0, len(parts), PLANES):
        total = parts[i][...]
        for ref in parts[i + 1 : i + PLANES]:
            total = total + ref[...].astype(F32)
        rows = total.shape[0]
        out[at : at + rows] = total.astype(out.dtype)
        at += rows
    if small:
        total = total[rows - 2 * SMALL : rows - SMALL] + total[rows - SMALL :]
        put_small(out, total, at - 2 * SMALL, idx_ref[1] == CHIPS - 1)


def sum_call(kernel, idx, ins, outs, name):
    vmem = pl.BlockSpec(memory_space=pltpu.VMEM)
    return pl.pallas_call(
        kernel,
        in_specs=[pl.BlockSpec(memory_space=pltpu.SMEM)] + [vmem] * len(ins),
        out_specs=[vmem] * len(outs),
        out_shape=outs,
        compiler_params=pltpu.CompilerParams(vmem_limit_bytes=56 * 1024 * 1024),
        cost_estimate=cost(2),
        name=name,
    )(idx, *ins)


def to_chips(parts):
    return [parts[0]] + [to_chip(parts[k], k) for k in range(1, CHIPS)]


def sum_over_chips(idx, parts, small=False):
    rows = sum(part.shape[1] for part in parts[::CHIPS])
    outs = [shape((rows, 256), dtype) for dtype in [F32] + [BF16] * (PLANES - 1)]
    return sum_call(functools.partial(chip_sum_kernel, small=small), idx, parts, outs, "chip_sum")


def to_planes(parts):
    return [parts[0]] + [to_plane(parts[k], k) for k in range(1, PLANES)]


def sum_over_planes(idx, parts, small=False):
    rows = sum(part.shape[0] for part in parts[::PLANES])
    kernel = functools.partial(plane_sum_kernel, small=small)
    return sum_call(kernel, idx, parts, [shape((rows, 256), BF16)], "plane_sum")[0]


def share_in_plane(block):
    return jnp.stack([block] + [to_chip(block, k) for k in range(1, CHIPS)])


def both_cores(plane):
    return plane, to_core(plane)


def finish_early_kernel(idx_ref, a_ref, b_ref, in_ref, out_ref, rows_ref, sem):
    q, c = idx_ref[1], idx_ref[2]
    block = 256
    for j in range(CHIPS):
        chip = lax.bitwise_xor(q, j)
        for core, ref in ((c, a_ref), (1 - c, b_ref)):
            rows_ref[lanes_at(core * CHIPS + chip)] = ref[j, block:].astype(F32)
            out_ref[lanes_at(core), lanes_at(chip)] = ref[j, :block].astype(F32)
    copy = pltpu.make_async_copy(rows_ref, in_ref.at[: rows_ref.shape[0]], sem)
    copy.start()
    copy.wait()


def finish_late_kernel(idx_ref, a_ref, b_ref, _, in_ref, small_ref, rows_ref, sem):
    q, c = idx_ref[1], idx_ref[2]
    block, share = 128, 64
    inner = 4 * CHIPS * block
    rest = rows_ref.shape[0] - inner
    for j in range(CHIPS):
        chip = lax.bitwise_xor(q, j)
        for core, ref in ((c, a_ref), (1 - c, b_ref)):
            for half in range(2):
                row = ((2 * half + core) * CHIPS + chip) * block
                rows_ref[pl.ds(pl.multiple_of(row, block), block)] = ref[j, half * block : (half + 1) * block].astype(F32)
            part = 2 * chip + core

            @pl.when(part < rest // share)
            def _(ref=ref, part=part, j=j):
                rows_ref[pl.ds(pl.multiple_of(inner + part * share, share), share)] = ref[j, 2 * block :].astype(F32)

            @pl.when(part == rest // share)
            def _(ref=ref, j=j):
                rows_ref[inner + rest // share * share :] = ref[j, 2 * block : 2 * block + rest % share].astype(F32)

            @pl.when(chip == CHIPS - 1)
            def _(ref=ref, core=core, j=j):
                first = 2 * block
                total = ref[j, first : first + SMALL].astype(F32) + ref[j, first + SMALL :].astype(F32)
                small_ref[lanes_at(core, SMALL)] = total

    copy = pltpu.make_async_copy(rows_ref, in_ref.at[in_ref.shape[0] - rows_ref.shape[0] :], sem)
    copy.start()
    copy.wait()


ANY, VMEM, SMEM = (pl.BlockSpec(memory_space=m) for m in (pl.ANY, pltpu.VMEM, pltpu.SMEM))


def finish_early(idx, early, in_dims, out_dims):
    return pl.pallas_call(
        finish_early_kernel,
        in_specs=[SMEM, VMEM, VMEM],
        out_specs=[ANY, VMEM],
        out_shape=[shape(in_dims), shape(out_dims)],
        scratch_shapes=[pltpu.VMEM((8 * 256, in_dims[1]), F32), pltpu.SemaphoreType.DMA],
        compiler_params=pltpu.CompilerParams(vmem_limit_bytes=56 * 1024 * 1024),
        cost_estimate=cost(4),
        name="finish_early",
    )(idx, *early)


def finish_late(idx, late, grad):
    return pl.pallas_call(
        finish_late_kernel,
        in_specs=[SMEM, VMEM, VMEM, ANY],
        out_specs=[ANY, VMEM],
        out_shape=[shape(grad.shape), shape((2 * SMALL, 256))],
        scratch_shapes=[pltpu.VMEM((grad.shape[0] - 8 * 256, grad.shape[1]), F32), pltpu.SemaphoreType.DMA],
        input_output_aliases={3: 0},
        compiler_params=pltpu.CompilerParams(vmem_limit_bytes=56 * 1024 * 1024),
        cost_estimate=cost(4),
        name="finish_late",
    )(idx, *late, grad)


def shift_seq(x, by):
    count = lax.axis_size(SEQ)
    pairs = [(i, i + by) for i in range(count) if 0 <= i + by < count]
    return lax.ppermute(x, SEQ, pairs)


def pass_on(part, hops, sign):
    return [shift_seq(part, sign * hop) for hop in range(1, hops + 1)]


def entering(passed):
    total, fade = None, None
    for moved in passed:
        moved = moved.astype(F32)
        state, kept = moved[:128], jnp.sum(moved[128:131], axis=0, keepdims=True)
        total = state if total is None else total + state * fade
        fade = kept if fade is None else fade * kept
    return total.astype(BF16)


def after(x, *others):
    return lax.optimization_barrier((x, others))[0]


def on_device(
    hidden, doc_ids, norm_gain, in_weight, conv_weight, conv_bias, step_bias, decay_log, skip_gain, out_gain,
    out_weight, cotangent,
):
    seq_count = lax.axis_size(SEQ)
    seq_index = lax.axis_index(SEQ)
    inner = out_gain.shape[0]
    heads = step_bias.shape[0]
    length = hidden.shape[1]
    state_dim = (conv_weight.shape[1] - inner) // 2
    width = hidden.shape[2]
    chunks = length // CHUNK
    x_cols = in_weight.shape[1] - inner
    x_pad = -x_cols % 128
    bc_block = inner // (2 * state_dim)
    dt_block = (inner + 2 * state_dim) // 128
    hops = (doc_ids.shape[1] // 4 - 2) // length + 1
    hops = min(hops, seq_count - 1)

    fast = (
        seq_count == 2 * CHIPS
        and lax.axis_size(WT) == PLANES
        and inner == seq_count * LANES
        and width == PLANES * 256
        and state_dim == 128
        and heads == 32
    )
    core = seq_index % 2
    idx = jnp.stack([lax.axis_index(WT), seq_index // 2, core]).astype(jnp.int32)
    shard = in_weight.T.astype(BF16)
    own_x = jnp.pad(shard[inner:], ((0, x_pad), (0, 0)))
    own_z = shard[:inner]
    own_out = out_weight.astype(BF16)
    if fast:
        share = own_x.shape[0] // seq_count
        far_x = gather_far(lax.dynamic_slice_in_dim(own_x, seq_index * share, share, 0))
        cut = share // 32 * 16
        first_x = [gather_first(far_x[:, :cut], 1), gather_first(far_x[:, cut:], 2)]
        plane_x = [gather_second(two, near) for near, two in enumerate(first_x, 1)]
        parts_x = (own_x, plane_x[0], to_core(plane_x[0]), plane_x[1], to_core(plane_x[1]))
        doc_ids, out_weight, conv_weight, conv_bias, step_bias, decay_log, skip_gain, out_gain = after(
            (doc_ids, out_weight, conv_weight, conv_bias, step_bias, decay_log, skip_gain, out_gain), far_x
        )
        own_z = after(shard, far_x)[:inner]
        own_out = out_weight.astype(BF16)
        mine = lax.dynamic_slice_in_dim(own_out, seq_index * 128, 128, 1)
        mine = [lax.dynamic_slice_in_dim(own_z, seq_index * 256, 256, 0), mine[:256], mine[256:]]
        far_rest = gather_far(after(jnp.concatenate(mine, axis=1), far_x))
        far_rest = after(far_rest, parts_x)
        first_rest = [gather_first(far_rest[:, :, 256:], 1), gather_first(far_rest[:, :, :256], 2)]
    else:
        w_x, w_z, w_out = gather_rows(own_x.T).T, gather_rows(own_z.T).T, gather_rows(own_out)

    docs_all = jnp.concatenate([jnp.full((HALO,), -1, jnp.int32), doc_ids[0]])
    docs_ext = lax.dynamic_slice_in_dim(docs_all, seq_index * length, length + HALO, 0)
    docs = docs_ext[HALO:].reshape(chunks, CHUNK)
    windows = jnp.stack([docs_ext[c * CHUNK : (c + 1) * CHUNK + HALO] for c in range(chunks)])
    at_t = jnp.arange(CHUNK)
    at_s = jnp.arange(CHUNK + HALO)
    back = jnp.arange(1, TAPS)
    hits = (at_s[None, None, :] == at_t[None, :, None] + HALO - back[:, None, None])[None] & (
        windows[:, None, None, :] == docs[:, None, :, None]
    )
    shifts = hits.astype(BF16).reshape(chunks, (TAPS - 1) * CHUNK, CHUNK + HALO)
    hits_t = (at_s[:, None, None] == at_t[None, None, :] + HALO - back[None, :, None])[None] & (
        windows[:, :, None, None] == docs[:, None, None, :]
    )
    shifts_t = hits_t.astype(BF16).reshape(chunks, CHUNK + HALO, (TAPS - 1) * CHUNK)
    mask = ((docs[:, :, None] == docs[:, None, :]) & (at_t[None, :] <= at_t[:, None])[None]).astype(F32)
    mask = mask.reshape(length, CHUNK)
    enters = docs == windows[:, HALO - 1 : HALO]
    leaves = docs == docs[:, CHUNK - 1 :]
    enters_device = docs == docs_ext[HALO - 1]
    cols = jnp.stack([enters, leaves, enters_device], axis=-1).reshape(length, 3).astype(F32)
    cols = jnp.pad(cols, ((0, 0), (0, 125)))

    part = np.arange(128)[:, None]
    in_use = part < 3 * heads
    expand = ((part % heads == np.arange(inner)[None, :] // HEAD) & in_use).astype(ml_dtypes.bfloat16)
    select = ((part % heads == np.arange(heads * CHUNK)[None, :] // CHUNK) & in_use).astype(ml_dtypes.bfloat16)
    owner = np.arange(inner)[:, None] // HEAD
    lane = np.arange(256)[None, :]
    collect = (owner + (lane // 128) * heads == lane % 128).astype(ml_dtypes.bfloat16)

    rate = -jnp.exp(decay_log)
    head_rows = jnp.pad(jnp.stack([step_bias, rate * LOG2E, rate, skip_gain]), ((0, 4), (0, 128 - heads)))
    skip_row = jnp.pad(jnp.repeat(skip_gain, HEAD), (0, 2 * state_dim))
    conv_rows = jnp.concatenate([conv_weight, conv_bias[None], skip_row[None]], axis=0)
    conv_rows = jnp.pad(conv_rows, ((0, 2), (0, 0)))
    gain_rows = jnp.broadcast_to(out_gain[None], (8, inner))

    tail = lax.ppermute(hidden[0, length - HALO :], SEQ, [(i, i + 1) for i in range(seq_count - 1)])
    tokens = jnp.concatenate([tail, hidden[0]], axis=0).astype(F32)
    ratio_ext = lax.rsqrt(jnp.mean(tokens * tokens, axis=-1, keepdims=True) + EPS)
    normed_ext = (tokens * ratio_ext * norm_gain[None, :]).astype(BF16)
    normed = normed_ext[HALO:]
    if fast:
        x_width = x_cols + x_pad
        proj_x, w_x = project(
            proj_x_kernel, idx, parts_x, [normed_ext], [shape((length + HALO, x_width), BF16)], [(x_width, width)],
            "proj_x",
        )
        plane_rest = [gather_second(two, near) for near, two in enumerate(after(first_rest, proj_x), 1)]
    else:
        proj_x = mm_cols(normed_ext, w_x).astype(BF16)
        gate = mm_cols(normed, w_z).astype(BF16)
        grad_final = mm_cols(cotangent[0], w_out)

    bc_spec = pl.BlockSpec((length + HALO, 2 * state_dim), lambda i: (0, bc_block))
    dt_spec = pl.BlockSpec((length + HALO, 128), lambda i: (0, dt_block))
    bc_rows = conv_rows[:, inner:]
    outs = [
        shape((length, 256), BF16), shape((length, 256), BF16), shape((256, length), BF16), shape((256, length), BF16),
        shape((length, 128)), shape((length, 128)), shape((length, 128), BF16), shape((length, 128), BF16),
        shape((length, 128), BF16), shape((length, 128), BF16), shape((length, 128), BF16),
        shape((chunks, heads, CHUNK)),
    ]
    ins = [shifts, mask, cols, bc_rows, head_rows]
    b_act, c_act, b_t, c_t, gram, dt_full, dt, e, f, ed, la, cat = pl.pallas_call(
        prep_kernel,
        grid=(1,),
        in_specs=[bc_spec, dt_spec] + [whole(a) for a in ins],
        out_specs=[whole(o) for o in outs],
        out_shape=outs,
        compiler_params=PARAMS,
        name="prep",
        cost_estimate=cost(4),
    )(proj_x, proj_x, *ins)

    steps = inner // LANES
    sel_width = (LANES // HEAD) * CHUNK
    x_rows = conv_rows[:, :inner]
    y_local, state_part, states = pl.pallas_call(
        fwd_kernel,
        grid=(steps,),
        in_specs=[
            lanes_block(proj_x), whole(shifts), lanes_block(x_rows), whole(gram), whole(c_act), whole(b_t),
            whole(dt), whole(e), whole(f), whole(la), lanes_block(select, sel_width), lanes_block(expand), whole(cat),
        ],
        out_specs=[
            pl.BlockSpec((length, LANES), lambda i: (0, i)), pl.BlockSpec((128 + HALO, LANES), lambda i: (0, i)),
            pl.BlockSpec((chunks, 128, LANES), lambda i: (0, 0, i)),
        ],
        out_shape=[shape((length, inner)), shape((128 + HALO, inner), BF16), shape((chunks, 128, inner))],
        compiler_params=PARAMS,
        name="scan_fwd",
        cost_estimate=cost(19),
    )(proj_x, shifts, x_rows, gram, c_act, b_t, dt, e, f, la, select, expand, cat)
    passed = pass_on(state_part, hops, 1)
    if fast:
        plane_rest = after(plane_rest, state_part)
        parts_rest = (own_z, own_out, plane_rest[0], to_core(plane_rest[0]), plane_rest[1], to_core(plane_rest[1]))
        gate, grad_final, w_z, w_out = project(
            proj_z_kernel, idx, parts_rest, [normed, cotangent[0]], [shape((length, inner), BF16), shape((length, inner))],
            [(inner, width), (inner, width)], "proj_z",
        )
        passed = after(passed, gate)
    state_in = entering(passed)

    def rows_spec(cols_):
        return pl.BlockSpec((CHUNK, cols_), lambda i: (i, 0))

    output, final, final_far, grad_gate, gate_near, gate_far, grad_mixed, q, gain_part, grad_state = pl.pallas_call(
        gate_kernel,
        grid=(chunks,),
        in_specs=[
            pl.BlockSpec(memory_space=pltpu.SMEM), rows_spec(inner), rows_spec(inner), rows_spec(256), pl.BlockSpec((256, CHUNK), lambda i: (0, i)),
            rows_spec(128), whole(state_in), whole(w_out), whole(expand),
            pl.BlockSpec((inner, 128), lambda i: (0, 0)), whole(gain_rows), rows_spec(width), rows_spec(inner),
        ],
        out_specs=[
            rows_spec(width), rows_spec(inner // 2), rows_spec(inner // 2), rows_spec(inner), rows_spec(inner // 2),
            rows_spec(inner // 2), rows_spec(inner), rows_spec(128),
            pl.BlockSpec((8, inner), lambda i: (0, 0)), pl.BlockSpec((128 + HALO, inner), lambda i: (0, 0)),
        ],
        out_shape=[
            shape((length, width), BF16), shape((length, inner // 2), BF16), shape((length, inner // 2), BF16),
            shape((length, inner), BF16), shape((length, inner // 2), BF16), shape((length, inner // 2), BF16),
            shape((length, inner), BF16), shape((length, 128)), shape((8, inner)), shape((128 + HALO, inner), BF16),
        ],
        scratch_shapes=[pltpu.VMEM((128, inner), F32)],
        compiler_params=PARAMS,
        name="gate",
        cost_estimate=cost(18),
    )(idx, y_local, gate, c_act, c_t, ed, state_in, w_out, expand, collect, gain_rows, hidden[0], grad_final)
    passed = pass_on(grad_state, hops, -1)

    if fast:
        other = 1 - core
        normed_far, cot_far = to_core(normed), to_core(cotangent[0])
        final_far, gate_far = to_core(final_far), to_core(gate_far)
        early = grads_call(
            early_grads_kernel, idx, [normed, normed_far, final, final_far],
            [gate_near, gate_far, cotangent[0], cot_far], 512,
            [pltpu.VMEM((CHIPS * 256, 2 * length), BF16), pltpu.VMEM((256, 2 * length), BF16)], "early_grads",
        )
        grad_normed = mm(after(grad_gate, early), w_z)
        grad_mixed = after(grad_mixed, early)
        passed = after(passed, grad_normed)
        early = to_chips(early)
    else:
        both = jnp.stack([final, final_far]).reshape(2, length, 4, inner // 8)
        order = jnp.where(core == 0, both, both[::-1])
        final = order.transpose(1, 2, 0, 3).reshape(length, inner)
        out_grad = reduce_rows(mm_rows(final, cotangent[0]))
        in_z = reduce_rows(mm_rows(normed, grad_gate))
        grad_normed = mm(grad_gate, w_z)
    grad_in = entering(passed)

    acc = lambda rows_, cols_: pl.BlockSpec((rows_, cols_), lambda i: (0, 0))
    halves = []
    for half in range(2):
        count = steps // 2
        first = half * count
        dy = after(grad_mixed, halves[0][0]) if half else grad_mixed
        block = lambda rows_: pl.BlockSpec((rows_, LANES), lambda i: (0, i))
        at = lambda array, size=LANES: lanes_block(array, size, first)
        halves.append(
            pl.pallas_call(
                functools.partial(back_kernel, first=first),
                grid=(count,),
                in_specs=[
                    at(proj_x), at(dy), whole(shifts), whole(shifts_t), at(x_rows),
                    whole(gram), whole(b_act), whole(c_t), whole(dt), whole(e), whole(f), whole(la),
                    at(select, sel_width), at(expand), pl.BlockSpec((LANES, 256), lambda i: (first + i, 0)),
                    whole(cat), pl.BlockSpec((chunks, 128, LANES), lambda i: (0, 0, first + i)), at(state_in), at(grad_in),
                ],
                out_specs=[
                    block(length), block(2 * HALO), block(8), acc(length, 128), acc(length, 256), acc(length, 128),
                    block(8),
                ],
                out_shape=[
                    shape((length, inner // 2), BF16), shape((2 * HALO, inner // 2)), shape((8, inner // 2)),
                    shape((length, 128)), shape((length, 256)), shape((length, 128)), shape((8, inner // 2)),
                ],
                scratch_shapes=[pltpu.VMEM((length + HALO, LANES), F32)],
                compiler_params=PARAMS,
                name="scan_bwd" + str(half),
                cost_estimate=cost(22),
            )(proj_x, dy, shifts, shifts_t, x_rows, gram, b_act, c_t, dt, e, f, la, select, expand,
              collect, cat, states, state_in, grad_in)
        )
    grad_x, edge_x, cg_x, pair_sum, dcb, red, ends = zip(*halves)

    ins = [shifts, shifts_t, mask, bc_rows, head_rows, b_act, c_act, *pair_sum, *dcb, *red, *ends, collect, q, dt_full]
    in_specs = [whole(a) for a in ins]
    in_specs[-3] = acc(inner, 128)
    outs = [
        shape((length, 2 * state_dim + 128), BF16), shape((2 * HALO, 2 * state_dim)), shape((8, 2 * state_dim)),
        shape((8, 128)),
    ]
    grad_bcd, edge_bc, cg_bc, head_grads = pl.pallas_call(
        post_kernel,
        grid=(1,),
        in_specs=[bc_spec, dt_spec] + in_specs,
        out_specs=[whole(o) for o in outs],
        out_shape=outs,
        scratch_shapes=[pltpu.VMEM((length + HALO, 2 * state_dim), F32)],
        compiler_params=PARAMS,
        name="post",
        cost_estimate=cost(5),
    )(proj_x, proj_x, *ins)

    def with_last(part, edge, from_next):
        from_next = jnp.pad(from_next, ((HALO - 8, 0), (0, 0)))
        return lax.dynamic_update_slice(part, (edge[HALO:] + from_next).astype(BF16), (length - HALO, 0))

    raw_bcd = grad_bcd
    first = shift_seq(edge_x[0][HALO - 8 : HALO], -1)
    second = shift_seq(jnp.concatenate([edge_x[1], edge_bc], axis=1)[HALO - 8 : HALO], -1)
    half = inner // 2
    grad_x = [with_last(grad_x[0], edge_x[0], first), with_last(grad_x[1], edge_x[1], second[:, :half])]
    grad_bcd = with_last(grad_bcd, edge_bc, second[:, half:])
    late = []
    if fast:
        quarter = inner // 4
        scratch = lambda others: [pltpu.VMEM((CHIPS * 128 + others, 2 * length), BF16)]
        halves = []
        for part in grad_x:
            near = jnp.where(core == 0, part[:, :quarter], part[:, quarter:])
            far = jnp.where(core == 0, part[:, quarter:], part[:, :quarter])
            if halves:
                far = jnp.concatenate([far, grad_bcd], axis=1)
            halves.append([near, to_core(far)])
        late = late_a = grads_call(
            functools.partial(late_grads_kernel, with_others=False), idx, [after(normed, raw_bcd, early), normed_far],
            halves[0], 128, scratch(0), "late_grads_a",
        )
    norm_row = jnp.broadcast_to(norm_gain[None], (8, width))
    input_grad, norm_gain_part = pl.pallas_call(
        norm_back_kernel,
        grid=(chunks,),
        in_specs=[
            rows_spec(width), rows_spec(inner // 2), rows_spec(inner // 2), rows_spec(grad_bcd.shape[1]),
            whole(w_x), rows_spec(width), rows_spec(width), whole(norm_row),
        ],
        out_specs=[rows_spec(width), acc(8, width)],
        out_shape=[shape((length, width)), shape((8, width))],
        compiler_params=PARAMS,
        cost_estimate=cost(8),
        name="norm_back",
    )(grad_normed, *after(grad_x, late), grad_bcd, w_x, hidden[0], cotangent[0], norm_row)
    norm_gain_part = jnp.sum(norm_gain_part, axis=0)
    small = [jnp.sum(gain_part, axis=0), jnp.concatenate([*cg_x, cg_bc], axis=1)[: TAPS + 1].reshape(-1)]
    small = after(jnp.concatenate(small + [head_grads[:3, :heads].reshape(-1)]), late)
    if fast:
        norm_rows = width // 256
        small_rows = SMALL - norm_rows
        small = jnp.pad(small, (0, 2 * small_rows * 256 - small.shape[0])).reshape(2, small_rows, 256)
        small = lax.dynamic_index_in_dim(small + to_core(small), core, 0, False)
        small = jnp.concatenate([small, norm_gain_part.reshape(norm_rows, 256)], axis=0)
        early = to_planes(sum_over_chips(idx, after(early, late_a)))
        late_a = to_chips(late_a)
        late_b = grads_call(
            functools.partial(late_grads_kernel, with_others=True), idx, [after(normed, late_a, early[0]), normed_far],
            [*halves[1], grad_bcd, small], 128 + 2 * SMALL,
            scratch(384) + [pltpu.VMEM((8 * 2 * SMALL, 256), F32)], "late_grads_b",
        )
        early = sum_over_planes(idx, after(early, late_b))
        late = sum_over_chips(idx, after([*late_a, *to_chips(late_b)], early), True)
        early = share_in_plane(after(early, late))
        late = to_planes(late)
        early = both_cores(after(early, late))
        late = share_in_plane(sum_over_planes(idx, late, True))
        in_grad, out_grad = finish_early(idx, early, (in_weight.shape[1], width // PLANES), (inner // PLANES, width))
        in_grad, small = finish_late(idx, both_cores(late), in_grad)
        in_grad = in_grad.T
        small = small.reshape(2, SMALL, 256)
        norm_total = jnp.sum(small[:, small_rows:], axis=0).reshape(-1)
        small = small[:, :small_rows].reshape(-1)
    else:
        in_x = reduce_rows(mm_rows(normed, jnp.concatenate([*grad_x, grad_bcd], axis=1)))
        in_grad = jnp.concatenate([in_z, in_x[:, :x_cols]], axis=1)
        small, norm_total = lax.psum((small, norm_gain_part), (SEQ, WT))
    at = 0
    pieces = []
    for size in (inner, TAPS * conv_bias.shape[0], conv_bias.shape[0], heads, heads, heads):
        pieces.append(small[at : at + size])
        at += size
    gain_total, conv_w_total, conv_b_total, step_total, decay_total, skip_total = pieces

    return (
        output[None], input_grad[None], norm_total, in_grad, conv_w_total.reshape(conv_weight.shape), conv_b_total,
        step_total, decay_total, skip_total, gain_total, out_grad,
    )


def solution(mesh):
    placed = (
        P(WT, SEQ, None), P(WT, None), P(), P(WT, None), P(), P(), P(), P(), P(), P(), P(WT, None), P(WT, SEQ, None),
    )
    return jax.shard_map(
        on_device,
        mesh=mesh,
        in_specs=placed,
        out_specs=(
            P(WT, SEQ, None), P(WT, SEQ, None), P(), P(WT, None), P(), P(), P(), P(), P(), P(), P(WT, None),
        ),
        check_vma=False,
    )
```

```python
import functools

import jax
import jax.numpy as jnp
import ml_dtypes
import numpy as np
from jax import lax
from jax.experimental import pallas as pl
from jax.experimental.pallas import tpu as pltpu
from jax.sharding import PartitionSpec as P

EPS = 1e-05
LOG2E = 1.4426950408889634
CHUNK = 128
HALO = 16
LANES = 256
HEAD = 64
TAPS = 4
FULL = lax.Precision.HIGHEST
F32 = jnp.float32
BF16 = jnp.bfloat16
SEQ = "seq"
WT = "wt"


def mm(a, b):
    return jnp.dot(a, b, preferred_element_type=F32)


def mm_cols(a, b):
    return lax.dot_general(a, b, (((1,), (1,)), ((), ())), preferred_element_type=F32)


def mm_rows(a, b):
    return lax.dot_general(a, b, (((0,), (0,)), ((), ())), preferred_element_type=F32)


def sigmoid(x):
    return 0.5 * jnp.tanh(0.5 * x) + 0.5


def split2(x):
    high = x.astype(BF16)
    return high, (x - high.astype(F32)).astype(BF16)


def mm_split(x, ones):
    high, low = split2(x)
    return mm(high, ones) + mm(low, ones)


def mm3(a, b, mult=mm):
    a_high, a_low = a if isinstance(a, tuple) else split2(a)
    b_high, b_low = b if isinstance(b, tuple) else split2(b)
    return mult(a_high, b_high) + mult(a_high, b_low) + mult(a_low, b_high)


def pack3(x):
    high = x.astype(BF16).astype(F32)
    rest = x - high
    mid = rest.astype(BF16).astype(F32)
    low = rest - mid
    return (high + pltpu.roll(mid, 32, 1) + pltpu.roll(low, 64, 1)).astype(BF16)


def softplus(x):
    small = jnp.exp(-jnp.abs(x))
    series = small * (1.0 - small * (0.5 - small * (1.0 / 3.0 - small * (0.25 - small * 0.2))))
    return jnp.maximum(x, 0.0) + jnp.where(small < 0.02, series, jnp.log(1.0 + small))


def conv_inputs(window, shifts):
    moved = mm(shifts, window)
    return [window[HALO:].astype(F32)] + [
        moved[j * CHUNK : (j + 1) * CHUNK] for j in range(TAPS - 1)
    ]


def conv_sum(taps, cw):
    total = cw[TAPS : TAPS + 1]
    for j in range(TAPS):
        total = total + cw[j : j + 1] * taps[j]
    return total


def pair_cols(x):
    return x[:, :128], x[:, 128:]


def pair_rows(x):
    return x[:128], x[128:]


def put_state(ref, state, kept):
    ref[:128] = state.astype(BF16)
    row = lax.broadcasted_iota(jnp.int32, (HALO, kept.shape[1]), 0)
    high = kept.astype(BF16).astype(F32)
    mid = (kept - high).astype(BF16).astype(F32)
    low = kept - high - mid
    parts = jnp.where(row == 0, high, jnp.where(row == 1, mid, jnp.where(row == 2, low, 0.0)))
    ref[128:] = parts.astype(BF16)


def rows_of(c):
    return slice(c * CHUNK, (c + 1) * CHUNK)


def window_of(c):
    return slice(c * CHUNK, (c + 1) * CHUNK + HALO)


def prep_kernel(
    bc_ref, dtr_ref, sh_ref, mask_ref, cols_ref, cw_ref, hp_ref,
    b_ref, c_ref, bt_ref, ct_ref, gm_ref, dtf_ref, dt_ref, e_ref, f_ref, ed_ref, la_ref, cat_ref,
):
    row = lax.broadcasted_iota(jnp.int32, (CHUNK, CHUNK), 0)
    col = lax.broadcasted_iota(jnp.int32, (CHUNK, CHUNK), 1)
    lower = jnp.where(col <= row, 1.0, 0.0).astype(F32)
    used = col < 32
    heads = cat_ref.shape[1]
    before = jnp.zeros((1, CHUNK), F32)
    cw = cw_ref[...]
    for c in range(sh_ref.shape[0]):
        rows = rows_of(c)
        taps = conv_inputs(bc_ref[window_of(c)], sh_ref[c])
        k = conv_sum(taps, cw)
        act = k * sigmoid(k)
        b_act, c_act = act[:, :128], act[:, 128:]
        b_high, b_low = split2(b_act)
        c_high, c_low = split2(c_act)
        gram = mm_cols(c_high, b_high) + mm_cols(c_high, b_low) + mm_cols(c_low, b_high)
        gm_ref[rows] = gram * mask_ref[rows]
        b_ref[rows] = jnp.concatenate([b_high, b_low], axis=1)
        c_ref[rows] = jnp.concatenate([c_high, c_low], axis=1)
        bt_ref[:, rows] = jnp.concatenate(split2(b_act.T), axis=0)
        ct_ref[:, rows] = jnp.concatenate(split2(c_act.T), axis=0)
        step_in = dtr_ref[c * CHUNK + HALO : (c + 1) * CHUNK + HALO].astype(F32) + hp_ref[0:1]
        dt = jnp.where(used, softplus(step_in), 0.0)
        cumul = jnp.dot(lower, dt * hp_ref[1:2], precision=FULL, preferred_element_type=F32)
        last = cumul[CHUNK - 1 : CHUNK]
        cols = cols_ref[rows]
        e = jnp.where(used, jnp.exp2(cumul) * cols[:, 0:1], 0.0)
        f = jnp.where(used, jnp.exp2(last - cumul) * cols[:, 1:2], 0.0)
        ed = jnp.where(used, jnp.exp2(before + cumul) * cols[:, 2:3], 0.0)
        before = before + last
        dtf_ref[rows] = dt
        dt_ref[rows] = pack3(dt)
        e_ref[rows] = pack3(e)
        f_ref[rows] = pack3(f)
        ed_ref[rows] = pack3(ed)
        la_ref[rows] = pack3(cumul)
        cat_ref[c] = cumul.T[:heads]


def weights_of(c, step, la_ref, sel, cat_ref):
    spread = mm(la_ref[rows_of(c)], sel)
    per_step = LANES // HEAD
    out = []
    for i in range(per_step):
        ahead = cat_ref[c, pl.ds(step * per_step + i, 1), :]
        out.append(jnp.exp2(jnp.minimum(spread[:, i * CHUNK : (i + 1) * CHUNK] - ahead, 0.0)))
    return out


def head_pairs(x):
    first = lax.broadcasted_iota(jnp.int32, x.shape, 1) < HEAD
    zero = jnp.zeros_like(x)
    return jnp.concatenate([jnp.where(first, x, zero), jnp.where(first, zero, x)], axis=0)


def fwd_kernel(
    x_ref, sh_ref, cw_ref, gm_ref, c_ref, bt_ref, dt_ref, e_ref, f_ref, la_ref, sel_ref, exp_ref, cat_ref,
    y_ref, s_ref, states_ref,
):
    step = pl.program_id(0)
    cw, sel, expand = cw_ref[...], sel_ref[...], exp_ref[...]
    state = jnp.zeros((128, LANES), F32)
    kept = jnp.ones((1, LANES), F32)
    for c in range(sh_ref.shape[0]):
        rows = rows_of(c)
        k = conv_sum(conv_inputs(x_ref[window_of(c)], sh_ref[c]), cw)
        xa = k * sigmoid(k)
        v = mm(dt_ref[rows], expand) * xa
        ex = mm(e_ref[rows], expand)
        fx = mm(f_ref[rows], expand)
        v_parts = split2(v)
        gm = gm_ref[rows]
        weights = [w * gm for w in weights_of(c, step, la_ref, sel, cat_ref)]
        local = []
        for p in range(LANES // 128):
            own = tuple(head_pairs(part[:, p * 128 : (p + 1) * 128]) for part in v_parts)
            local.append(mm3(jnp.concatenate(weights[2 * p : 2 * p + 2], axis=1), own))
        y = jnp.concatenate(local, axis=1) + ex * mm3(pair_cols(c_ref[rows]), state)
        y_ref[rows] = y + cw[5:6] * xa
        state = ex[CHUNK - 1 : CHUNK] * state + mm3(pair_rows(bt_ref[:, rows]), fx * v)
        states_ref[c] = state
        kept = kept * ex[CHUNK - 1 : CHUNK]
    put_state(s_ref, state, kept)


def gate_kernel(
    idx_ref, y_ref, z_ref, c_ref, ct_ref, ed_ref, sin_ref, wo_ref, exp_ref, expt_ref, gain_ref, hid_ref, df_ref,
    out_ref, fin_ref, fin_far_ref, dz_ref, dz_near_ref, dz_far_ref, dy_ref, q_ref, og_ref, gs_ref, acc_ref,
):
    i = pl.program_id(0)

    @pl.when(i == 0)
    def _():
        og_ref[...] = jnp.zeros_like(og_ref)
        acc_ref[...] = jnp.zeros_like(acc_ref)

    gain = gain_ref[0:1]
    inner = y_ref.shape[1]
    edx = mm(ed_ref[...], exp_ref[...])
    y_full = y_ref[...] + edx * (mm(c_ref[:, :128], sin_ref[...]) + mm(c_ref[:, 128:], sin_ref[...]))
    y = y_full.astype(BF16).astype(F32)
    z = z_ref[...].astype(F32)
    sig = sigmoid(z)
    sz = z * sig
    gated = y * sz
    gnorm = lax.rsqrt(jnp.sum(gated * gated, axis=1, keepdims=True) * (1.0 / inner) + EPS)
    normal = gated * gnorm
    final = (normal * gain).astype(BF16)
    first_core = idx_ref[2] == 0
    block = inner // 8
    for part in range(4):
        a = final[:, 2 * part * block : (2 * part + 1) * block]
        b = final[:, (2 * part + 1) * block : (2 * part + 2) * block]
        fin_ref[:, part * block : (part + 1) * block] = jnp.where(first_core, a, b)
        fin_far_ref[:, part * block : (part + 1) * block] = jnp.where(first_core, b, a)
    out_ref[...] = (hid_ref[...].astype(F32) + mm(final, wo_ref[...])).astype(BF16)
    dfinal = df_ref[...]
    share = dfinal * normal
    og_ref[...] += jnp.sum(share.reshape(-1, 8, inner), axis=0)
    e = dfinal * gain
    mean = jnp.sum(share * gain, axis=1, keepdims=True) * (1.0 / inner)
    dgated = gnorm * (e - normal * mean)
    dz = (dgated * y * (sig * (1.0 + z * (1.0 - sig)))).astype(BF16)
    dz_ref[...] = dz
    dz_near_ref[...] = jnp.where(first_core, dz[:, : inner // 2], dz[:, inner // 2 :])
    dz_far_ref[...] = jnp.where(first_core, dz[:, inner // 2 :], dz[:, : inner // 2])
    dyb = (dgated * sz).astype(BF16)
    dy_ref[...] = dyb
    dy = dyb.astype(F32)
    q_ref[...] = mm_split(dy * y_full, expt_ref[...])
    acc_ref[...] += mm3(pair_rows(ct_ref[...]), edx * dy)

    @pl.when(i == pl.num_programs(0) - 1)
    def _():
        put_state(gs_ref, acc_ref[...], edx[CHUNK - 1 : CHUNK])


def back_kernel(
    x_ref, dy_ref, sh_ref, sht_ref, cw_ref, gm_ref, b_ref, ct_ref, dt_ref, e_ref, f_ref, la_ref,
    sel_ref, exp_ref, expt_ref, cat_ref, states_ref, sin_ref, din_ref,
    dx_ref, edge_ref, cg_ref, m_ref, dcb_ref, red_ref, sd_ref,
    dxw_ref,
    *, first,
):
    step = pl.program_id(0) + first

    @pl.when(pl.program_id(0) == 0)
    def _():
        m_ref[...] = jnp.zeros_like(m_ref)
        dcb_ref[...] = jnp.zeros_like(dcb_ref)
        red_ref[...] = jnp.zeros_like(red_ref)

    count = sh_ref.shape[0]
    cw, sel, expand = cw_ref[...], sel_ref[...], exp_ref[...]
    first_state = sin_ref[...].astype(F32)
    fades = [jnp.ones((1, LANES), F32)]
    for c in range(count):
        end = mm(e_ref[(c + 1) * CHUNK - 16 : (c + 1) * CHUNK], expand)
        fades.append(fades[-1] * end[15:])
    grad = din_ref[...].astype(F32)
    cg = [jnp.zeros((8, LANES), F32) for _ in range(TAPS + 1)]
    sd_ref[...] = jnp.zeros_like(sd_ref)
    after = states_ref[count - 1] + fades[count] * first_state
    for c in reversed(range(count)):
        rows = rows_of(c)
        gradb = grad.astype(BF16)
        sd_ref[c : c + 1] = jnp.sum(after * grad, axis=0, keepdims=True)
        after = fades[c] * first_state
        if c > 0:
            after += states_ref[c - 1]
        taps = conv_inputs(x_ref[window_of(c)], sh_ref[c])
        k = conv_sum(taps, cw)
        sig = sigmoid(k)
        xa = k * sig
        dtx = mm(dt_ref[rows], expand)
        ex = mm(e_ref[rows], expand)
        fx = mm(f_ref[rows], expand)
        v = dtx * xa
        vb = v.astype(BF16)
        dyb = dy_ref[rows]
        dy = dyb.astype(F32)
        gm = gm_ref[rows]
        weights = weights_of(c, step, la_ref, sel, cat_ref)
        dv = []
        total = None
        for p in range(LANES // 128):
            lanes = slice(p * 128, (p + 1) * 128)
            pair = weights[2 * p : 2 * p + 2]
            products = mm_cols(dyb[:, lanes], head_pairs(vb[:, lanes]))
            part = products[:, :CHUNK] * pair[0] + products[:, CHUNK:] * pair[1]
            total = part if total is None else total + part
            stacked = jnp.concatenate([w * gm for w in pair], axis=0)
            own = head_pairs(dyb[:, lanes])
            high, low = split2(stacked)
            dv.append(mm_rows(high, own) + mm_rows(low, own))
        m_ref[rows] += total
        dv = jnp.concatenate(dv, axis=1) + fx * mm3(pair_cols(b_ref[rows]), grad)
        edy = ex * dy
        edyb = edy.astype(BF16)
        dcb_ref[rows, 0:128] += mm_cols((fx * v).astype(BF16), gradb)
        dcb_ref[rows, 128:256] += mm_cols(edyb, after.astype(BF16))
        grad = ex[CHUNK - 1 : CHUNK] * grad + mm3(pair_rows(ct_ref[:, rows]), edy)
        red = mm_split(xa * dv, expt_ref[:, 0:128])
        red += mm_split(dy * xa, expt_ref[:, 128:256])
        red_ref[rows] += red
        dxa = dtx * dv + cw[5:6] * dy
        dk = dxa * (sig * (1.0 + k * (1.0 - sig)))
        cg[TAPS] += jnp.sum(dk.reshape(-1, 8, LANES), axis=0)
        for j in range(TAPS):
            cg[j] += jnp.sum((dk * taps[j]).reshape(-1, 8, LANES), axis=0)
        shifted = jnp.concatenate([(cw[j : j + 1] * dk).astype(BF16) for j in range(1, TAPS)], axis=0)
        moved = mm(sht_ref[c], shifted)
        low, high = c * CHUNK, (c + 1) * CHUNK
        own = cw[0:1] * dk
        dxw_ref[low : low + HALO] = moved[:HALO]
        dxw_ref[low + HALO : high] = moved[HALO:CHUNK] + own[: CHUNK - HALO]
        end = moved[CHUNK:] + own[CHUNK - HALO :]
        if c == count - 1:
            dxw_ref[high : high + HALO] = end
        else:
            dxw_ref[high : high + HALO] += end
    cg_ref[...] = jnp.zeros_like(cg_ref)
    for j in range(TAPS + 1):
        cg_ref[j : j + 1] = jnp.sum(cg[j], axis=0, keepdims=True)
    dx_ref[...] = dxw_ref[HALO:].astype(BF16)
    edge_ref[:HALO] = dxw_ref[:HALO]
    edge_ref[HALO:] = dxw_ref[count * CHUNK :]


def post_kernel(
    bc_ref, dtr_ref, sh_ref, sht_ref, mask_ref, cw_ref, hp_ref, b_ref, c_ref, m0_ref, m1_ref, dcb0_ref, dcb1_ref,
    red0_ref, red1_ref, sd0_ref, sd1_ref, expt_ref, q_ref, dtf_ref,
    dbcd_ref, edge_ref, cg_ref, hg_ref,
    dxw_ref,
):
    count = sh_ref.shape[0]
    cw = cw_ref[...]
    width = bc_ref.shape[1]
    row = lax.broadcasted_iota(jnp.int32, (CHUNK, CHUNK), 0)
    col = lax.broadcasted_iota(jnp.int32, (CHUNK, CHUNK), 1)
    upper = jnp.where(col >= row, 1.0, 0.0).astype(F32)
    used = col < 32
    cg = [jnp.zeros((8, width), F32) for _ in range(TAPS + 1)]
    step_grad = jnp.zeros((8, CHUNK), F32)
    decay_grad = jnp.zeros((8, CHUNK), F32)
    skip_grad = jnp.zeros((8, CHUNK), F32)
    half = sd0_ref.shape[1]
    ends = mm_split(sd0_ref[...], expt_ref[:half]) + mm_split(sd1_ref[...], expt_ref[half:])
    rate = hp_ref[2:3]
    for c in reversed(range(count)):
        rows = rows_of(c)
        taps = conv_inputs(bc_ref[window_of(c)], sh_ref[c])
        k = conv_sum(taps, cw)
        sig = sigmoid(k)
        both = ((m0_ref[rows] + m1_ref[rows]) * mask_ref[rows]).astype(BF16)
        dcb = dcb0_ref[rows] + dcb1_ref[rows]
        db = mm_rows(both, c_ref[rows, :128]) + dcb[:, :128]
        dc = mm(both, b_ref[rows, :128]) + dcb[:, 128:]
        dk = jnp.concatenate([db, dc], axis=1) * (sig * (1.0 + k * (1.0 - sig)))
        cg[TAPS] += jnp.sum(dk.reshape(-1, 8, width), axis=0)
        for j in range(TAPS):
            cg[j] += jnp.sum((dk * taps[j]).reshape(-1, 8, width), axis=0)
        shifted = jnp.concatenate([(cw[j : j + 1] * dk).astype(BF16) for j in range(1, TAPS)], axis=0)
        moved = mm(sht_ref[c], shifted)
        low, high = c * CHUNK, (c + 1) * CHUNK
        own = cw[0:1] * dk
        dxw_ref[low : low + HALO] = moved[:HALO]
        dxw_ref[low + HALO : high] = moved[HALO:CHUNK] + own[: CHUNK - HALO]
        end = moved[CHUNK:] + own[CHUNK - HALO :]
        if c == count - 1:
            dxw_ref[high : high + HALO] = end
        else:
            dxw_ref[high : high + HALO] += end
        red = red0_ref[rows] + red1_ref[rows]
        xdv = red
        dt = dtf_ref[rows]
        vdv = dt * xdv
        dyx = pltpu.roll(red, 96, 1)
        change = q_ref[rows] - hp_ref[3:4] * dyx - vdv
        change = jnp.where(used, change, 0.0)
        da = jnp.dot(upper, change, precision=FULL, preferred_element_type=F32) + ends[c : c + 1]
        step_in = dtr_ref[c * CHUNK + HALO : (c + 1) * CHUNK + HALO].astype(F32) + hp_ref[0:1]
        ddt = jnp.where(used, (xdv + rate * da) * sigmoid(step_in), 0.0)
        dbcd_ref[rows, width:] = ddt.astype(BF16)
        step_grad += jnp.sum(ddt.reshape(-1, 8, CHUNK), axis=0)
        decay_grad += jnp.sum((dt * da).reshape(-1, 8, CHUNK), axis=0)
        skip_grad += jnp.sum(dyx.reshape(-1, 8, CHUNK), axis=0)
    cg_ref[...] = jnp.zeros_like(cg_ref)
    for j in range(TAPS + 1):
        cg_ref[j : j + 1] = jnp.sum(cg[j], axis=0, keepdims=True)
    dbcd_ref[:, :width] = dxw_ref[HALO:].astype(BF16)
    edge_ref[:HALO] = dxw_ref[:HALO]
    edge_ref[HALO:] = dxw_ref[count * CHUNK :]
    hg_ref[...] = jnp.zeros_like(hg_ref)
    hg_ref[0:1] = jnp.sum(step_grad, axis=0, keepdims=True)
    hg_ref[1:2] = rate * jnp.sum(decay_grad, axis=0, keepdims=True)
    hg_ref[2:3] = jnp.sum(skip_grad, axis=0, keepdims=True)


def norm_back_kernel(
    dn_ref, dx0_ref, dx1_ref, db_ref, wx_ref, hid_ref, cot_ref, gain_ref, out_ref, ng_ref
):
    @pl.when(pl.program_id(0) == 0)
    def _():
        ng_ref[...] = jnp.zeros_like(ng_ref)

    half = dx0_ref.shape[1]
    width = out_ref.shape[1]
    dn = dn_ref[...] + mm(dx0_ref[...], wx_ref[:half])
    dn = dn + mm(dx1_ref[...], wx_ref[half : 2 * half]) + mm(db_ref[...], wx_ref[2 * half :])
    x = hid_ref[...].astype(F32)
    ratio = lax.rsqrt(jnp.sum(x * x, axis=1, keepdims=True) * (1.0 / width) + EPS)
    ng_ref[...] += jnp.sum((dn * (x * ratio)).reshape(-1, 8, width), axis=0)
    e = dn * gain_ref[0:1]
    mean = jnp.sum(e * x, axis=1, keepdims=True) * (1.0 / width)
    out_ref[...] = cot_ref[...].astype(F32) + ratio * e - x * (ratio * ratio * ratio * mean)


def whole(array):
    return pl.BlockSpec(array.shape, lambda *_: (0,) * array.ndim)


def lanes_block(array, width=LANES, first=0):
    return pl.BlockSpec((array.shape[0], width), lambda i: (0, first + i))


def shape(dims, dtype=F32):
    return jax.ShapeDtypeStruct(dims, dtype)


PARAMS = pltpu.CompilerParams(vmem_limit_bytes=56 * 1024 * 1024, dimension_semantics=("arbitrary",))


def cost(micros):
    return pl.CostEstimate(flops=int(micros * 1.1e9), transcendentals=0, bytes_accessed=0)


def gather_rows(part):
    count = lax.axis_size(SEQ)
    share = part.shape[0] // count
    mine = lax.dynamic_slice_in_dim(part, lax.axis_index(SEQ) * share, share, 0)
    return lax.all_gather(mine, (WT, SEQ), axis=0, tiled=True)


def reduce_rows(part):
    count = lax.axis_size(SEQ)
    part = part.reshape(lax.axis_size(WT), count, -1, part.shape[1]).transpose(1, 0, 2, 3).reshape(part.shape)
    mine = lax.psum_scatter(part, SEQ, scatter_dimension=0, tiled=True)
    mine = lax.psum_scatter(mine, WT, scatter_dimension=0, tiled=True)
    return lax.all_gather(mine, SEQ, axis=0, tiled=True)


PLANES = 4
CHIPS = 4


def to_chip(x, k):
    return lax.ppermute(x, SEQ, [(i, i ^ (2 * k)) for i in range(2 * CHIPS)])


def to_core(x):
    return lax.ppermute(x, SEQ, [(i, i ^ 1) for i in range(2 * CHIPS)])


def to_plane(x, k):
    return lax.ppermute(x, WT, [(i, (i + k) % PLANES) for i in range(PLANES)])


def copies_into(idx_ref, own, parts, sem):
    z, q, c = idx_ref[0], idx_ref[1], idx_ref[2]
    pairs = own(z)
    for a_ref, b_ref, near, place in parts:
        for j, away in enumerate((0, near, CHIPS - 1 - near, CHIPS - 1)):
            for k in range(1, PLANES):
                plane = lax.rem(z + PLANES - k, PLANES)
                chip = lax.bitwise_xor(q, away)
                at = j * (PLANES - 1) + k - 1
                pairs.append(place(a_ref.at[at], plane, 2 * chip + c))
                pairs.append(place(b_ref.at[at], plane, 2 * chip + 1 - c))
    return [pltpu.make_async_copy(source, target, sem) for source, target in pairs]


def rows_from(start, size):
    return pl.ds(pl.multiple_of(start, 16), size)


def run(copies):
    for copy in copies:
        copy.start()
    for copy in copies:
        copy.wait()


def lanes_at(index, width=256):
    return pl.ds(pl.multiple_of(index * width, width), width)


def proj_x_kernel(
    idx_ref, own_ref, a0_ref, b0_ref, a1_ref, b1_ref, x_ref, out_ref, w_out_ref, w_ref, sem, sem_out
):
    first = a0_ref.shape[1]
    second = a1_ref.shape[1]

    def place_first(source, plane, part):
        return source, w_ref.at[rows_from(part * (first + second), first), lanes_at(plane)]

    def place_second(source, plane, part):
        return source, w_ref.at[rows_from(part * (first + second) + first, second), lanes_at(plane)]

    def own(plane):
        return [(own_ref, w_ref.at[:, lanes_at(plane)])]

    parts = [(a0_ref, b0_ref, 1, place_first), (a1_ref, b1_ref, 2, place_second)]
    run(copies_into(idx_ref, own, parts, sem))
    keep = pltpu.make_async_copy(w_ref, w_out_ref, sem_out)
    keep.start()
    rows = w_ref.shape[0]
    for first in range(0, rows, 512):
        last = min(first + 512, rows)
        out_ref[:, first:last] = mm_cols(x_ref[...], w_ref[first:last]).astype(BF16)
    keep.wait()


def proj_z_kernel(
    idx_ref, oz_ref, oo_ref, a0_ref, b0_ref, a1_ref, b1_ref, x_ref, cot_ref,
    out_ref, df_ref, wz_out_ref, wo_out_ref, wz_ref, wo_ref, sem, sem_out,
):
    share_z = a1_ref.shape[1]
    rows = wo_ref.shape[0] // PLANES

    def place_out(half):
        def place(source, plane, part):
            to = wo_ref.at[rows_from((2 * plane + half) * (rows // 2), rows // 2), lanes_at(part, 128)]
            return source.at[:, half * 128 : (half + 1) * 128], to

        return place

    def place_z(source, plane, part):
        return source, wz_ref.at[rows_from(part * share_z, share_z), lanes_at(plane)]

    def own(plane):
        return [(oz_ref, wz_ref.at[:, lanes_at(plane)]), (oo_ref, wo_ref.at[lanes_at(plane, rows)])]

    parts = [(a0_ref, b0_ref, 1, place_out(half)) for half in range(2)]
    run(copies_into(idx_ref, own, parts + [(a1_ref, b1_ref, 2, place_z)], sem))
    keep = [
        pltpu.make_async_copy(wz_ref, wz_out_ref, sem_out),
        pltpu.make_async_copy(wo_ref, wo_out_ref, sem_out),
    ]
    for copy in keep:
        copy.start()
    for first in range(0, wz_ref.shape[0], 512):
        cols = slice(first, first + 512)
        out_ref[:, cols] = mm_cols(x_ref[...], wz_ref[cols]).astype(BF16)
        df_ref[:, cols] = mm_cols(cot_ref[...], wo_ref[cols])
    for copy in keep:
        copy.wait()


def project(kernel, idx, gathered, ins, outs, kept, name):
    hbm = pl.BlockSpec(memory_space=pl.ANY)
    vmem = pl.BlockSpec(memory_space=pltpu.VMEM)
    return pl.pallas_call(
        kernel,
        in_specs=[pl.BlockSpec(memory_space=pltpu.SMEM)] + [hbm] * len(gathered) + [vmem] * len(ins),
        out_specs=[vmem] * len(outs) + [hbm] * len(kept),
        out_shape=outs + [shape(d, BF16) for d in kept],
        scratch_shapes=[pltpu.VMEM(d, BF16) for d in kept] + [pltpu.SemaphoreType.DMA, pltpu.SemaphoreType.DMA],
        compiler_params=pltpu.CompilerParams(vmem_limit_bytes=56 * 1024 * 1024),
        name=name,
        cost_estimate=cost(10),
    )(idx, *gathered, *ins)


def gather_far(mine):
    return jnp.stack([to_plane(mine, k) for k in range(1, PLANES)])


def gather_first(far, near):
    return jnp.concatenate([far, to_chip(far, near)], axis=0)


def gather_second(two, near):
    return jnp.concatenate([two, to_chip(two, CHIPS - 1 - near)], axis=0)


def keep_transposed(ref, near_ref, far_ref, cols, far_cols=None):
    length = near_ref.shape[0]
    ref[:, :length] = near_ref[:, cols].T
    ref[:, length:] = far_ref[:, cols if far_cols is None else far_cols].T


def early_grads_kernel(idx_ref, n0_ref, n1_ref, f0_ref, f1_ref, dz0_ref, dz1_ref, g0_ref, g1_ref, *refs):
    outs, (dzt_ref, ft_ref) = refs[:CHIPS], refs[CHIPS:]
    block = 256
    length = n0_ref.shape[0]

    @pl.when(pl.program_id(0) == 0)
    def _():
        for k in range(CHIPS):
            rows = dzt_ref.at[k * block : (k + 1) * block]
            keep_transposed(rows, dz0_ref, dz1_ref, lanes_at(lax.bitwise_xor(idx_ref[1], k)))

    keep_transposed(ft_ref, f0_ref, f1_ref, slice(None))
    second = mm(dzt_ref[:, :length], n0_ref[...]) + mm(dzt_ref[:, length:], n1_ref[...])
    for k, out in enumerate(outs):
        lanes = lanes_at(lax.bitwise_xor(idx_ref[1], k))
        first = mm(ft_ref[:, :length], g0_ref[:, lanes]) + mm(ft_ref[:, length:], g1_ref[:, lanes])
        out[0, :block] = first.astype(out.dtype)
        out[0, block:] = second[k * block : (k + 1) * block].astype(out.dtype)


def late_grads_kernel(idx_ref, n0_ref, n1_ref, dx0_ref, dx1_ref, *refs, with_others):
    if with_others:
        db0_ref, small_ref, *outs, dxt_ref, rest_ref = refs
    else:
        *outs, dxt_ref = refs
    block, share = 128, 64
    length = n0_ref.shape[0]
    q, c = idx_ref[1], idx_ref[2]

    @pl.when(pl.program_id(0) == 0)
    def _():
        for k in range(CHIPS):
            rows = dxt_ref.at[k * block : (k + 1) * block]
            keep_transposed(rows, dx0_ref, dx1_ref, lanes_at(lax.bitwise_xor(q, k), block))
        if with_others:
            far_cols = slice(dx0_ref.shape[1], None)
            keep_transposed(dxt_ref.at[CHIPS * block :], db0_ref, dx1_ref, slice(None), far_cols)

    total = mm(dxt_ref[:, :length], n0_ref[...]) + mm(dxt_ref[:, length:], n1_ref[...])
    if with_others:
        rest_ref[: total.shape[0] - CHIPS * block] = total[CHIPS * block :]
        for part in range(2 * CHIPS - 2, 2 * CHIPS):
            for i, x in enumerate(split2(small_ref[...])):
                rest_ref[part * share + i * SMALL : part * share + (i + 1) * SMALL] = x.astype(F32)
    for k, out in enumerate(outs):
        chip = lax.bitwise_xor(q, k)
        out[0, :block] = total[k * block : (k + 1) * block].astype(out.dtype)
        if with_others:
            out[0, block:] = rest_ref[pl.ds(pl.multiple_of((2 * chip + c) * share, share), share)].astype(out.dtype)


def plane_blocks(rows, cols):
    return pl.BlockSpec((rows, cols), lambda i, idx: (0, lax.rem(idx[0] + i, PLANES)))


def grads_call(kernel, idx, blocked, full, rows, scratch, name):
    length = blocked[0].shape[0]
    out = lambda dtype: shape((PLANES, rows, 256), dtype)
    return pl.pallas_call(
        kernel,
        grid_spec=pltpu.PrefetchScalarGridSpec(
            num_scalar_prefetch=1,
            grid=(PLANES,),
            in_specs=[plane_blocks(length, a.shape[1] // PLANES) for a in blocked]
            + [pl.BlockSpec(a.shape, lambda i, idx, n=a.ndim: (0,) * n) for a in full],
            out_specs=[pl.BlockSpec((1, rows, 256), lambda i, idx: (i, 0, 0)) for _ in range(CHIPS)],
            scratch_shapes=scratch,
        ),
        out_shape=[out(F32)] + [out(BF16)] * (CHIPS - 1),
        compiler_params=PARAMS,
        name=name,
        cost_estimate=cost(9),
    )(idx, *blocked, *full)


SMALL = 32


def put_small(ref, total, first, active):
    @pl.when(active)
    def _():
        high, low = split2(total)
        ref[first : first + SMALL] = high.astype(ref.dtype)
        ref[first + SMALL : first + 2 * SMALL] = low.astype(ref.dtype)


def chip_sum_kernel(idx_ref, *refs, small):
    parts, outs = refs[:-PLANES], refs[-PLANES:]
    for k, out in enumerate(outs):
        at = 0
        for i in range(0, len(parts), CHIPS):
            total = parts[i][k]
            for ref in parts[i + 1 : i + CHIPS]:
                total = total + ref[k].astype(F32)
            out[at : at + total.shape[0]] = total.astype(out.dtype)
            at += total.shape[0]
        if small:
            first = total.shape[0] - 2 * SMALL
            total = total[first : first + SMALL] + total[first + SMALL :]
            put_small(out, total, at - 2 * SMALL, idx_ref[1] == CHIPS - 1)


def plane_sum_kernel(idx_ref, *refs, small):
    parts, out = refs[:-1], refs[-1]
    at = 0
    for i in range(0, len(parts), PLANES):
        total = parts[i][...]
        for ref in parts[i + 1 : i + PLANES]:
            total = total + ref[...].astype(F32)
        rows = total.shape[0]
        out[at : at + rows] = total.astype(out.dtype)
        at += rows
    if small:
        total = total[rows - 2 * SMALL : rows - SMALL] + total[rows - SMALL :]
        put_small(out, total, at - 2 * SMALL, idx_ref[1] == CHIPS - 1)


def sum_call(kernel, idx, ins, outs, name):
    vmem = pl.BlockSpec(memory_space=pltpu.VMEM)
    return pl.pallas_call(
        kernel,
        in_specs=[pl.BlockSpec(memory_space=pltpu.SMEM)] + [vmem] * len(ins),
        out_specs=[vmem] * len(outs),
        out_shape=outs,
        compiler_params=pltpu.CompilerParams(vmem_limit_bytes=56 * 1024 * 1024),
        cost_estimate=cost(2),
        name=name,
    )(idx, *ins)


def to_chips(parts):
    return [parts[0]] + [to_chip(parts[k], k) for k in range(1, CHIPS)]


def sum_over_chips(idx, parts, small=False):
    rows = sum(part.shape[1] for part in parts[::CHIPS])
    outs = [shape((rows, 256), dtype) for dtype in [F32] + [BF16] * (PLANES - 1)]
    return sum_call(functools.partial(chip_sum_kernel, small=small), idx, parts, outs, "chip_sum")


def to_planes(parts):
    return [parts[0]] + [to_plane(parts[k], k) for k in range(1, PLANES)]


def sum_over_planes(idx, parts, small=False):
    rows = sum(part.shape[0] for part in parts[::PLANES])
    kernel = functools.partial(plane_sum_kernel, small=small)
    return sum_call(kernel, idx, parts, [shape((rows, 256), BF16)], "plane_sum")[0]


def share_in_plane(block):
    return jnp.stack([block] + [to_chip(block, k) for k in range(1, CHIPS)])


def both_cores(plane):
    return plane, to_core(plane)


def finish_early_kernel(idx_ref, a_ref, b_ref, in_ref, out_ref, rows_ref, sem):
    q, c = idx_ref[1], idx_ref[2]
    block = 256
    for j in range(CHIPS):
        chip = lax.bitwise_xor(q, j)
        for core, ref in ((c, a_ref), (1 - c, b_ref)):
            rows_ref[lanes_at(core * CHIPS + chip)] = ref[j, block:].astype(F32)
            out_ref[lanes_at(core), lanes_at(chip)] = ref[j, :block].astype(F32)
    copy = pltpu.make_async_copy(rows_ref, in_ref.at[: rows_ref.shape[0]], sem)
    copy.start()
    copy.wait()


def finish_late_kernel(idx_ref, a_ref, b_ref, _, in_ref, small_ref, rows_ref, sem):
    q, c = idx_ref[1], idx_ref[2]
    block, share = 128, 64
    inner = 4 * CHIPS * block
    rest = rows_ref.shape[0] - inner
    for j in range(CHIPS):
        chip = lax.bitwise_xor(q, j)
        for core, ref in ((c, a_ref), (1 - c, b_ref)):
            for half in range(2):
                row = ((2 * half + core) * CHIPS + chip) * block
                rows_ref[pl.ds(pl.multiple_of(row, block), block)] = ref[j, half * block : (half + 1) * block].astype(F32)
            part = 2 * chip + core

            @pl.when(part < rest // share)
            def _(ref=ref, part=part, j=j):
                rows_ref[pl.ds(pl.multiple_of(inner + part * share, share), share)] = ref[j, 2 * block :].astype(F32)

            @pl.when(part == rest // share)
            def _(ref=ref, j=j):
                rows_ref[inner + rest // share * share :] = ref[j, 2 * block : 2 * block + rest % share].astype(F32)

            @pl.when(chip == CHIPS - 1)
            def _(ref=ref, core=core, j=j):
                first = 2 * block
                total = ref[j, first : first + SMALL].astype(F32) + ref[j, first + SMALL :].astype(F32)
                small_ref[lanes_at(core, SMALL)] = total

    copy = pltpu.make_async_copy(rows_ref, in_ref.at[in_ref.shape[0] - rows_ref.shape[0] :], sem)
    copy.start()
    copy.wait()


ANY, VMEM, SMEM = (pl.BlockSpec(memory_space=m) for m in (pl.ANY, pltpu.VMEM, pltpu.SMEM))


def finish_early(idx, early, in_dims, out_dims):
    return pl.pallas_call(
        finish_early_kernel,
        in_specs=[SMEM, VMEM, VMEM],
        out_specs=[ANY, VMEM],
        out_shape=[shape(in_dims), shape(out_dims)],
        scratch_shapes=[pltpu.VMEM((8 * 256, in_dims[1]), F32), pltpu.SemaphoreType.DMA],
        compiler_params=pltpu.CompilerParams(vmem_limit_bytes=56 * 1024 * 1024),
        cost_estimate=cost(4),
        name="finish_early",
    )(idx, *early)


def finish_late(idx, late, grad):
    return pl.pallas_call(
        finish_late_kernel,
        in_specs=[SMEM, VMEM, VMEM, ANY],
        out_specs=[ANY, VMEM],
        out_shape=[shape(grad.shape), shape((2 * SMALL, 256))],
        scratch_shapes=[pltpu.VMEM((grad.shape[0] - 8 * 256, grad.shape[1]), F32), pltpu.SemaphoreType.DMA],
        input_output_aliases={3: 0},
        compiler_params=pltpu.CompilerParams(vmem_limit_bytes=56 * 1024 * 1024),
        cost_estimate=cost(4),
        name="finish_late",
    )(idx, *late, grad)


def shift_seq(x, by):
    count = lax.axis_size(SEQ)
    pairs = [(i, i + by) for i in range(count) if 0 <= i + by < count]
    return lax.ppermute(x, SEQ, pairs)


def pass_on(part, hops, sign):
    return [shift_seq(part, sign * hop) for hop in range(1, hops + 1)]


def entering(passed):
    total, fade = None, None
    for moved in passed:
        moved = moved.astype(F32)
        state, kept = moved[:128], jnp.sum(moved[128:131], axis=0, keepdims=True)
        total = state if total is None else total + state * fade
        fade = kept if fade is None else fade * kept
    return total.astype(BF16)


def after(x, *others):
    return lax.optimization_barrier((x, others))[0]


def on_device(
    hidden, doc_ids, norm_gain, in_weight, conv_weight, conv_bias, step_bias, decay_log, skip_gain, out_gain,
    out_weight, cotangent,
):
    seq_count = lax.axis_size(SEQ)
    seq_index = lax.axis_index(SEQ)
    inner = out_gain.shape[0]
    heads = step_bias.shape[0]
    length = hidden.shape[1]
    state_dim = (conv_weight.shape[1] - inner) // 2
    width = hidden.shape[2]
    chunks = length // CHUNK
    x_cols = in_weight.shape[1] - inner
    x_pad = -x_cols % 128
    bc_block = inner // (2 * state_dim)
    dt_block = (inner + 2 * state_dim) // 128
    hops = (doc_ids.shape[1] // 4 - 2) // length + 1
    hops = min(hops, seq_count - 1)

    fast = (
        seq_count == 2 * CHIPS
        and lax.axis_size(WT) == PLANES
        and inner == seq_count * LANES
        and width == PLANES * 256
        and state_dim == 128
        and heads == 32
    )
    core = seq_index % 2
    idx = jnp.stack([lax.axis_index(WT), seq_index // 2, core]).astype(jnp.int32)
    shard = in_weight.T.astype(BF16)
    own_x = jnp.pad(shard[inner:], ((0, x_pad), (0, 0)))
    own_z = shard[:inner]
    own_out = out_weight.astype(BF16)
    if fast:
        share = own_x.shape[0] // seq_count
        far_x = gather_far(lax.dynamic_slice_in_dim(own_x, seq_index * share, share, 0))
        cut = share // 32 * 16
        first_x = [gather_first(far_x[:, :cut], 1), gather_first(far_x[:, cut:], 2)]
        plane_x = [gather_second(two, near) for near, two in enumerate(first_x, 1)]
        parts_x = (own_x, plane_x[0], to_core(plane_x[0]), plane_x[1], to_core(plane_x[1]))
        doc_ids, out_weight, conv_weight, conv_bias, step_bias, decay_log, skip_gain, out_gain = after(
            (doc_ids, out_weight, conv_weight, conv_bias, step_bias, decay_log, skip_gain, out_gain), far_x
        )
        own_z = after(shard, far_x)[:inner]
        own_out = out_weight.astype(BF16)
        mine = lax.dynamic_slice_in_dim(own_out, seq_index * 128, 128, 1)
        mine = [lax.dynamic_slice_in_dim(own_z, seq_index * 256, 256, 0), mine[:256], mine[256:]]
        far_rest = gather_far(after(jnp.concatenate(mine, axis=1), far_x))
        far_rest = after(far_rest, parts_x)
        first_rest = [gather_first(far_rest[:, :, 256:], 1), gather_first(far_rest[:, :, :256], 2)]
    else:
        w_x, w_z, w_out = gather_rows(own_x.T).T, gather_rows(own_z.T).T, gather_rows(own_out)

    docs_all = jnp.concatenate([jnp.full((HALO,), -1, jnp.int32), doc_ids[0]])
    docs_ext = lax.dynamic_slice_in_dim(docs_all, seq_index * length, length + HALO, 0)
    docs = docs_ext[HALO:].reshape(chunks, CHUNK)
    windows = jnp.stack([docs_ext[c * CHUNK : (c + 1) * CHUNK + HALO] for c in range(chunks)])
    at_t = jnp.arange(CHUNK)
    at_s = jnp.arange(CHUNK + HALO)
    back = jnp.arange(1, TAPS)
    hits = (at_s[None, None, :] == at_t[None, :, None] + HALO - back[:, None, None])[None] & (
        windows[:, None, None, :] == docs[:, None, :, None]
    )
    shifts = hits.astype(BF16).reshape(chunks, (TAPS - 1) * CHUNK, CHUNK + HALO)
    hits_t = (at_s[:, None, None] == at_t[None, None, :] + HALO - back[None, :, None])[None] & (
        windows[:, :, None, None] == docs[:, None, None, :]
    )
    shifts_t = hits_t.astype(BF16).reshape(chunks, CHUNK + HALO, (TAPS - 1) * CHUNK)
    mask = ((docs[:, :, None] == docs[:, None, :]) & (at_t[None, :] <= at_t[:, None])[None]).astype(F32)
    mask = mask.reshape(length, CHUNK)
    enters = docs == windows[:, HALO - 1 : HALO]
    leaves = docs == docs[:, CHUNK - 1 :]
    enters_device = docs == docs_ext[HALO - 1]
    cols = jnp.stack([enters, leaves, enters_device], axis=-1).reshape(length, 3).astype(F32)
    cols = jnp.pad(cols, ((0, 0), (0, 125)))

    part = np.arange(128)[:, None]
    in_use = part < 3 * heads
    expand = ((part % heads == np.arange(inner)[None, :] // HEAD) & in_use).astype(ml_dtypes.bfloat16)
    select = ((part % heads == np.arange(heads * CHUNK)[None, :] // CHUNK) & in_use).astype(ml_dtypes.bfloat16)
    owner = np.arange(inner)[:, None] // HEAD
    lane = np.arange(256)[None, :]
    collect = (owner + (lane // 128) * heads == lane % 128).astype(ml_dtypes.bfloat16)

    rate = -jnp.exp(decay_log)
    head_rows = jnp.pad(jnp.stack([step_bias, rate * LOG2E, rate, skip_gain]), ((0, 4), (0, 128 - heads)))
    skip_row = jnp.pad(jnp.repeat(skip_gain, HEAD), (0, 2 * state_dim))
    conv_rows = jnp.concatenate([conv_weight, conv_bias[None], skip_row[None]], axis=0)
    conv_rows = jnp.pad(conv_rows, ((0, 2), (0, 0)))
    gain_rows = jnp.broadcast_to(out_gain[None], (8, inner))

    tail = lax.ppermute(hidden[0, length - HALO :], SEQ, [(i, i + 1) for i in range(seq_count - 1)])
    tokens = jnp.concatenate([tail, hidden[0]], axis=0).astype(F32)
    ratio_ext = lax.rsqrt(jnp.mean(tokens * tokens, axis=-1, keepdims=True) + EPS)
    normed_ext = (tokens * ratio_ext * norm_gain[None, :]).astype(BF16)
    normed = normed_ext[HALO:]
    if fast:
        x_width = x_cols + x_pad
        proj_x, w_x = project(
            proj_x_kernel, idx, parts_x, [after(normed_ext, shifts_t, gain_rows)], [shape((length + HALO, x_width), BF16)], [(x_width, width)],
            "proj_x",
        )
        plane_rest = [gather_second(two, near) for near, two in enumerate(after(first_rest, proj_x), 1)]
    else:
        proj_x = mm_cols(normed_ext, w_x).astype(BF16)
        gate = mm_cols(normed, w_z).astype(BF16)
        grad_final = mm_cols(cotangent[0], w_out)

    bc_spec = pl.BlockSpec((length + HALO, 2 * state_dim), lambda i: (0, bc_block))
    dt_spec = pl.BlockSpec((length + HALO, 128), lambda i: (0, dt_block))
    bc_rows = conv_rows[:, inner:]
    outs = [
        shape((length, 256), BF16), shape((length, 256), BF16), shape((256, length), BF16), shape((256, length), BF16),
        shape((length, 128)), shape((length, 128)), shape((length, 128), BF16), shape((length, 128), BF16),
        shape((length, 128), BF16), shape((length, 128), BF16), shape((length, 128), BF16),
        shape((chunks, heads, CHUNK)),
    ]
    ins = [shifts, mask, cols, bc_rows, head_rows]
    b_act, c_act, b_t, c_t, gram, dt_full, dt, e, f, ed, la, cat = pl.pallas_call(
        prep_kernel,
        grid=(1,),
        in_specs=[bc_spec, dt_spec] + [whole(a) for a in ins],
        out_specs=[whole(o) for o in outs],
        out_shape=outs,
        compiler_params=PARAMS,
        name="prep",
        cost_estimate=cost(4),
    )(proj_x, proj_x, *ins)

    steps = inner // LANES
    sel_width = (LANES // HEAD) * CHUNK
    x_rows = conv_rows[:, :inner]
    y_local, state_part, states = pl.pallas_call(
        fwd_kernel,
        grid=(steps,),
        in_specs=[
            lanes_block(proj_x), whole(shifts), lanes_block(x_rows), whole(gram), whole(c_act), whole(b_t),
            whole(dt), whole(e), whole(f), whole(la), lanes_block(select, sel_width), lanes_block(expand), whole(cat),
        ],
        out_specs=[
            pl.BlockSpec((length, LANES), lambda i: (0, i)), pl.BlockSpec((128 + HALO, LANES), lambda i: (0, i)),
            pl.BlockSpec((chunks, 128, LANES), lambda i: (0, 0, i)),
        ],
        out_shape=[shape((length, inner)), shape((128 + HALO, inner), BF16), shape((chunks, 128, inner))],
        compiler_params=PARAMS,
        name="scan_fwd",
        cost_estimate=cost(19),
    )(proj_x, shifts, x_rows, gram, c_act, b_t, dt, e, f, la, select, expand, cat)
    passed = pass_on(state_part, hops, 1)
    if fast:
        plane_rest = after(plane_rest, state_part)
        parts_rest = (own_z, own_out, plane_rest[0], to_core(plane_rest[0]), plane_rest[1], to_core(plane_rest[1]))
        gate, grad_final, w_z, w_out = project(
            proj_z_kernel, idx, parts_rest, [normed, cotangent[0]], [shape((length, inner), BF16), shape((length, inner))],
            [(inner, width), (inner, width)], "proj_z",
        )
        passed = after(passed, gate)
    state_in = entering(passed)

    def rows_spec(cols_):
        return pl.BlockSpec((CHUNK, cols_), lambda i: (i, 0))

    output, final, final_far, grad_gate, gate_near, gate_far, grad_mixed, q, gain_part, grad_state = pl.pallas_call(
        gate_kernel,
        grid=(chunks,),
        in_specs=[
            pl.BlockSpec(memory_space=pltpu.SMEM), rows_spec(inner), rows_spec(inner), rows_spec(256), pl.BlockSpec((256, CHUNK), lambda i: (0, i)),
            rows_spec(128), whole(state_in), whole(w_out), whole(expand),
            pl.BlockSpec((inner, 128), lambda i: (0, 0)), whole(gain_rows), rows_spec(width), rows_spec(inner),
        ],
        out_specs=[
            rows_spec(width), rows_spec(inner // 2), rows_spec(inner // 2), rows_spec(inner), rows_spec(inner // 2),
            rows_spec(inner // 2), rows_spec(inner), rows_spec(128),
            pl.BlockSpec((8, inner), lambda i: (0, 0)), pl.BlockSpec((128 + HALO, inner), lambda i: (0, 0)),
        ],
        out_shape=[
            shape((length, width), BF16), shape((length, inner // 2), BF16), shape((length, inner // 2), BF16),
            shape((length, inner), BF16), shape((length, inner // 2), BF16), shape((length, inner // 2), BF16),
            shape((length, inner), BF16), shape((length, 128)), shape((8, inner)), shape((128 + HALO, inner), BF16),
        ],
        scratch_shapes=[pltpu.VMEM((128, inner), F32)],
        compiler_params=PARAMS,
        name="gate",
        cost_estimate=cost(18),
    )(idx, y_local, gate, c_act, c_t, ed, state_in, w_out, expand, collect, gain_rows, hidden[0], grad_final)
    passed = pass_on(grad_state, hops, -1)

    if fast:
        other = 1 - core
        normed_far, cot_far = to_core(normed), to_core(cotangent[0])
        final_far, gate_far = to_core(final_far), to_core(gate_far)
        early = grads_call(
            early_grads_kernel, idx, [normed, normed_far, final, final_far],
            [gate_near, gate_far, cotangent[0], cot_far], 512,
            [pltpu.VMEM((CHIPS * 256, 2 * length), BF16), pltpu.VMEM((256, 2 * length), BF16)], "early_grads",
        )
        grad_normed = mm(after(grad_gate, early), w_z)
        grad_mixed = after(grad_mixed, early)
        passed = after(passed, grad_normed)
        early = to_chips(early)
    else:
        both = jnp.stack([final, final_far]).reshape(2, length, 4, inner // 8)
        order = jnp.where(core == 0, both, both[::-1])
        final = order.transpose(1, 2, 0, 3).reshape(length, inner)
        out_grad = reduce_rows(mm_rows(final, cotangent[0]))
        in_z = reduce_rows(mm_rows(normed, grad_gate))
        grad_normed = mm(grad_gate, w_z)
    grad_in = entering(passed)

    acc = lambda rows_, cols_: pl.BlockSpec((rows_, cols_), lambda i: (0, 0))
    halves = []
    for half in range(2):
        count = steps // 2
        first = half * count
        dy = after(grad_mixed, halves[0][0]) if half else grad_mixed
        block = lambda rows_: pl.BlockSpec((rows_, LANES), lambda i: (0, i))
        at = lambda array, size=LANES: lanes_block(array, size, first)
        halves.append(
            pl.pallas_call(
                functools.partial(back_kernel, first=first),
                grid=(count,),
                in_specs=[
                    at(proj_x), at(dy), whole(shifts), whole(shifts_t), at(x_rows),
                    whole(gram), whole(b_act), whole(c_t), whole(dt), whole(e), whole(f), whole(la),
                    at(select, sel_width), at(expand), pl.BlockSpec((LANES, 256), lambda i: (first + i, 0)),
                    whole(cat), pl.BlockSpec((chunks, 128, LANES), lambda i: (0, 0, first + i)), at(state_in), at(grad_in),
                ],
                out_specs=[
                    block(length), block(2 * HALO), block(8), acc(length, 128), acc(length, 256), acc(length, 128),
                    block(8),
                ],
                out_shape=[
                    shape((length, inner // 2), BF16), shape((2 * HALO, inner // 2)), shape((8, inner // 2)),
                    shape((length, 128)), shape((length, 256)), shape((length, 128)), shape((8, inner // 2)),
                ],
                scratch_shapes=[pltpu.VMEM((length + HALO, LANES), F32)],
                compiler_params=PARAMS,
                name="scan_bwd" + str(half),
                cost_estimate=cost(22),
            )(proj_x, dy, shifts, shifts_t, x_rows, gram, b_act, c_t, dt, e, f, la, select, expand,
              collect, cat, states, state_in, grad_in)
        )
    grad_x, edge_x, cg_x, pair_sum, dcb, red, ends = zip(*halves)

    ins = [shifts, shifts_t, mask, bc_rows, head_rows, b_act, c_act, *pair_sum, *dcb, *red, *ends, collect, q, dt_full]
    in_specs = [whole(a) for a in ins]
    in_specs[-3] = acc(inner, 128)
    outs = [
        shape((length, 2 * state_dim + 128), BF16), shape((2 * HALO, 2 * state_dim)), shape((8, 2 * state_dim)),
        shape((8, 128)),
    ]
    grad_bcd, edge_bc, cg_bc, head_grads = pl.pallas_call(
        post_kernel,
        grid=(1,),
        in_specs=[bc_spec, dt_spec] + in_specs,
        out_specs=[whole(o) for o in outs],
        out_shape=outs,
        scratch_shapes=[pltpu.VMEM((length + HALO, 2 * state_dim), F32)],
        compiler_params=PARAMS,
        name="post",
        cost_estimate=cost(5),
    )(proj_x, proj_x, *ins)

    def with_last(part, edge, from_next):
        from_next = jnp.pad(from_next, ((HALO - 8, 0), (0, 0)))
        return lax.dynamic_update_slice(part, (edge[HALO:] + from_next).astype(BF16), (length - HALO, 0))

    raw_bcd = grad_bcd
    first = shift_seq(edge_x[0][HALO - 8 : HALO], -1)
    second = shift_seq(jnp.concatenate([edge_x[1], edge_bc], axis=1)[HALO - 8 : HALO], -1)
    half = inner // 2
    grad_x = [with_last(grad_x[0], edge_x[0], first), with_last(grad_x[1], edge_x[1], second[:, :half])]
    grad_bcd = with_last(grad_bcd, edge_bc, second[:, half:])
    late = []
    if fast:
        quarter = inner // 4
        scratch = lambda others: [pltpu.VMEM((CHIPS * 128 + others, 2 * length), BF16)]
        halves = []
        for part in grad_x:
            near = jnp.where(core == 0, part[:, :quarter], part[:, quarter:])
            far = jnp.where(core == 0, part[:, quarter:], part[:, :quarter])
            if halves:
                far = jnp.concatenate([far, grad_bcd], axis=1)
            halves.append([near, to_core(far)])
        late = late_a = grads_call(
            functools.partial(late_grads_kernel, with_others=False), idx, [after(normed, raw_bcd, early), normed_far],
            halves[0], 128, scratch(0), "late_grads_a",
        )
    norm_row = jnp.broadcast_to(norm_gain[None], (8, width))
    input_grad, norm_gain_part = pl.pallas_call(
        norm_back_kernel,
        grid=(chunks,),
        in_specs=[
            rows_spec(width), rows_spec(inner // 2), rows_spec(inner // 2), rows_spec(grad_bcd.shape[1]),
            whole(w_x), rows_spec(width), rows_spec(width), whole(norm_row),
        ],
        out_specs=[rows_spec(width), acc(8, width)],
        out_shape=[shape((length, width)), shape((8, width))],
        compiler_params=PARAMS,
        cost_estimate=cost(8),
        name="norm_back",
    )(grad_normed, *after(grad_x, late), grad_bcd, w_x, hidden[0], cotangent[0], norm_row)
    norm_gain_part = jnp.sum(norm_gain_part, axis=0)
    small = [jnp.sum(gain_part, axis=0), jnp.concatenate([*cg_x, cg_bc], axis=1)[: TAPS + 1].reshape(-1)]
    small = after(jnp.concatenate(small + [head_grads[:3, :heads].reshape(-1)]), late)
    if fast:
        norm_rows = width // 256
        small_rows = SMALL - norm_rows
        small = jnp.pad(small, (0, 2 * small_rows * 256 - small.shape[0])).reshape(2, small_rows, 256)
        small = lax.dynamic_index_in_dim(small + to_core(small), core, 0, False)
        small = jnp.concatenate([small, norm_gain_part.reshape(norm_rows, 256)], axis=0)
        early = to_planes(sum_over_chips(idx, after(early, late_a)))
        late_a = to_chips(late_a)
        late_b = grads_call(
            functools.partial(late_grads_kernel, with_others=True), idx, [after(normed, late_a, early[0]), normed_far],
            [*halves[1], grad_bcd, small], 128 + 2 * SMALL,
            scratch(384) + [pltpu.VMEM((8 * 2 * SMALL, 256), F32)], "late_grads_b",
        )
        early = sum_over_planes(idx, after(early, late_b))
        late = sum_over_chips(idx, after([*late_a, *to_chips(late_b)], early), True)
        early = share_in_plane(after(early, late))
        late = to_planes(late)
        early = both_cores(after(early, late))
        late = share_in_plane(sum_over_planes(idx, late, True))
        in_grad, out_grad = finish_early(idx, early, (in_weight.shape[1], width // PLANES), (inner // PLANES, width))
        in_grad, small = finish_late(idx, both_cores(late), in_grad)
        in_grad = in_grad.T
        small = small.reshape(2, SMALL, 256)
        norm_total = jnp.sum(small[:, small_rows:], axis=0).reshape(-1)
        small = small[:, :small_rows].reshape(-1)
    else:
        in_x = reduce_rows(mm_rows(normed, jnp.concatenate([*grad_x, grad_bcd], axis=1)))
        in_grad = jnp.concatenate([in_z, in_x[:, :x_cols]], axis=1)
        small, norm_total = lax.psum((small, norm_gain_part), (SEQ, WT))
    at = 0
    pieces = []
    for size in (inner, TAPS * conv_bias.shape[0], conv_bias.shape[0], heads, heads, heads):
        pieces.append(small[at : at + size])
        at += size
    gain_total, conv_w_total, conv_b_total, step_total, decay_total, skip_total = pieces

    return (
        output[None], input_grad[None], norm_total, in_grad, conv_w_total.reshape(conv_weight.shape), conv_b_total,
        step_total, decay_total, skip_total, gain_total, out_grad,
    )


def solution(mesh):
    placed = (
        P(WT, SEQ, None), P(WT, None), P(), P(WT, None), P(), P(), P(), P(), P(), P(), P(WT, None), P(WT, SEQ, None),
    )
    return jax.shard_map(
        on_device,
        mesh=mesh,
        in_specs=placed,
        out_specs=(
            P(WT, SEQ, None), P(WT, SEQ, None), P(), P(WT, None), P(), P(), P(), P(), P(), P(), P(WT, None),
        ),
        check_vma=False,
    )
```
